32 devices in a mesh: dom: 16 (over z, y, x), rep: 2 (over core).
Axes of the slice: x: 2, y: 2, z: 4, core: 2. Of those that a mesh axis runs over, the one named last changes fastest.
Arguments:
- embeds: bfloat16 [16384, 1024], P(('dom', 'rep')), may hold values from -6 to 6
- weight_in: bfloat16 [1024, 4096], replicated, may hold values from -0.1875 to 0.1875
- weight_out: bfloat16 [4096, 512], replicated, may hold values from -0.09375 to 0.09375
- prototypes: bfloat16 [1000, 512], replicated, may hold values from -4 to 4
- tile_column: int32 [128, 8], P(('dom', 'rep')), may hold values from 0 to 5, as said below
- tile_weight: bfloat16 [128, 8, 128, 128], P(('dom', 'rep')), may hold values from 0 to 1
- send_rows: int32 [32, 32, 8], P(('dom', 'rep')), may hold values from 0 to 511
- send_count: int32 [32, 32], P(('dom', 'rep')), may hold values from 1 to 8, as said below
- label_rows: int32 [2048], P(('dom', 'rep')), may hold values from 0 to 511, as said below
- label_class: int32 [2048], P(('dom', 'rep')), may hold values from 0 to 999
Outputs:
- embed_grad: bfloat16 [16384, 1024], P(('dom', 'rep'))
- grad_weight_out: float32 [4096, 512], P(('dom', 'rep'))
The draws below stay inside these ranges and needn't reach their ends.
Inputs may be any that keep to these rules, and one draw needn't show every extreme that they name: `tile_column`: in each row block b the first tile names block b mod 4, tiles 1 to 3 name blocks below 4, the others name received blocks; every received block is named by some tile of its partition. `send_count`: every partition fills all 8 slots for at least one other partition. `label_rows`: distinct within a partition.
All inputs are finite; a program needn't handle non-finite values.
Results may differ from the reference program's by a relative error of at most 0.006.
The reference program's roundings to bfloat16 on the way count: a program that leaves them out, or rounds other values in their place, can miss the bound.
Values may be sent and summed in bfloat16 or wider, within the bound.
No kernel may reach another device: no remote copies, remote signals or barrier semaphores. Data moves between devices by JAX's collectives and lax.ppermute only.
A program may use at most 128 MiB of HBM per device.

```python
import math
import jax
import jax.numpy as jnp
from jax import lax

D_IN = 1024
FF = 4096
D_OUT = 512
CLASSES = 1000
BLOCK = 128
TILES_ROW = 8
BLOCKS_DEV = 4
SEND_CAP = 8
LABELS_DEV = 64
NODE_DEV = 512
PEERS = 32
NODES = 16384
RECV_BLOCKS = 2
LABELS = 2048
N_DOM = 16
N_REP = 2


def draw_tile_column(key, part):
    half_count = TILES_ROW // 2
    key_local, key_turn = jax.random.split(key)
    shape_all = (PEERS, BLOCKS_DEV, TILES_ROW)
    local_pick = jax.random.randint(key_local, shape_all, 0, BLOCKS_DEV)
    turning = jax.random.randint(key_turn, (PEERS, 1, 1), 0, RECV_BLOCKS)
    block_index = lax.broadcasted_iota(jnp.int32, shape_all, 1)
    tile_index = lax.broadcasted_iota(jnp.int32, shape_all, 2)
    remote_order = block_index * (TILES_ROW - half_count) + (tile_index - half_count)
    remote_pick = BLOCKS_DEV + (remote_order + turning) % RECV_BLOCKS
    chosen = jnp.where(tile_index == 0, block_index, jnp.where(tile_index < half_count, local_pick, remote_pick))
    return chosen.reshape(PEERS * BLOCKS_DEV, TILES_ROW).astype(jnp.int32)


def draw_tile_weight(key, part):
    uniform_draw = jax.random.uniform(key, (PEERS * BLOCKS_DEV, TILES_ROW, BLOCK, BLOCK), jnp.float32)
    return (uniform_draw ** 96.0).astype(jnp.bfloat16)


def draw_send_count(key, part):
    counts = jax.random.randint(key, (PEERS, PEERS), 1, SEND_CAP + 1)
    sender = lax.broadcasted_iota(jnp.int32, (PEERS, PEERS), 0)
    receiver = lax.broadcasted_iota(jnp.int32, (PEERS, PEERS), 1)
    return jnp.where(receiver == (sender + 1) % PEERS, SEND_CAP, counts).astype(jnp.int32)


def pick_labels(single):
    return jax.random.permutation(single, NODE_DEV)[:LABELS_DEV]


def draw_label_rows(key, part):
    key_all = jax.random.split(key, PEERS)
    picked = jax.vmap(pick_labels)(key_all)
    return picked.reshape(PEERS * LABELS_DEV).astype(jnp.int32)


def with_ends(array, own_key, low, largest):
    longest = array.shape.index(max(array.shape))
    spots = []
    for shift in (0, 1):
        where = [jax.random.randint(jax.random.fold_in(own_key, axis), (), 0, length) for axis, length in enumerate(array.shape)]
        where[longest] = (where[longest] + shift) % array.shape[longest]
        spots.append(tuple(where))
    return array.at[spots[0]].set(low).at[spots[1]].set(largest)


def steps_of(key, extent, pieces, smallest, high):
    def one(dim, blocks):
        heights = jax.random.uniform(jax.random.fold_in(jax.random.fold_in(key, 6), dim), (blocks,), jnp.float32, smallest / len(pieces), high / len(pieces))
        return jnp.repeat(jnp.exp(heights), extent[dim] // blocks).reshape((-1,) + (1,) * (len(extent) - dim - 1))

    factor_of = one(*pieces[0])
    for cut in pieces[1:]:
        factor_of = factor_of * one(*cut)
    return factor_of


def scatter_about(key, dims, width, most, pieces=(), held_as=jnp.bfloat16):
    array = width * jax.random.normal(key, dims, jnp.float32)
    if pieces:
        array = array * steps_of(key, dims, pieces, -0.22, 0.18)
    return jnp.clip(array, -most, most).astype(held_as)


def setup_inputs(seed: int = 0) -> dict:
    arg_keys = jax.random.split(jax.random.key(seed), 11)
    embeds = scatter_about(arg_keys[0], (NODES, D_IN), 1.0, 6.0, ((0, 32),))
    weight_in = scatter_about(arg_keys[1], (D_IN, FF), D_IN ** -0.5, 0.1875)
    weight_out = scatter_about(arg_keys[2], (FF, D_OUT), FF ** -0.5, 0.09375)
    prototypes = scatter_about(arg_keys[3], (CLASSES, D_OUT), 0.5, 4.0)
    tile_column = draw_tile_column(jax.random.fold_in(arg_keys[10], 71), 0)
    tile_weight = draw_tile_weight(jax.random.fold_in(arg_keys[10], 71), 0)
    send_rows = with_ends(jax.random.randint(arg_keys[6], (PEERS, PEERS, SEND_CAP), 0, NODE_DEV), jax.random.fold_in(arg_keys[6], 1), 0, NODE_DEV - 1).astype(jnp.int32)
    send_count = draw_send_count(jax.random.fold_in(arg_keys[10], 71), 0)
    label_rows = draw_label_rows(jax.random.fold_in(arg_keys[10], 71), 0)
    label_class = with_ends(jax.random.randint(arg_keys[9], (LABELS,), 0, CLASSES), jax.random.fold_in(arg_keys[9], 1), 0, CLASSES - 1).astype(jnp.int32)
    return dict(embeds=embeds, weight_in=weight_in, weight_out=weight_out, prototypes=prototypes, tile_column=tile_column, tile_weight=tile_weight, send_rows=send_rows, send_count=send_count, label_rows=label_rows, label_class=label_class)


gelu_inner = 0.7978845608028654
gelu_cubic = 0.044715

def gelu_value(values):
    inner_arg = gelu_inner * (values + gelu_cubic * values * values * values)
    return 0.5 * values * (1.0 + jnp.tanh(inner_arg))

def gelu_slope(values):
    inner_arg = gelu_inner * (values + gelu_cubic * values * values * values)
    tangent = jnp.tanh(inner_arg)
    return 0.5 * (1.0 + tangent) + 0.5 * values * (1.0 - tangent * tangent) * gelu_inner * (1.0 + 3.0 * gelu_cubic * values * values)

def reference(embeds, weight_in, weight_out, prototypes, tile_column, tile_weight, send_rows, send_count, label_rows, label_class):
    peer_count = N_DOM * N_REP
    inputs_dev = embeds.reshape(peer_count, NODE_DEV, D_IN)

    def forward(block_in):
        pre_act = jnp.dot(block_in, weight_in, preferred_element_type=jnp.float32)
        hidden = gelu_value(pre_act).astype(jnp.bfloat16)
        return jnp.dot(hidden, weight_out, preferred_element_type=jnp.float32)
    projected = lax.map(forward, inputs_dev)
    weights_dev = tile_weight.reshape(peer_count, BLOCKS_DEV, TILES_ROW, BLOCK, BLOCK)

    def row_sums(tile_set):
        return lax.optimization_barrier(jnp.sum(tile_set.astype(jnp.float32), axis=(1, 3)))
    rowsum = lax.map(row_sums, weights_dev).reshape(peer_count, NODE_DEV)
    scaling = lax.rsqrt(1.0 + rowsum)
    unit_rows = (projected * scaling[:, :, None]).astype(jnp.bfloat16)
    slot_index = lax.broadcasted_iota(jnp.int32, (peer_count, peer_count, SEND_CAP), 2)
    slot_mask = slot_index < send_count[:, :, None]

    def pick_rows(unit_local, index_local):
        return jnp.take(unit_local, index_local, axis=0)
    picked = jax.vmap(pick_rows)(unit_rows, send_rows.reshape(peer_count, peer_count * SEND_CAP))
    picked = picked.reshape(peer_count, peer_count, SEND_CAP, D_OUT)
    picked = jnp.where(slot_mask[:, :, :, None], picked, jnp.zeros_like(picked))
    received = jnp.swapaxes(picked, 0, 1).reshape(peer_count, peer_count * SEND_CAP, D_OUT)
    columns_dev = tile_column.reshape(peer_count, BLOCKS_DEV, TILES_ROW)

    def graph_part(operands):
        unit_local, incoming, tile_set, column_set, rowsum_local = operands
        extended = jnp.concatenate([unit_local, incoming], axis=0)
        extended = extended.reshape(BLOCKS_DEV + RECV_BLOCKS, BLOCK, D_OUT).astype(jnp.float32)
        flat_columns = column_set.reshape(BLOCKS_DEV * TILES_ROW).astype(jnp.int32)
        sources = extended[flat_columns].reshape(BLOCKS_DEV, TILES_ROW, BLOCK, D_OUT)
        weight_set = tile_set.astype(jnp.float32)
        neighbour = jnp.einsum('rtab,rtbd->rad', weight_set, sources, precision=lax.Precision.HIGHEST)
        unit_float = unit_local.astype(jnp.float32)
        row_term = rowsum_local[:, None] * unit_float - neighbour.reshape(NODE_DEV, D_OUT)
        column_sum = lax.optimization_barrier(jnp.sum(weight_set, axis=2))
        column_term = column_sum[:, :, :, None] * sources - jnp.einsum('rtab,rad->rtbd', weight_set, unit_float.reshape(BLOCKS_DEV, BLOCK, D_OUT), precision=lax.Precision.HIGHEST)
        collected = jnp.zeros((BLOCKS_DEV + RECV_BLOCKS, BLOCK, D_OUT), jnp.float32)
        collected = collected.at[flat_columns].add(column_term.reshape(BLOCKS_DEV * TILES_ROW, BLOCK, D_OUT))
        local_grad = row_term + collected[:BLOCKS_DEV].reshape(NODE_DEV, D_OUT)
        returned = collected[BLOCKS_DEV:].reshape(peer_count, SEND_CAP, D_OUT).astype(jnp.bfloat16)
        return (local_grad, returned)
    local_grad, returned = lax.map(graph_part, (unit_rows, received, weights_dev, columns_dev, rowsum))
    back_values = jnp.swapaxes(returned, 0, 1)

    def collect_back(operands):
        values_local, rows_local, mask_local = operands
        masked = jnp.where(mask_local.reshape(peer_count * SEND_CAP)[:, None], values_local.reshape(peer_count * SEND_CAP, D_OUT).astype(jnp.float32), jnp.zeros((peer_count * SEND_CAP, D_OUT), jnp.float32))
        return jnp.zeros((NODE_DEV, D_OUT), jnp.float32).at[rows_local.reshape(peer_count * SEND_CAP)].add(masked)
    back_sum = lax.map(collect_back, (back_values, send_rows, slot_mask))
    grad_proj = (local_grad + back_sum) * scaling[:, :, None]
    targets = prototypes.astype(jnp.float32)[label_class].reshape(peer_count, LABELS_DEV, D_OUT)
    labels_dev = label_rows.reshape(peer_count, LABELS_DEV)

    def add_labels(operands):
        grad_local, proj_local, rows_local, target_local = operands
        return grad_local.at[rows_local].add(proj_local[rows_local] - target_local)
    grad_proj = lax.map(add_labels, (grad_proj, projected, labels_dev, targets))
    grad_node = grad_proj.astype(jnp.bfloat16)

    def backward(running, operands):
        block_in, grad_local = operands
        pre_act = jnp.dot(block_in, weight_in, preferred_element_type=jnp.float32)
        hidden = gelu_value(pre_act).astype(jnp.bfloat16)
        grad_hidden = jnp.dot(grad_local, weight_out.T, preferred_element_type=jnp.float32)
        grad_pre = (grad_hidden * gelu_slope(pre_act)).astype(jnp.bfloat16)
        embed_local = jnp.dot(grad_pre, weight_in.T, preferred_element_type=jnp.float32).astype(jnp.bfloat16)
        running = running + jnp.dot(hidden.T, grad_local, preferred_element_type=jnp.float32)
        return (running, embed_local)
    running, embed_grad = lax.scan(backward, jnp.zeros((FF, D_OUT), jnp.float32), (inputs_dev, grad_node))
    return (embed_grad.reshape(NODES, D_IN), running * (1.0 / math.sqrt(NODES)))
```

```python
import math

import jax
import jax.numpy as jnp
from jax import lax
from jax.sharding import PartitionSpec as P

gelu_inner = 0.7978845608028654
gelu_cubic = 0.044715


def gelu_value(values):
    inner_arg = gelu_inner * (values + gelu_cubic * values * values * values)
    return 0.5 * values * (1.0 + jnp.tanh(inner_arg))


def gelu_slope(values):
    inner_arg = gelu_inner * (values + gelu_cubic * values * values * values)
    tangent = jnp.tanh(inner_arg)
    return 0.5 * (1.0 + tangent) + 0.5 * values * (1.0 - tangent * tangent) * gelu_inner * (
        1.0 + 3.0 * gelu_cubic * values * values
    )


def bit_orders(count):
    bits = list(range(count.bit_length() - 1))
    first = len(bits) // 3
    second = first + max(first, (len(bits) - first) // 3)
    low, middle, high = bits[:first], bits[first:second], bits[second:]
    return (low + middle + high, middle + low + high, high + low + middle)


def halve_over(part, axis, spot, pairs, mine):
    kept = lax.dynamic_index_in_dim(part, mine, spot, keepdims=False)
    sent = lax.dynamic_index_in_dim(part, 1 - mine, spot, keepdims=False).astype(jnp.bfloat16)
    return kept + lax.ppermute(sent, axis, pairs).astype(jnp.float32)


def scatter_sum(total):
    dom_count = lax.axis_size("dom")
    rep_count = lax.axis_size("rep")
    width = total.shape[1]
    if rep_count != 2 or dom_count & (dom_count - 1) or dom_count < 8:
        return lax.psum_scatter(total, ("dom", "rep"), scatter_dimension=0, tiled=True)
    depth = total.shape[0] // (dom_count * rep_count)
    place = lax.axis_index("dom")
    blocks = total.reshape(dom_count, rep_count, depth, width)
    chip_sum = halve_over(blocks, "rep", 1, [(0, 1), (1, 0)], lax.axis_index("rep"))
    cut = depth * 3 // 8
    edges = (0, cut, 2 * cut, depth)
    streams = []
    for order, low, high in zip(bit_orders(dom_count), edges[:-1], edges[1:]):
        bit_count = len(order)
        streams.append(
            (chip_sum[:, low:high].reshape((2,) * bit_count + (high - low, width)), list(reversed(range(bit_count))), order)
        )
    for step in range(dom_count.bit_length() - 1):
        later = []
        for part, left, order in streams:
            bit = order[step]
            pairs = [(device, device ^ (1 << bit)) for device in range(dom_count)]
            spot = left.index(bit)
            part = halve_over(part, "dom", spot, pairs, (place >> bit) & 1)
            later.append((part, [other for other in left if other != bit], order))
        streams = later
    return jnp.concatenate([part for part, _, _ in streams], axis=0)


def body(
    embeds,
    weight_in,
    weight_out,
    prototypes,
    tile_column,
    tile_weight,
    send_rows,
    send_count,
    label_rows,
    label_class,
):
    node_count = embeds.shape[0]
    block_count = tile_weight.shape[0]
    tile_count = tile_weight.shape[1]
    block_size = tile_weight.shape[2]
    width_out = weight_out.shape[1]
    dom_count = lax.axis_size("dom")
    rep_count = lax.axis_size("rep")
    peer_count = dom_count * rep_count
    slot_count = send_rows.shape[2]
    pre_act = jnp.dot(embeds, weight_in, preferred_element_type=jnp.float32)
    hidden = gelu_value(pre_act).astype(jnp.bfloat16)
    projected = jnp.dot(hidden, weight_out, preferred_element_type=jnp.float32)
    rowsum = jnp.sum(tile_weight, axis=(1, 3), dtype=jnp.float32).reshape(node_count)
    scaling = lax.rsqrt(1.0 + rowsum)
    unit_rows = (projected * scaling[:, None]).astype(jnp.bfloat16)
    slot_mask = (
        lax.broadcasted_iota(jnp.int32, (peer_count, slot_count), 1) < send_count[0][:, None]
    )
    flat_sends = send_rows[0].reshape(peer_count * slot_count)
    outgoing = jnp.take(unit_rows, flat_sends, axis=0).reshape(peer_count, slot_count, width_out)
    outgoing = jnp.where(slot_mask[:, :, None], outgoing, jnp.zeros_like(outgoing))
    incoming = lax.all_to_all(outgoing, ("dom", "rep"), split_axis=0, concat_axis=0, tiled=True)
    incoming = incoming.reshape(peer_count * slot_count, width_out)
    extended = jnp.concatenate([unit_rows, incoming], axis=0).reshape(-1, block_size, width_out)
    total_blocks = extended.shape[0]
    flat_columns = tile_column.reshape(block_count * tile_count)
    sources = jnp.take(extended, flat_columns, axis=0).reshape(
        block_count, tile_count, block_size, width_out
    )
    neighbour = jnp.einsum(
        "rtab,rtbd->rad", tile_weight, sources, preferred_element_type=jnp.float32
    )
    row_term = rowsum[:, None] * unit_rows.astype(jnp.float32) - neighbour.reshape(
        node_count, width_out
    )
    unit_blocks = unit_rows.reshape(block_count, block_size, width_out)
    column_sum = jnp.sum(tile_weight, axis=2, dtype=jnp.float32)
    column_term = column_sum[:, :, :, None] * sources.astype(jnp.float32) - jnp.einsum(
        "rtab,rad->rtbd", tile_weight, unit_blocks, preferred_element_type=jnp.float32
    )
    selector = (
        flat_columns[:, None]
        == lax.broadcasted_iota(jnp.int32, (block_count * tile_count, total_blocks), 1)
    ).astype(jnp.float32)
    gathered_terms = jnp.einsum(
        "tc,tf->cf",
        selector,
        column_term.reshape(block_count * tile_count, block_size * width_out),
        precision=lax.Precision.HIGHEST,
    )
    own_term = gathered_terms[:block_count].reshape(node_count, width_out)
    returned = (
        gathered_terms[block_count:].reshape(peer_count, slot_count, width_out).astype(jnp.bfloat16)
    )
    arrived = lax.all_to_all(returned, ("dom", "rep"), split_axis=0, concat_axis=0, tiled=True)
    back_rows = arrived.reshape(peer_count * slot_count, width_out)
    placement = (
        flat_sends[None, :]
        == lax.broadcasted_iota(jnp.int32, (node_count, peer_count * slot_count), 0)
    ) & slot_mask.reshape(peer_count * slot_count)[None, :]
    back_sum = jnp.dot(
        placement.astype(jnp.bfloat16), back_rows, preferred_element_type=jnp.float32
    )
    grad_proj = (row_term + own_term + back_sum) * scaling[:, None]
    class_table = (
        label_class[:, None]
        == lax.broadcasted_iota(jnp.int32, (label_class.shape[0], prototypes.shape[0]), 1)
    ).astype(jnp.bfloat16)
    targets = jnp.dot(class_table, prototypes, preferred_element_type=jnp.float32)
    grad_proj = grad_proj.at[label_rows].add(jnp.take(projected, label_rows, axis=0) - targets)
    grad_node = grad_proj.astype(jnp.bfloat16)
    grad_hidden = lax.dot_general(
        grad_node, weight_out, (((1,), (1,)), ((), ())), preferred_element_type=jnp.float32
    )
    grad_pre = (grad_hidden * gelu_slope(pre_act)).astype(jnp.bfloat16)
    embed_grad = lax.dot_general(
        grad_pre, weight_in, (((1,), (1,)), ((), ())), preferred_element_type=jnp.float32
    ).astype(jnp.bfloat16)
    factor = 1.0 / math.sqrt(node_count * peer_count)
    grad_weight = scatter_sum(
        lax.dot_general(
            hidden, grad_node, (((0,), (0,)), ((), ())), preferred_element_type=jnp.float32
        )
    )
    return (embed_grad, grad_weight * factor)


def solution(mesh):
    placed = (
        P(("dom", "rep"), None),
        P(),
        P(),
        P(),
        P(("dom", "rep"), None),
        P(("dom", "rep"), None, None, None),
        P(("dom", "rep"), None, None),
        P(("dom", "rep"), None),
        P(("dom", "rep")),
        P(("dom", "rep")),
    )
    return jax.shard_map(
        body,
        mesh=mesh,
        in_specs=placed,
        out_specs=(P(("dom", "rep"), None), P(("dom", "rep"), None)),
        check_vma=False,
    )
```

```python
import math

import jax
import jax.numpy as jnp
from jax import lax
from jax.experimental import pallas as pl
from jax.experimental.pallas import tpu as pltpu
from jax.sharding import PartitionSpec as P

gelu_inner = 0.7978845608028654
gelu_cubic = 0.044715
LANES = 128
VMEM_BYTES = 48 * 1024 * 1024
both = ("dom", "rep")


def gelu_value(values):
    inner_arg = gelu_inner * (values + gelu_cubic * values * values * values)
    return 0.5 * values * (1.0 + jnp.tanh(inner_arg))


def gelu_slope(values):
    inner_arg = gelu_inner * (values + gelu_cubic * values * values * values)
    tangent = jnp.tanh(inner_arg)
    return 0.5 * (1.0 + tangent) + 0.5 * values * (1.0 - tangent * tangent) * gelu_inner * (
        1.0 + 3.0 * gelu_cubic * values * values
    )


def dot(left, right, left_dim=1, right_dim=0):
    return lax.dot_general(
        left, right, (((left_dim,), (right_dim,)), ((), ())), preferred_element_type=jnp.float32
    )


def params():
    return pltpu.CompilerParams(vmem_limit_bytes=VMEM_BYTES)


def whole(shape):
    return pl.BlockSpec(shape, lambda *_: (0,) * len(shape))


def bits_of(values):
    high = values.astype(jnp.bfloat16).astype(jnp.float32)
    middle = (values - high).astype(jnp.bfloat16).astype(jnp.float32)
    return high, middle, values - high - middle


def prepare_kernel(rows_ref, count_ref, tiles_ref, embeds_ref, out_ref, pick_ref, side_ref):
    slots, peers = rows_ref.shape
    nodes, width = embeds_ref.shape
    sent = slots * peers
    blocks, tiles = tiles_ref.shape[:2]
    spread = jnp.concatenate([rows_ref[...].astype(jnp.float32)] * peers, axis=0)
    row = lax.broadcasted_iota(jnp.int32, (sent, peers), 0)
    chosen = lax.div(row, slots) == lax.broadcasted_iota(jnp.int32, (sent, peers), 1)
    index = jnp.sum(jnp.where(chosen, spread, 0.0), axis=1, keepdims=True).astype(jnp.int32)
    counts = jnp.broadcast_to(count_ref[...].astype(jnp.float32), (sent, peers))
    count = jnp.sum(jnp.where(chosen, counts, 0.0), axis=1, keepdims=True).astype(jnp.int32)
    slot = lax.rem(lax.broadcasted_iota(jnp.int32, (sent, nodes), 0), slots)
    node = lax.broadcasted_iota(jnp.int32, (sent, nodes), 1)
    pick = jnp.where((node == index) & (slot < count), 1.0, 0.0).astype(jnp.bfloat16)
    pick_ref[...] = pick
    out_ref[:, :width] = dot(pick, embeds_ref[...]).astype(jnp.bfloat16)
    size = tiles_ref.shape[2]
    lane = lax.broadcasted_iota(jnp.int32, (size, LANES), 1)
    parts = []
    for block in range(blocks):
        total = tiles_ref[block, 0].astype(jnp.float32)
        for tile in range(1, tiles):
            total = total + tiles_ref[block, tile].astype(jnp.float32)
        rowsum = jnp.sum(total, axis=1, keepdims=True)
        scaling = lax.rsqrt(1.0 + rowsum)
        side_ref[block * size : (block + 1) * size, :] = jnp.where(lane == 0, rowsum, scaling)
        high, middle, low = bits_of(scaling)
        part = jnp.where(lane == 0, high, jnp.where(lane == 1, middle, jnp.where(lane == 2, low, 0.0)))
        parts.append(part.astype(jnp.bfloat16))
    out_ref[:, width:] = dot(pick, jnp.concatenate(parts, axis=0)).astype(jnp.bfloat16)


def prepare(rows, count, tile_weight, embeds):
    sent = rows.shape[0] * rows.shape[1]
    nodes, width = embeds.shape
    return pl.pallas_call(
        prepare_kernel,
        out_shape=(
            jax.ShapeDtypeStruct((sent, width + LANES), jnp.bfloat16),
            jax.ShapeDtypeStruct((sent, nodes), jnp.bfloat16),
            jax.ShapeDtypeStruct((nodes, LANES), jnp.float32),
        ),
        compiler_params=params(),
        name="prepare",
    )(rows, count, tile_weight, embeds)


def forward_kernel(x_ref, win_ref, wout_ref, pre_ref, hid_ref, proj_ref):
    step = pl.program_id(0)
    pre = dot(x_ref[...], win_ref[...])
    pre_ref[...] = pre
    hidden = gelu_value(pre).astype(jnp.bfloat16)
    for pair in range(hidden.shape[1] // (2 * LANES)):
        for rep in range(2):
            low = (2 * pair + rep) * LANES
            hid_ref[rep, :, pair * LANES : (pair + 1) * LANES] = hidden[:, low : low + LANES]
    part = dot(hidden, wout_ref[...])

    @pl.when(step == 0)
    def _():
        proj_ref[...] = part

    @pl.when(step > 0)
    def _():
        proj_ref[...] += part


def forward(embeds, weight_in, weight_out, chunk=512):
    nodes, depth = embeds.shape
    hidden = weight_in.shape[1]
    width = weight_out.shape[1]
    return pl.pallas_call(
        forward_kernel,
        grid=(hidden // chunk,),
        in_specs=[
            whole((nodes, depth)),
            pl.BlockSpec((depth, chunk), lambda i: (0, i)),
            pl.BlockSpec((chunk, width), lambda i: (i, 0)),
        ],
        out_specs=(
            pl.BlockSpec((nodes, chunk), lambda i: (0, i)),
            pl.BlockSpec((2, nodes, chunk // 2), lambda i: (0, 0, i)),
            whole((nodes, width)),
        ),
        out_shape=(
            jax.ShapeDtypeStruct((nodes, hidden), jnp.float32),
            jax.ShapeDtypeStruct((2, nodes, hidden // 2), jnp.bfloat16),
            jax.ShapeDtypeStruct((nodes, width), jnp.float32),
        ),
        compiler_params=params(),
        name="forward",
    )(embeds, weight_in, weight_out)


def local_kernel(
    column_ref,
    tiles_ref,
    side_ref,
    proj_ref,
    rows_ref,
    class_ref,
    proto_ref,
    grad_ref,
    weight_ref,
    back_ref,
    dense_ref,
):
    blocks, tiles, size, _ = tiles_ref.shape
    nodes, width = proj_ref.shape
    extent = dense_ref.shape[0]
    dense_ref[...] = jnp.zeros_like(dense_ref)
    for block in range(blocks):
        for tile in range(tiles):
            column = column_ref[block, tile]
            place = slice(block * size, (block + 1) * size)
            dense_ref[column, place, :] += tiles_ref[block, tile].astype(jnp.float32)
    dense = jnp.concatenate([dense_ref[column] for column in range(extent)], axis=1)
    high = dense.astype(jnp.bfloat16)
    low = (dense - high.astype(jnp.float32)).astype(jnp.bfloat16)
    weight_ref[0] = high[:, nodes:]
    weight_ref[1] = low[:, nodes:]
    rowsum = side_ref[:, 0:1]
    scaling = side_ref[:, 1:2]
    projected = proj_ref[...]
    unit = (projected * scaling).astype(jnp.bfloat16)
    unit_float = unit.astype(jnp.float32)
    beside = jnp.concatenate([unit, jnp.ones((nodes, LANES), jnp.bfloat16)], axis=1)
    turned = dot(high, beside, 0, 0) + dot(low, beside, 0, 0)
    back_ref[...] = turned[nodes:]
    neighbour = dot(high[:, :nodes], unit) + dot(low[:, :nodes], unit)
    own = turned[:nodes, width : width + 1] * unit_float - turned[:nodes, :width]
    marked = rows_ref.shape[1]
    node = lax.broadcasted_iota(jnp.int32, (nodes, marked), 0)
    label = jnp.where(node == rows_ref[...], 1.0, 0.0)
    name = lax.broadcasted_iota(jnp.int32, (proto_ref.shape[0], marked), 0)
    named = jnp.where(name == class_ref[...], 1.0, 0.0).astype(jnp.bfloat16)
    target = dot(named, proto_ref[...], 0, 0).astype(jnp.bfloat16)
    pull = jnp.sum(label, axis=1, keepdims=True) * projected - dot(label.astype(jnp.bfloat16), target)
    grad_ref[...] = (rowsum * unit_float - neighbour + own) * scaling + pull


def local_part(tile_column, tile_weight, side, projected, label_rows, label_class, prototypes, received):
    nodes, width = projected.shape
    size = tile_weight.shape[2]
    vmem = pl.BlockSpec(memory_space=pltpu.VMEM)
    return pl.pallas_call(
        local_kernel,
        in_specs=[pl.BlockSpec(memory_space=pltpu.SMEM)] + [vmem] * 6,
        out_shape=(
            jax.ShapeDtypeStruct((nodes, width), jnp.float32),
            jax.ShapeDtypeStruct((2, nodes, received), jnp.bfloat16),
            jax.ShapeDtypeStruct((received, width + LANES), jnp.float32),
        ),
        scratch_shapes=[pltpu.VMEM(((nodes + received) // size, nodes, size), jnp.float32)],
        compiler_params=params(),
        name="local_part",
    )(tile_column, tile_weight, side, projected, label_rows, label_class, prototypes)


def received_kernel(
    x_ref,
    win_ref,
    wout_ref,
    side_ref,
    grad_ref,
    weight_ref,
    back_ref,
    hid_ref,
    full_ref,
    turned_ref,
    return_ref,
    proj_ref,
):
    step = pl.program_id(0)
    depth = win_ref.shape[0]
    pre = dot(x_ref[:, :depth], win_ref[...])
    hidden = gelu_value(pre).astype(jnp.bfloat16)
    for pair in range(hidden.shape[1] // (2 * LANES)):
        for rep in range(2):
            low = (2 * pair + rep) * LANES
            hid_ref[rep, :, pair * LANES : (pair + 1) * LANES] = hidden[:, low : low + LANES]
    part = dot(hidden, wout_ref[...])

    @pl.when(step == 0)
    def _():
        proj_ref[...] = part

    @pl.when(step > 0)
    def _():
        proj_ref[...] += part

    @pl.when(step == pl.num_programs(0) - 1)
    def _():
        nodes, width = grad_ref.shape
        scaling = jnp.sum(x_ref[:, depth:].astype(jnp.float32), axis=1, keepdims=True)
        unit = (proj_ref[...] * scaling).astype(jnp.bfloat16)
        neighbour = dot(weight_ref[0], unit) + dot(weight_ref[1], unit)
        full = grad_ref[...] - neighbour * side_ref[:, 1:2]
        full_ref[...] = full
        back = (back_ref[:, width : width + 1] * unit.astype(jnp.float32) - back_ref[:, :width]).astype(jnp.bfloat16)
        return_ref[...] = back
        turned_ref[:, :nodes] = full.T.astype(jnp.bfloat16)
        turned_ref[:, nodes:] = (back.astype(jnp.float32) * scaling).T.astype(jnp.bfloat16)


def received_part(arrived, weight_in, weight_out, side, grad, weight, back, chunk=512):
    rows = arrived.shape[0]
    depth, hidden = weight_in.shape
    nodes, width = grad.shape
    return pl.pallas_call(
        received_kernel,
        grid=(hidden // chunk,),
        in_specs=[
            whole(arrived.shape),
            pl.BlockSpec((depth, chunk), lambda i: (0, i)),
            pl.BlockSpec((chunk, width), lambda i: (i, 0)),
            whole(side.shape),
            whole(grad.shape),
            whole(weight.shape),
            whole(back.shape),
        ],
        out_specs=(
            pl.BlockSpec((2, rows, chunk // 2), lambda i: (0, 0, i)),
            whole((nodes, width)),
            whole((width, nodes + rows)),
            whole((rows, width)),
        ),
        out_shape=(
            jax.ShapeDtypeStruct((2, rows, hidden // 2), jnp.bfloat16),
            jax.ShapeDtypeStruct((nodes, width), jnp.float32),
            jax.ShapeDtypeStruct((width, nodes + rows), jnp.bfloat16),
            jax.ShapeDtypeStruct((rows, width), jnp.bfloat16),
        ),
        scratch_shapes=[pltpu.VMEM((rows, width), jnp.float32)],
        compiler_params=params(),
        name="received_part",
    )(arrived, weight_in, weight_out, side, grad, weight, back)


def product_kernel(rep_ref, turned_ref, other_ref, own_ref, came_ref, other_own_ref, other_came_ref, out_ref):
    nodes = own_ref.shape[1]
    total = dot(turned_ref[:, :nodes], own_ref[0]) + dot(turned_ref[:, nodes:], came_ref[0])
    total += dot(other_ref[:, :nodes], other_own_ref[...]) + dot(other_ref[:, nodes:], other_came_ref[...])
    for place in range(out_ref.shape[0]):
        out_ref[place] = total[:, place * LANES : (place + 1) * LANES]


def product(rep, turned, other, own, came, other_own, other_came, chunk=512):
    width = turned.shape[0]
    nodes, hidden = other_own.shape
    rows = other_came.shape[0]
    return pl.pallas_call(
        product_kernel,
        grid_spec=pltpu.PrefetchScalarGridSpec(
            num_scalar_prefetch=1,
            grid=(hidden // chunk,),
            in_specs=[
                whole(turned.shape),
                whole(other.shape),
                pl.BlockSpec((1, nodes, chunk), lambda i, rep: (rep[0], 0, i)),
                pl.BlockSpec((1, rows, chunk), lambda i, rep: (rep[0], 0, i)),
                pl.BlockSpec((nodes, chunk), lambda i, rep: (0, i)),
                pl.BlockSpec((rows, chunk), lambda i, rep: (0, i)),
            ],
            out_specs=pl.BlockSpec((chunk // LANES, width, LANES), lambda i, rep: (i, 0, 0)),
        ),
        out_shape=jax.ShapeDtypeStruct((hidden // LANES, width, LANES), jnp.float32),
        compiler_params=params(),
        name="product",
    )(rep, turned, other, own, came, other_own, other_came)


def backward_kernel(full_ref, pick_ref, back_ref, side_ref, pre_ref, wout_ref, win_ref, out_ref, node_ref, total_ref):
    step = pl.program_id(0)

    @pl.when(step == 0)
    def _():
        back = dot(pick_ref[...], back_ref[...], 0, 0)
        node_ref[...] = (full_ref[...] + back * side_ref[:, 1:2]).astype(jnp.bfloat16)

    grad_hidden = dot(node_ref[...], wout_ref[...], 1, 1)
    grad_pre = (grad_hidden * gelu_slope(pre_ref[...])).astype(jnp.bfloat16)
    part = dot(grad_pre, win_ref[...], 1, 1)

    @pl.when(step == 0)
    def _():
        total_ref[...] = part

    @pl.when(step > 0)
    def _():
        total_ref[...] += part

    @pl.when(step == pl.num_programs(0) - 1)
    def _():
        out_ref[...] = total_ref[...].astype(jnp.bfloat16)


def backward(full, pick, back, side, pre, weight_out, weight_in, chunk=512):
    nodes, hidden = pre.shape
    depth = weight_in.shape[0]
    width = weight_out.shape[1]
    return pl.pallas_call(
        backward_kernel,
        grid=(hidden // chunk,),
        in_specs=[
            whole(full.shape),
            whole(pick.shape),
            whole(back.shape),
            whole(side.shape),
            pl.BlockSpec((nodes, chunk), lambda i: (0, i)),
            pl.BlockSpec((chunk, width), lambda i: (i, 0)),
            pl.BlockSpec((depth, chunk), lambda i: (0, i)),
        ],
        out_specs=whole((nodes, depth)),
        out_shape=jax.ShapeDtypeStruct((nodes, depth), jnp.bfloat16),
        scratch_shapes=[pltpu.VMEM((nodes, width), jnp.bfloat16), pltpu.VMEM((nodes, depth), jnp.float32)],
        compiler_params=params(),
        name="backward",
    )(full, pick, back, side, pre, weight_out, weight_in)


def bit_orders(count):
    bits = list(range(count.bit_length() - 1))
    first = len(bits) // 3
    second = first + max(first, (len(bits) - first) // 3)
    low, middle, high = bits[:first], bits[first:second], bits[second:]
    return (low + middle + high, middle + low + high, high + low + middle)


def halve_over(part, axis, spot, pairs, mine):
    kept = lax.dynamic_index_in_dim(part, mine, spot, keepdims=False)
    sent = lax.dynamic_index_in_dim(part, 1 - mine, spot, keepdims=False).astype(jnp.bfloat16)
    return kept + lax.ppermute(sent, axis, pairs).astype(jnp.float32)


def scatter_sum(chip_sum):
    dom_count, width, depth = chip_sum.shape
    place = lax.axis_index("dom")
    cut = width * 3 // 8
    edges = (0, cut, 2 * cut, width)
    streams = []
    for order, low, high in zip(bit_orders(dom_count), edges[:-1], edges[1:]):
        bit_count = len(order)
        part = chip_sum[:, low:high].reshape((2,) * bit_count + (high - low, depth))
        streams.append((part, list(reversed(range(bit_count))), order))
    for step in range(dom_count.bit_length() - 1):
        later = []
        for part, left, order in streams:
            bit = order[step]
            pairs = [(device, device ^ (1 << bit)) for device in range(dom_count)]
            spot = left.index(bit)
            part = halve_over(part, "dom", spot, pairs, (place >> bit) & 1)
            later.append((part, [other for other in left if other != bit], order))
        streams = later
    return jnp.concatenate([part for part, _, _ in streams], axis=0)


def body(
    embeds,
    weight_in,
    weight_out,
    prototypes,
    tile_column,
    tile_weight,
    send_rows,
    send_count,
    label_rows,
    label_class,
):
    nodes = embeds.shape[0]
    dom_count = lax.axis_size("dom")
    rep_count = lax.axis_size("rep")
    peers = dom_count * rep_count
    slots = send_rows.shape[2]
    hidden_width, width = weight_out.shape
    depth = hidden_width // peers
    rep = lax.axis_index("rep")
    swap = [(0, 1), (1, 0)]
    fold = LANES // depth
    if fold > 1:
        order = (dom_count // fold, fold, rep_count, depth)
        weight_in = weight_in.reshape((-1,) + order).swapaxes(2, 3).reshape(-1, hidden_width)
        weight_out = weight_out.reshape(order + (-1,)).swapaxes(1, 2).reshape(hidden_width, -1)

    outgoing, pick, side = prepare(send_rows[0].T, send_count, tile_weight, embeds)
    arrived = lax.all_to_all(
        outgoing.reshape(peers, slots, -1), both, split_axis=0, concat_axis=0, tiled=True
    ).reshape(peers * slots, -1)
    pre_act, own_hidden, projected = forward(embeds, weight_in, weight_out)
    other_own = lax.ppermute(lax.dynamic_index_in_dim(own_hidden, 1 - rep, 0, keepdims=False), "rep", swap)
    grad, weight, back = local_part(
        tile_column,
        tile_weight,
        side,
        projected,
        label_rows[None, :],
        label_class[None, :],
        prototypes,
        peers * slots,
    )
    came_hidden, full, turned, returned = received_part(arrived, weight_in, weight_out, side, grad, weight, back)
    other_turned = lax.ppermute(turned, "rep", swap)
    other_came = lax.ppermute(lax.dynamic_index_in_dim(came_hidden, 1 - rep, 0, keepdims=False), "rep", swap)
    given = lax.all_to_all(
        returned.reshape(peers, slots, width), both, split_axis=0, concat_axis=0, tiled=True
    ).reshape(peers * slots, width)
    chip_sum = product(rep[None], turned, other_turned, own_hidden, came_hidden, other_own, other_came)
    if fold > 1:
        chip_sum = chip_sum.reshape(-1, width, fold, depth).swapaxes(1, 2).reshape(dom_count, width, depth)
    summed = scatter_sum(chip_sum)
    embed_grad = backward(full, pick, given, side, pre_act, weight_out, weight_in)
    return (embed_grad, summed.T * (1.0 / math.sqrt(nodes * peers)))


def solution(mesh):
    placed = (
        P(both, None),
        P(),
        P(),
        P(),
        P(both, None),
        P(both, None, None, None),
        P(both, None, None),
        P(both, None),
        P(both),
        P(both),
    )
    return jax.shard_map(
        body,
        mesh=mesh,
        in_specs=placed,
        out_specs=(P(both, None), P(both, None)),
        check_vma=False,
    )
```

```python
import functools
import math

import jax
import jax.numpy as jnp
from jax import lax
from jax.experimental import pallas as pl
from jax.experimental.pallas import tpu as pltpu
from jax.sharding import PartitionSpec as P

gelu_inner = 0.7978845608028654
gelu_cubic = 0.044715
LANES = 128
MIB = 1024 * 1024
both = ("dom", "rep")


def gelu_pair(values):
    square = values * values
    half = 0.5 + 0.5 * jnp.tanh(values * (gelu_inner + gelu_inner * gelu_cubic * square))
    value = values * half
    slope = half + value * (2.0 - 2.0 * half) * (gelu_inner + 3.0 * gelu_inner * gelu_cubic * square)
    return value, slope


def dot(left, right, left_dim=1, right_dim=0):
    return lax.dot_general(
        left, right, (((left_dim,), (right_dim,)), ((), ())), preferred_element_type=jnp.float32
    )


def params(mib=64):
    return pltpu.CompilerParams(vmem_limit_bytes=mib * MIB)


VMEM = pl.BlockSpec(memory_space=pltpu.VMEM)
SMEM = pl.BlockSpec(memory_space=pltpu.SMEM)
HBM = pl.BlockSpec(memory_space=pltpu.HBM)


class Copies:
    def __init__(self, semaphores):
        self.semaphores = semaphores
        self.started = {}

    def start(self, name, source, target):
        copy = pltpu.make_async_copy(source, target, self.semaphores.at[len(self.started)])
        copy.start()
        self.started[name] = copy

    def wait(self, name):
        self.started[name].wait()


def bits_of(values):
    high = values.astype(jnp.bfloat16).astype(jnp.float32)
    middle = (values - high).astype(jnp.bfloat16).astype(jnp.float32)
    return high, middle, values - high - middle


def prepare_kernel(
    rows_any,
    count_any,
    tiles_any,
    embeds_any,
    out_ref,
    pick_ref,
    side_ref,
    rows_ref,
    count_ref,
    tiles_ref,
    embeds_ref,
    semaphores,
):
    copies = Copies(semaphores)
    copies.start("rows", rows_any, rows_ref)
    copies.start("count", count_any, count_ref)
    copies.start("tiles", tiles_any, tiles_ref)
    copies.start("embeds", embeds_any, embeds_ref)
    copies.wait("rows")
    copies.wait("count")
    slots, peers = rows_ref.shape
    nodes, width = embeds_ref.shape
    sent = slots * peers
    blocks, tiles = tiles_ref.shape[:2]
    spread = jnp.concatenate([rows_ref[...].astype(jnp.float32)] * peers, axis=0)
    row = lax.broadcasted_iota(jnp.int32, (sent, peers), 0)
    chosen = lax.div(row, slots) == lax.broadcasted_iota(jnp.int32, (sent, peers), 1)
    index = jnp.sum(jnp.where(chosen, spread, 0.0), axis=1, keepdims=True).astype(jnp.int32)
    counts = jnp.broadcast_to(count_ref[...].astype(jnp.float32), (sent, peers))
    count = jnp.sum(jnp.where(chosen, counts, 0.0), axis=1, keepdims=True).astype(jnp.int32)
    slot = lax.rem(lax.broadcasted_iota(jnp.int32, (sent, nodes), 0), slots)
    node = lax.broadcasted_iota(jnp.int32, (sent, nodes), 1)
    pick = jnp.where((node == index) & (slot < count), 1.0, 0.0).astype(jnp.bfloat16)
    pick_ref[...] = pick
    copies.wait("tiles")
    size = tiles_ref.shape[2]
    lane = lax.broadcasted_iota(jnp.int32, (size, LANES), 1)
    parts = []
    for block in range(blocks):
        total = tiles_ref[block, 0].astype(jnp.float32)
        for tile in range(1, tiles):
            total = total + tiles_ref[block, tile].astype(jnp.float32)
        rowsum = jnp.sum(total, axis=1, keepdims=True)
        scaling = lax.rsqrt(1.0 + rowsum)
        side_ref[block * size : (block + 1) * size, :] = jnp.where(lane == 0, rowsum, scaling)
        high, middle, low = bits_of(scaling)
        part = jnp.where(lane == 0, high, jnp.where(lane == 1, middle, jnp.where(lane == 2, low, 0.0)))
        parts.append(part.astype(jnp.bfloat16))
    out_ref[:, width:] = dot(pick, jnp.concatenate(parts, axis=0)).astype(jnp.bfloat16)
    copies.wait("embeds")
    out_ref[:, :width] = dot(pick, embeds_ref[...]).astype(jnp.bfloat16)


def prepare(rows, count, tile_weight, embeds):
    sent = rows.shape[0] * rows.shape[1]
    nodes, width = embeds.shape
    return pl.pallas_call(
        prepare_kernel,
        in_specs=[HBM] * 4,
        out_shape=(
            jax.ShapeDtypeStruct((sent, width + LANES), jnp.bfloat16),
            jax.ShapeDtypeStruct((sent, nodes), jnp.bfloat16),
            jax.ShapeDtypeStruct((nodes, LANES), jnp.float32),
        ),
        scratch_shapes=[
            pltpu.VMEM(rows.shape, jnp.int32),
            pltpu.VMEM(count.shape, jnp.int32),
            pltpu.VMEM(tile_weight.shape, jnp.bfloat16),
            pltpu.VMEM(embeds.shape, jnp.bfloat16),
            pltpu.SemaphoreType.DMA((4,)),
        ],
        compiler_params=params(),
        name="prepare",
    )(rows, count, tile_weight, embeds)


def split_hidden(hidden, rep, mine_ref, other_ref, start):
    for pair in range(hidden.shape[1] // (2 * LANES)):
        low = hidden[:, 2 * pair * LANES : (2 * pair + 1) * LANES]
        high = hidden[:, (2 * pair + 1) * LANES : (2 * pair + 2) * LANES]
        place = slice(start // 2 + pair * LANES, start // 2 + (pair + 1) * LANES)
        mine_ref[:, place] = jnp.where(rep == 0, low, high)
        other_ref[:, place] = jnp.where(rep == 0, high, low)


def hidden_chunks(x, win_ref, wout_ref, waiting, arrive, take):
    chunk = waiting[0].shape[1]
    count = win_ref.shape[1] // chunk
    projected = None
    for step in range(count + 1):
        arrive(step)
        if step < count:
            waiting[step % 2][...] = dot(x, win_ref[:, step * chunk : (step + 1) * chunk])
        if step > 0:
            start = (step - 1) * chunk
            value, slope = gelu_pair(waiting[(step - 1) % 2][...])
            hidden = value.astype(jnp.bfloat16)
            take(start, hidden, slope)
            part = dot(hidden, wout_ref[start : start + chunk])
            projected = part if projected is None else projected + part
    return projected


class Weights:
    def __init__(self, copies, win_any, wout_any, win_ref, wout_ref, chunk):
        self.copies = copies
        self.count = win_ref.shape[1] // chunk
        for step in range(self.count):
            place = pl.ds(step * chunk, chunk)
            copies.start(("in", step), win_any.at[:, place], win_ref.at[:, place])
            copies.start(("out", step), wout_any.at[place], wout_ref.at[place])

    def wait(self, step):
        if step < self.count:
            self.copies.wait(("in", step))
        if step > 0:
            self.copies.wait(("out", step - 1))


def forward_kernel(
    rep_ref,
    column_ref,
    x_any,
    win_any,
    wout_any,
    tiles_any,
    side_any,
    rows_any,
    class_any,
    proto_any,
    slope_any,
    mine_any,
    other_any,
    grad_ref,
    weight_ref,
    back_ref,
    x_ref,
    win_ref,
    wout_ref,
    tiles_ref,
    side_ref,
    rows_ref,
    class_ref,
    proto_ref,
    slope_ref,
    mine_ref,
    other_ref,
    even_ref,
    odd_ref,
    dense_ref,
    semaphores,
):
    copies = Copies(semaphores)
    chunk = even_ref.shape[1]
    copies.start("x", x_any, x_ref)
    weights = Weights(copies, win_any, wout_any, win_ref, wout_ref, chunk)
    later = {
        "tiles": (tiles_any, tiles_ref),
        "side": (side_any, side_ref),
        "rows": (rows_any, rows_ref),
        "class": (class_any, class_ref),
        "proto": (proto_any, proto_ref),
    }
    for name, (source, target) in later.items():
        copies.start(name, source, target)
    copies.wait("x")

    def give(step):
        whole_place = pl.ds(step * chunk, chunk)
        half_place = pl.ds(step * chunk // 2, chunk // 2)
        copies.start(("slope", step), slope_ref.at[:, whole_place], slope_any.at[:, whole_place])
        copies.start(("mine", step), mine_ref.at[:, half_place], mine_any.at[:, half_place])
        copies.start(("other", step), other_ref.at[:, half_place], other_any.at[:, half_place])

    def arrive(step):
        weights.wait(step)
        if step > 1:
            give(step - 2)

    def take(start, hidden, slope):
        slope_ref[:, start : start + hidden.shape[1]] = slope.astype(jnp.bfloat16)
        split_hidden(hidden, rep_ref[0], mine_ref, other_ref, start)

    projected = hidden_chunks(x_ref[...], win_ref, wout_ref, (even_ref, odd_ref), arrive, take)
    give(weights.count - 1)
    for name in later:
        copies.wait(name)
    local_part(
        column_ref,
        tiles_ref,
        side_ref,
        projected,
        rows_ref,
        class_ref,
        proto_ref,
        grad_ref,
        weight_ref,
        back_ref,
        dense_ref,
    )
    for step in range(weights.count):
        for name in ("slope", "mine", "other"):
            copies.wait((name, step))


def local_part(
    column_ref,
    tiles_ref,
    side_ref,
    projected,
    rows_ref,
    class_ref,
    proto_ref,
    grad_ref,
    weight_ref,
    back_ref,
    dense_ref,
):
    blocks, tiles, size, _ = tiles_ref.shape
    nodes, width = projected.shape
    extent = dense_ref.shape[0]
    dense_ref[...] = jnp.zeros_like(dense_ref)
    for block in range(blocks):
        for tile in range(tiles):
            column = column_ref[block, tile]
            place = slice(block * size, (block + 1) * size)
            dense_ref[column, place, :] += tiles_ref[block, tile].astype(jnp.float32)
    dense = jnp.concatenate([dense_ref[column] for column in range(extent)], axis=1)
    high = dense.astype(jnp.bfloat16)
    low = (dense - high.astype(jnp.float32)).astype(jnp.bfloat16)
    weight_ref[0] = high[:, nodes:]
    weight_ref[1] = low[:, nodes:]
    rowsum = side_ref[:, 0:1]
    scaling = side_ref[:, 1:2]
    unit = (projected * scaling).astype(jnp.bfloat16)
    unit_float = unit.astype(jnp.float32)
    beside = jnp.concatenate([unit, jnp.ones((nodes, LANES), jnp.bfloat16)], axis=1)
    turned = dot(high, beside, 0, 0) + dot(low, beside, 0, 0)
    back_ref[...] = turned[nodes:]
    neighbour = dot(high[:, :nodes], unit) + dot(low[:, :nodes], unit)
    own = turned[:nodes, width : width + 1] * unit_float - turned[:nodes, :width]
    marked = rows_ref.shape[1]
    node = lax.broadcasted_iota(jnp.int32, (nodes, marked), 0)
    label = jnp.where(node == rows_ref[...], 1.0, 0.0)
    name = lax.broadcasted_iota(jnp.int32, (proto_ref.shape[0], marked), 0)
    named = jnp.where(name == class_ref[...], 1.0, 0.0).astype(jnp.bfloat16)
    target = dot(named, proto_ref[...], 0, 0).astype(jnp.bfloat16)
    pull = jnp.sum(label, axis=1, keepdims=True) * projected - dot(label.astype(jnp.bfloat16), target)
    grad_ref[...] = (rowsum * unit_float - neighbour + own) * scaling + pull


def forward(
    rep,
    tile_column,
    embeds,
    weight_in,
    weight_out,
    tile_weight,
    side,
    label_rows,
    label_class,
    prototypes,
    received,
    chunk=1024,
):
    nodes, depth = embeds.shape
    hidden = weight_in.shape[1]
    width = weight_out.shape[1]
    size = tile_weight.shape[2]
    low = jnp.bfloat16
    arrays = (embeds, weight_in, weight_out, tile_weight, side, label_rows, label_class, prototypes)
    return pl.pallas_call(
        forward_kernel,
        in_specs=[SMEM] * 2 + [HBM] * 8,
        out_specs=(HBM, HBM, HBM, VMEM, VMEM, VMEM),
        out_shape=(
            jax.ShapeDtypeStruct((nodes, hidden), low),
            jax.ShapeDtypeStruct((nodes, hidden // 2), low),
            jax.ShapeDtypeStruct((nodes, hidden // 2), low),
            jax.ShapeDtypeStruct((nodes, width), jnp.float32),
            jax.ShapeDtypeStruct((2, nodes, received), low),
            jax.ShapeDtypeStruct((received, width + LANES), jnp.float32),
        ),
        scratch_shapes=[pltpu.VMEM(array.shape, array.dtype) for array in arrays]
        + [
            pltpu.VMEM((nodes, hidden), low),
            pltpu.VMEM((nodes, hidden // 2), low),
            pltpu.VMEM((nodes, hidden // 2), low),
            pltpu.VMEM((nodes, chunk), jnp.float32),
            pltpu.VMEM((nodes, chunk), jnp.float32),
            pltpu.VMEM(((nodes + received) // size, nodes, size), jnp.float32),
            pltpu.SemaphoreType.DMA((6 + 5 * (hidden // chunk),)),
        ],
        compiler_params=params(),
        name="forward",
    )(rep, tile_column, *arrays)


def received_kernel(
    rep_ref,
    x_any,
    win_any,
    wout_any,
    side_any,
    grad_any,
    weight_any,
    back_any,
    mine_any,
    other_any,
    full_ref,
    turned_ref,
    return_ref,
    x_ref,
    win_ref,
    wout_ref,
    side_ref,
    grad_ref,
    weight_ref,
    back_ref,
    mine_ref,
    other_ref,
    even_ref,
    odd_ref,
    semaphores,
):
    depth = win_ref.shape[0]
    nodes, width = grad_ref.shape
    chunk = even_ref.shape[1]
    copies = Copies(semaphores)
    copies.start("x", x_any, x_ref)
    weights = Weights(copies, win_any, wout_any, win_ref, wout_ref, chunk)
    later = {
        "side": (side_any, side_ref),
        "grad": (grad_any, grad_ref),
        "weight": (weight_any, weight_ref),
        "back": (back_any, back_ref),
    }
    for name, (source, target) in later.items():
        copies.start(name, source, target)
    copies.wait("x")

    def give(step):
        place = pl.ds(step * chunk // 2, chunk // 2)
        copies.start(("mine", step), mine_ref.at[:, place], mine_any.at[:, place])
        copies.start(("other", step), other_ref.at[:, place], other_any.at[:, place])

    def arrive(step):
        weights.wait(step)
        if step > 1:
            give(step - 2)

    def take(start, hidden, slope):
        split_hidden(hidden, rep_ref[0], mine_ref, other_ref, start)

    projected = hidden_chunks(x_ref[:, :depth], win_ref, wout_ref, (even_ref, odd_ref), arrive, take)
    give(weights.count - 1)
    for name in later:
        copies.wait(name)
    scaling = jnp.sum(x_ref[:, depth:].astype(jnp.float32), axis=1, keepdims=True)
    unit = (projected * scaling).astype(jnp.bfloat16)
    neighbour = dot(weight_ref[0], unit) + dot(weight_ref[1], unit)
    full = grad_ref[...] - neighbour * side_ref[:, 1:2]
    full_ref[...] = full
    back = (back_ref[:, width : width + 1] * unit.astype(jnp.float32) - back_ref[:, :width]).astype(jnp.bfloat16)
    return_ref[...] = back
    turned_ref[:, :nodes] = full.T.astype(jnp.bfloat16)
    turned_ref[:, nodes:] = (back.astype(jnp.float32) * scaling).T.astype(jnp.bfloat16)
    for step in range(weights.count):
        copies.wait(("mine", step))
        copies.wait(("other", step))


def received_part(rep, arrived, weight_in, weight_out, side, grad, weight, back, chunk=1024):
    rows = arrived.shape[0]
    hidden = weight_in.shape[1]
    nodes, width = grad.shape
    low = jnp.bfloat16
    arrays = (arrived, weight_in, weight_out, side, grad, weight, back)
    return pl.pallas_call(
        received_kernel,
        in_specs=[SMEM] + [HBM] * 7,
        out_specs=(HBM, HBM, VMEM, VMEM, VMEM),
        out_shape=(
            jax.ShapeDtypeStruct((rows, hidden // 2), low),
            jax.ShapeDtypeStruct((rows, hidden // 2), low),
            jax.ShapeDtypeStruct((nodes, width), jnp.float32),
            jax.ShapeDtypeStruct((width, nodes + rows), low),
            jax.ShapeDtypeStruct((rows, width), low),
        ),
        scratch_shapes=[pltpu.VMEM(array.shape, array.dtype) for array in arrays]
        + [
            pltpu.VMEM((rows, hidden // 2), low),
            pltpu.VMEM((rows, hidden // 2), low),
            pltpu.VMEM((rows, chunk), jnp.float32),
            pltpu.VMEM((rows, chunk), jnp.float32),
            pltpu.SemaphoreType.DMA((5 + 4 * (hidden // chunk),)),
        ],
        compiler_params=params(),
        name="received_part",
    )(rep, *arrays)


def chip_total(arrays, turned_ref, other_ref, own_ref, came_ref, other_own_ref, other_came_ref, semaphores, total_ref, chunk):
    nodes, hidden = own_ref.shape
    copies = Copies(semaphores)
    steps = range(0, hidden, chunk)
    whole = (turned_ref, other_ref, came_ref, other_came_ref)
    copies.start(0, arrays[0], turned_ref)
    copies.start(1, arrays[1], other_ref)
    for start in steps:
        place = pl.ds(start, chunk)
        for index, target in ((2, own_ref), (3, came_ref), (4, other_own_ref), (5, other_came_ref)):
            copies.start((index, start), arrays[index].at[:, place], target.at[:, place])
    copies.wait(0)
    copies.wait(1)
    for start in steps:
        for index in range(2, 6):
            copies.wait((index, start))
        place = slice(start, start + chunk)
        total = dot(turned_ref[:, :nodes], own_ref[:, place]) + dot(turned_ref[:, nodes:], came_ref[:, place])
        total += dot(other_ref[:, :nodes], other_own_ref[:, place])
        total += dot(other_ref[:, nodes:], other_came_ref[:, place])
        for step in range(chunk // LANES):
            total_ref[start // LANES + step] = total[:, step * LANES : (step + 1) * LANES]


def total_kernel(chunk, *refs):
    chip_total(refs[:6], *refs[7:13], refs[13], refs[6], chunk)


def product_kernel(streams, chunk, place_ref, *refs):
    outputs = refs[6 : 6 + 2 * len(streams)]
    scratch = refs[6 + 2 * len(streams) :]
    total_ref = scratch[-1]
    chip_total(refs[:6], *scratch[:7], total_ref, chunk)
    for stream, (order, low, high) in enumerate(streams):
        sent_ref, kept_ref = outputs[2 * stream : 2 * stream + 2]
        for spot in range(sent_ref.shape[0]):
            sent, kept = places(spot, order[0], place_ref[0])
            sent_ref[spot] = total_ref[sent, low:high].astype(jnp.bfloat16)
            kept_ref[spot] = total_ref[kept, low:high]


def places(spot, weight, place, bit=None):
    mine = lax.rem(lax.div(place, 1 << (weight if bit is None else bit)), 2)
    base = ((spot >> weight) << (weight + 1)) | (spot & ((1 << weight) - 1))
    return base + (1 - mine) * (1 << weight), base + mine * (1 << weight)


def fold_kernel(weight, bit, place_ref, kept_ref, came_ref, sent_ref, next_ref):
    for spot in range(sent_ref.shape[0]):
        sent, kept = places(spot, weight, place_ref[0], bit)
        sent_ref[spot] = (kept_ref[sent] + came_ref[sent].astype(jnp.float32)).astype(jnp.bfloat16)
    for spot in range(sent_ref.shape[0]):
        sent, kept = places(spot, weight, place_ref[0], bit)
        next_ref[spot] = kept_ref[kept] + came_ref[kept].astype(jnp.float32)


def fold_halves(place, weight, bit, kept, came):
    half = (kept.shape[0] // 2,) + kept.shape[1:]
    return pl.pallas_call(
        functools.partial(fold_kernel, weight, bit),
        in_specs=[SMEM, VMEM, VMEM],
        out_shape=(jax.ShapeDtypeStruct(half, jnp.bfloat16), jax.ShapeDtypeStruct(half, jnp.float32)),
        compiler_params=params(12),
        name="fold_halves",
    )(place, kept, came)


def product(place, streams, operands, chunk=512):
    width = operands[0].shape[0]
    hidden = operands[2].shape[1]
    blocks = hidden // LANES
    total = (blocks, width, LANES)
    scratch = [pltpu.VMEM(array.shape, array.dtype) for array in operands]
    scratch.append(pltpu.SemaphoreType.DMA((2 + 4 * (hidden // chunk),)))
    if not streams:
        return pl.pallas_call(
            functools.partial(total_kernel, chunk),
            in_specs=[HBM] * 6,
            out_shape=jax.ShapeDtypeStruct(total, jnp.float32),
            scratch_shapes=scratch,
            compiler_params=params(),
            name="chip_total",
        )(*operands)
    shapes = []
    for _, low, high in streams:
        shapes.append(jax.ShapeDtypeStruct((blocks // 2, high - low, LANES), jnp.bfloat16))
        shapes.append(jax.ShapeDtypeStruct((blocks // 2, high - low, LANES), jnp.float32))
    return pl.pallas_call(
        functools.partial(product_kernel, streams, chunk),
        in_specs=[SMEM] + [HBM] * 6,
        out_shape=tuple(shapes),
        scratch_shapes=scratch + [pltpu.VMEM(total, jnp.float32)],
        compiler_params=params(),
        name="product",
    )(place, *operands)


def backward_kernel(
    full_any,
    pick_any,
    back_any,
    side_any,
    slope_any,
    wout_any,
    win_any,
    out_ref,
    full_ref,
    pick_ref,
    back_ref,
    side_ref,
    slope_ref,
    wout_ref,
    win_ref,
    grad_ref,
    semaphores,
):
    hidden = slope_ref.shape[1]
    depth = win_ref.shape[0]
    count = 4
    chunk, rows = hidden // count, depth // count
    copies = Copies(semaphores)
    first = ((full_any, full_ref), (pick_any, pick_ref), (back_any, back_ref), (side_any, side_ref))
    for index, (source, target) in enumerate(first):
        copies.start(index, source, target)
    for step in range(count):
        place = pl.ds(step * chunk, chunk)
        copies.start(("out", step), wout_any.at[place], wout_ref.at[place])
        copies.start(("slope", step), slope_any.at[:, place], slope_ref.at[:, place])
    for step in range(count):
        place = pl.ds(step * rows, rows)
        copies.start(("in", step), win_any.at[place], win_ref.at[place])
    for index in range(len(first)):
        copies.wait(index)
    back = dot(pick_ref[...], back_ref[...], 0, 0)
    node = (full_ref[...] + back * side_ref[:, 1:2]).astype(jnp.bfloat16)
    for step in range(count):
        place = slice(step * chunk, (step + 1) * chunk)
        copies.wait(("out", step))
        copies.wait(("slope", step))
        grad_hidden = dot(node, wout_ref[place], 1, 1)
        grad_ref[:, place] = (grad_hidden * slope_ref[:, place].astype(jnp.float32)).astype(jnp.bfloat16)
    for step in range(count):
        place = slice(step * rows, (step + 1) * rows)
        copies.wait(("in", step))
        out_ref[:, place] = dot(grad_ref[...], win_ref[place], 1, 1).astype(jnp.bfloat16)


def backward(full, pick, back, side, slope, weight_out, weight_in):
    low = jnp.bfloat16
    arrays = (full, pick, back, side, slope, weight_out, weight_in)
    return pl.pallas_call(
        backward_kernel,
        in_specs=[HBM] * 7,
        out_shape=jax.ShapeDtypeStruct((full.shape[0], weight_in.shape[0]), low),
        scratch_shapes=[pltpu.VMEM(array.shape, array.dtype) for array in arrays]
        + [pltpu.VMEM(slope.shape, low), pltpu.SemaphoreType.DMA((16,))],
        compiler_params=params(61),
        name="backward",
    )(*arrays)


def bit_orders(count):
    bits = list(range(count.bit_length() - 1))
    first = len(bits) // 3
    second = first + max(first, (len(bits) - first) // 3)
    low, middle, high = bits[:first], bits[first:second], bits[second:]
    return (low + middle + high, middle + low + high, high + low + middle)


def streams_of(dom_count, width):
    cut = width * 3 // 8
    edges = (0, cut, 2 * cut, width)
    return tuple(zip(bit_orders(dom_count), edges[:-1], edges[1:]))


def halves(part, spot, mine):
    sent = lax.dynamic_index_in_dim(part, 1 - mine, spot, keepdims=False).astype(jnp.bfloat16)
    return sent, lax.dynamic_index_in_dim(part, mine, spot, keepdims=False)


def exchange(sent, bit):
    dom_count = lax.axis_size("dom")
    return lax.ppermute(sent, "dom", [(device, device ^ (1 << bit)) for device in range(dom_count)])


def body(
    embeds,
    weight_in,
    weight_out,
    prototypes,
    tile_column,
    tile_weight,
    send_rows,
    send_count,
    label_rows,
    label_class,
):
    nodes = embeds.shape[0]
    dom_count = lax.axis_size("dom")
    rep_count = lax.axis_size("rep")
    peers = dom_count * rep_count
    slots = send_rows.shape[2]
    hidden_width, width = weight_out.shape
    depth = hidden_width // peers
    place = lax.axis_index("dom")
    rep = lax.axis_index("rep")
    swap = [(0, 1), (1, 0)]
    fold = LANES // depth
    if fold > 1:
        order = (dom_count // fold, fold, rep_count, depth)
        weight_in = weight_in.reshape((-1,) + order).swapaxes(2, 3).reshape(-1, hidden_width)
        weight_out = weight_out.reshape(order + (-1,)).swapaxes(1, 2).reshape(hidden_width, -1)

    outgoing, pick, side = prepare(send_rows[0].T, send_count, tile_weight, embeds)
    arrived = lax.all_to_all(
        outgoing.reshape(peers, slots, -1), both, split_axis=0, concat_axis=0, tiled=True
    ).reshape(peers * slots, -1)
    slope, own, sent_own, grad, weight, back = forward(
        rep[None],
        tile_column,
        embeds,
        weight_in,
        weight_out,
        tile_weight,
        side,
        label_rows[None, :],
        label_class[None, :],
        prototypes,
        peers * slots,
    )
    other_own = lax.ppermute(sent_own, "rep", swap)
    came, sent_came, full, turned, returned = received_part(
        rep[None], arrived, weight_in, weight_out, side, grad, weight, back
    )
    other_turned = lax.ppermute(turned, "rep", swap)
    other_came = lax.ppermute(sent_came, "rep", swap)
    operands = (turned, other_turned, own, came, other_own, other_came)

    streams = streams_of(dom_count, width)
    bit_count = dom_count.bit_length() - 1
    parts = []
    if fold > 1:
        total = product(place[None], (), operands)
        total = total.reshape(-1, width, fold, depth).swapaxes(1, 2).reshape((2,) * bit_count + (width, depth))
        for order, low, high in streams:
            spot = bit_count - 1 - order[0]
            pair = halves(total[..., low:high, :], spot, (place >> order[0]) & 1)
            parts.append(tuple(array.reshape(-1, high - low, depth) for array in pair))
    else:
        flat = product(place[None], streams, operands)
        parts = [tuple(flat[2 * stream : 2 * stream + 2]) for stream in range(len(streams))]
    parts, returned = lax.optimization_barrier((parts, returned))
    given = lax.all_to_all(
        returned.reshape(peers, slots, width), both, split_axis=0, concat_axis=0, tiled=True
    ).reshape(peers * slots, width)
    left = [[bit for bit in range(bit_count) if bit != order[0]] for order, _, _ in streams]
    for step in range(bit_count - 1):
        if step == 1:
            parts, full = lax.optimization_barrier((parts, full))
        later = []
        for (sent, kept), bits, (order, _, _) in zip(parts, left, streams):
            bit = order[step + 1]
            later.append(fold_halves(place[None], bits.index(bit), bit, kept, exchange(sent, order[step])))
            bits.remove(bit)
        parts = later
    sums = [
        kept[0] + exchange(sent, order[-1])[0].astype(jnp.float32)
        for (sent, kept), (order, _, _) in zip(parts, streams)
    ]
    summed = jnp.concatenate(sums, axis=0)
    embed_grad = backward(full, pick, given, side, slope, weight_out, weight_in)
    return (embed_grad, summed.T * (1.0 / math.sqrt(nodes * peers)))


def solution(mesh):
    placed = (
        P(both, None),
        P(),
        P(),
        P(),
        P(both, None),
        P(both, None, None, None),
        P(both, None, None),
        P(both, None),
        P(both),
        P(both),
    )
    return jax.shard_map(
        body,
        mesh=mesh,
        in_specs=placed,
        out_specs=(P(both, None), P(both, None)),
        check_vma=False,
    )
```

```python
import functools
import math

import jax
import jax.numpy as jnp
from jax import lax
from jax.experimental import pallas as pl
from jax.experimental.pallas import tpu as pltpu
from jax.sharding import PartitionSpec as P

gelu_inner = 0.7978845608028654
gelu_cubic = 0.044715
LANES = 128
MIB = 1024 * 1024
both = ("dom", "rep")


def gelu_pair(values):
    square = values * values
    half = 0.5 + 0.5 * jnp.tanh(values * (gelu_inner + gelu_inner * gelu_cubic * square))
    value = values * half
    slope = half + value * (2.0 - 2.0 * half) * (gelu_inner + 3.0 * gelu_inner * gelu_cubic * square)
    return value, slope


def dot(left, right, left_dim=1, right_dim=0):
    return lax.dot_general(
        left, right, (((left_dim,), (right_dim,)), ((), ())), preferred_element_type=jnp.float32
    )


def params(mib=64):
    return pltpu.CompilerParams(vmem_limit_bytes=mib * MIB)


VMEM = pl.BlockSpec(memory_space=pltpu.VMEM)
SMEM = pl.BlockSpec(memory_space=pltpu.SMEM)
HBM = pl.BlockSpec(memory_space=pltpu.HBM)


class Copies:
    def __init__(self, semaphores):
        self.semaphores = semaphores
        self.started = {}

    def start(self, name, source, target):
        copy = pltpu.make_async_copy(source, target, self.semaphores.at[len(self.started)])
        copy.start()
        self.started[name] = copy

    def wait(self, name):
        self.started[name].wait()


def bits_of(values):
    high = values.astype(jnp.bfloat16).astype(jnp.float32)
    middle = (values - high).astype(jnp.bfloat16).astype(jnp.float32)
    return high, middle, values - high - middle


def prepare_kernel(
    rows_any,
    count_any,
    tiles_any,
    embeds_any,
    out_ref,
    pick_ref,
    side_ref,
    rows_ref,
    count_ref,
    tiles_ref,
    embeds_ref,
    semaphores,
):
    copies = Copies(semaphores)
    copies.start("rows", rows_any, rows_ref)
    copies.start("count", count_any, count_ref)
    copies.start("tiles", tiles_any, tiles_ref)
    copies.start("embeds", embeds_any, embeds_ref)
    copies.wait("rows")
    copies.wait("count")
    slots, peers = rows_ref.shape
    nodes, width = embeds_ref.shape
    sent = slots * peers
    blocks, tiles = tiles_ref.shape[:2]
    spread = jnp.concatenate([rows_ref[...].astype(jnp.float32)] * peers, axis=0)
    row = lax.broadcasted_iota(jnp.int32, (sent, peers), 0)
    chosen = lax.div(row, slots) == lax.broadcasted_iota(jnp.int32, (sent, peers), 1)
    index = jnp.sum(jnp.where(chosen, spread, 0.0), axis=1, keepdims=True).astype(jnp.int32)
    counts = jnp.broadcast_to(count_ref[...].astype(jnp.float32), (sent, peers))
    count = jnp.sum(jnp.where(chosen, counts, 0.0), axis=1, keepdims=True).astype(jnp.int32)
    slot = lax.rem(lax.broadcasted_iota(jnp.int32, (sent, nodes), 0), slots)
    node = lax.broadcasted_iota(jnp.int32, (sent, nodes), 1)
    pick = jnp.where((node == index) & (slot < count), 1.0, 0.0).astype(jnp.bfloat16)
    pick_ref[...] = pick
    copies.wait("tiles")
    size = tiles_ref.shape[2]
    lane = lax.broadcasted_iota(jnp.int32, (size, LANES), 1)
    parts = []
    for block in range(blocks):
        total = tiles_ref[block, 0].astype(jnp.float32)
        for tile in range(1, tiles):
            total = total + tiles_ref[block, tile].astype(jnp.float32)
        rowsum = jnp.sum(total, axis=1, keepdims=True)
        scaling = lax.rsqrt(1.0 + rowsum)
        side_ref[block * size : (block + 1) * size, :] = jnp.where(lane == 0, rowsum, scaling)
        high, middle, low = bits_of(scaling)
        part = jnp.where(lane == 0, high, jnp.where(lane == 1, middle, jnp.where(lane == 2, low, 0.0)))
        parts.append(part.astype(jnp.bfloat16))
    out_ref[:, width:] = dot(pick, jnp.concatenate(parts, axis=0)).astype(jnp.bfloat16)
    copies.wait("embeds")
    out_ref[:, :width] = dot(pick, embeds_ref[...]).astype(jnp.bfloat16)


def prepare(rows, count, tile_weight, embeds):
    sent = rows.shape[0] * rows.shape[1]
    nodes, width = embeds.shape
    return pl.pallas_call(
        prepare_kernel,
        in_specs=[HBM] * 4,
        out_shape=(
            jax.ShapeDtypeStruct((sent, width + LANES), jnp.bfloat16),
            jax.ShapeDtypeStruct((sent, nodes), jnp.bfloat16),
            jax.ShapeDtypeStruct((nodes, LANES), jnp.float32),
        ),
        scratch_shapes=[
            pltpu.VMEM(rows.shape, jnp.int32),
            pltpu.VMEM(count.shape, jnp.int32),
            pltpu.VMEM(tile_weight.shape, jnp.bfloat16),
            pltpu.VMEM(embeds.shape, jnp.bfloat16),
            pltpu.SemaphoreType.DMA((4,)),
        ],
        compiler_params=params(),
        name="prepare",
    )(rows, count, tile_weight, embeds)


def split_hidden(hidden, rep, mine_ref, other_ref, start):
    for pair in range(hidden.shape[1] // (2 * LANES)):
        low = hidden[:, 2 * pair * LANES : (2 * pair + 1) * LANES]
        high = hidden[:, (2 * pair + 1) * LANES : (2 * pair + 2) * LANES]
        place = slice(start // 2 + pair * LANES, start // 2 + (pair + 1) * LANES)
        mine_ref[:, place] = jnp.where(rep == 0, low, high)
        other_ref[:, place] = jnp.where(rep == 0, high, low)


def hidden_chunks(x, win_ref, wout_ref, waiting, arrive, take):
    chunk = waiting[0].shape[1]
    count = win_ref.shape[1] // chunk
    projected = None
    for step in range(count + 1):
        arrive(step)
        if step < count:
            waiting[step % 2][...] = dot(x, win_ref[:, step * chunk : (step + 1) * chunk])
        if step > 0:
            start = (step - 1) * chunk
            value, slope = gelu_pair(waiting[(step - 1) % 2][...])
            hidden = value.astype(jnp.bfloat16)
            take(start, hidden, slope)
            part = dot(hidden, wout_ref[start : start + chunk])
            projected = part if projected is None else projected + part
    return projected


class Weights:
    def __init__(self, copies, win_any, wout_any, win_ref, wout_ref, chunk):
        self.copies = copies
        self.count = win_ref.shape[1] // chunk
        for step in range(self.count):
            place = pl.ds(step * chunk, chunk)
            copies.start(("in", step), win_any.at[:, place], win_ref.at[:, place])
            copies.start(("out", step), wout_any.at[place], wout_ref.at[place])

    def wait(self, step):
        if step < self.count:
            self.copies.wait(("in", step))
        if step > 0:
            self.copies.wait(("out", step - 1))


def forward_kernel(
    rep_ref,
    column_ref,
    x_any,
    win_any,
    wout_any,
    tiles_any,
    side_any,
    rows_any,
    class_any,
    proto_any,
    slope_any,
    mine_any,
    other_any,
    grad_any,
    weight_any,
    back_any,
    x_ref,
    win_ref,
    wout_ref,
    tiles_ref,
    side_ref,
    rows_ref,
    class_ref,
    proto_ref,
    slope_ref,
    mine_ref,
    other_ref,
    even_ref,
    odd_ref,
    dense_ref,
    high_ref,
    low_ref,
    grad_ref,
    back_ref,
    semaphores,
):
    copies = Copies(semaphores)
    chunk = even_ref.shape[1]
    copies.start("x", x_any, x_ref)
    copies.start("tiles", tiles_any, tiles_ref)
    weights = Weights(copies, win_any, wout_any, win_ref, wout_ref, chunk)
    later = {
        "side": (side_any, side_ref),
        "rows": (rows_any, rows_ref),
        "class": (class_any, class_ref),
        "proto": (proto_any, proto_ref),
    }
    for name, (source, target) in later.items():
        copies.start(name, source, target)
    nodes = x_ref.shape[0]
    copies.wait("x")

    def give(step):
        whole_place = pl.ds(step * chunk, chunk)
        half_place = pl.ds(step * chunk // 2, chunk // 2)
        copies.start(("slope", step), slope_ref.at[:, whole_place], slope_any.at[:, whole_place])
        copies.start(("mine", step), mine_ref.at[:, half_place], mine_any.at[:, half_place])
        copies.start(("other", step), other_ref.at[:, half_place], other_any.at[:, half_place])

    def arrive(step):
        weights.wait(step)
        if step > 1:
            give(step - 2)
        if step == 0:
            copies.wait("tiles")
            dense_graph(column_ref, tiles_ref, dense_ref, high_ref, low_ref)
        if step == 1:
            extra = pl.ds(nodes, high_ref.shape[1] - nodes)
            copies.start("high", high_ref.at[:, extra], weight_any.at[0])
            copies.start("low", low_ref.at[:, extra], weight_any.at[1])

    def take(start, hidden, slope):
        slope_ref[:, start : start + hidden.shape[1]] = slope.astype(jnp.bfloat16)
        split_hidden(hidden, rep_ref[0], mine_ref, other_ref, start)

    projected = hidden_chunks(x_ref[...], win_ref, wout_ref, (even_ref, odd_ref), arrive, take)
    give(weights.count - 1)
    for name in later:
        copies.wait(name)
    width = projected.shape[1]
    rowsum = side_ref[:, 0:1]
    scaling = side_ref[:, 1:2]
    unit = (projected * scaling).astype(jnp.bfloat16)
    unit_float = unit.astype(jnp.float32)
    beside = jnp.concatenate([unit, jnp.ones((nodes, LANES), jnp.bfloat16)], axis=1)
    high, low = high_ref[...], low_ref[...]
    turned = dot(high, beside, 0, 0) + dot(low, beside, 0, 0)
    back_ref[...] = turned[nodes:]
    copies.start("back", back_ref, back_any)
    neighbour = dot(high[:, :nodes], unit) + dot(low[:, :nodes], unit)
    own = turned[:nodes, width : width + 1] * unit_float - turned[:nodes, :width]
    marked = rows_ref.shape[1]
    node = lax.broadcasted_iota(jnp.int32, (nodes, marked), 0)
    label = jnp.where(node == rows_ref[...], 1.0, 0.0)
    name = lax.broadcasted_iota(jnp.int32, (proto_ref.shape[0], marked), 0)
    named = jnp.where(name == class_ref[...], 1.0, 0.0).astype(jnp.bfloat16)
    target = dot(named, proto_ref[...], 0, 0).astype(jnp.bfloat16)
    pull = jnp.sum(label, axis=1, keepdims=True) * projected - dot(label.astype(jnp.bfloat16), target)
    grad_ref[...] = (rowsum * unit_float - neighbour + own) * scaling + pull
    copies.start("grad", grad_ref, grad_any)
    for step in range(weights.count):
        for name in ("slope", "mine", "other"):
            copies.wait((name, step))
    for name in ("high", "low", "back", "grad"):
        copies.wait(name)


def dense_graph(column_ref, tiles_ref, dense_ref, high_ref, low_ref):
    blocks, tiles, size, _ = tiles_ref.shape
    dense_ref[...] = jnp.zeros_like(dense_ref)
    for block in range(blocks):
        for tile in range(tiles):
            column = column_ref[block, tile]
            place = slice(block * size, (block + 1) * size)
            dense_ref[column, place, :] += tiles_ref[block, tile].astype(jnp.float32)
    for column in range(dense_ref.shape[0]):
        dense = dense_ref[column]
        high = dense.astype(jnp.bfloat16)
        place = slice(column * size, (column + 1) * size)
        high_ref[:, place] = high
        low_ref[:, place] = (dense - high.astype(jnp.float32)).astype(jnp.bfloat16)


def forward(
    rep,
    tile_column,
    embeds,
    weight_in,
    weight_out,
    tile_weight,
    side,
    label_rows,
    label_class,
    prototypes,
    received,
    chunk=1024,
):
    nodes, depth = embeds.shape
    hidden = weight_in.shape[1]
    width = weight_out.shape[1]
    size = tile_weight.shape[2]
    low = jnp.bfloat16
    arrays = (embeds, weight_in, weight_out, tile_weight, side, label_rows, label_class, prototypes)
    return pl.pallas_call(
        forward_kernel,
        in_specs=[SMEM] * 2 + [HBM] * 8,
        out_specs=(HBM,) * 6,
        out_shape=(
            jax.ShapeDtypeStruct((nodes, hidden), low),
            jax.ShapeDtypeStruct((nodes, hidden // 2), low),
            jax.ShapeDtypeStruct((nodes, hidden // 2), low),
            jax.ShapeDtypeStruct((nodes, width), jnp.float32),
            jax.ShapeDtypeStruct((2, nodes, received), low),
            jax.ShapeDtypeStruct((received, width + LANES), jnp.float32),
        ),
        scratch_shapes=[pltpu.VMEM(array.shape, array.dtype) for array in arrays]
        + [
            pltpu.VMEM((nodes, hidden), low),
            pltpu.VMEM((nodes, hidden // 2), low),
            pltpu.VMEM((nodes, hidden // 2), low),
            pltpu.VMEM((nodes, chunk), jnp.float32),
            pltpu.VMEM((nodes, chunk), jnp.float32),
            pltpu.VMEM(((nodes + received) // size, nodes, size), jnp.float32),
            pltpu.VMEM((nodes, nodes + received), low),
            pltpu.VMEM((nodes, nodes + received), low),
            pltpu.VMEM((nodes, width), jnp.float32),
            pltpu.VMEM((received, width + LANES), jnp.float32),
            pltpu.SemaphoreType.DMA((10 + 5 * (hidden // chunk),)),
        ],
        compiler_params=params(),
        name="forward",
    )(rep, tile_column, *arrays)


def received_kernel(
    rep_ref,
    x_any,
    win_any,
    wout_any,
    side_any,
    grad_any,
    weight_any,
    back_any,
    mine_any,
    other_any,
    full_ref,
    turned_ref,
    return_ref,
    x_ref,
    win_ref,
    wout_ref,
    side_ref,
    grad_ref,
    weight_ref,
    back_ref,
    mine_ref,
    other_ref,
    even_ref,
    odd_ref,
    semaphores,
):
    depth = win_ref.shape[0]
    nodes, width = grad_ref.shape
    chunk = even_ref.shape[1]
    copies = Copies(semaphores)
    copies.start("x", x_any, x_ref)
    weights = Weights(copies, win_any, wout_any, win_ref, wout_ref, chunk)
    later = {
        "side": (side_any, side_ref),
        "grad": (grad_any, grad_ref),
        "weight": (weight_any, weight_ref),
        "back": (back_any, back_ref),
    }
    for name, (source, target) in later.items():
        copies.start(name, source, target)
    copies.wait("x")

    def give(step):
        place = pl.ds(step * chunk // 2, chunk // 2)
        copies.start(("mine", step), mine_ref.at[:, place], mine_any.at[:, place])
        copies.start(("other", step), other_ref.at[:, place], other_any.at[:, place])

    def arrive(step):
        weights.wait(step)
        if step > 1:
            give(step - 2)

    def take(start, hidden, slope):
        split_hidden(hidden, rep_ref[0], mine_ref, other_ref, start)

    projected = hidden_chunks(x_ref[:, :depth], win_ref, wout_ref, (even_ref, odd_ref), arrive, take)
    give(weights.count - 1)
    for name in later:
        copies.wait(name)
    scaling = jnp.sum(x_ref[:, depth:].astype(jnp.float32), axis=1, keepdims=True)
    unit = (projected * scaling).astype(jnp.bfloat16)
    neighbour = dot(weight_ref[0], unit) + dot(weight_ref[1], unit)
    full = grad_ref[...] - neighbour * side_ref[:, 1:2]
    full_ref[...] = full
    back = (back_ref[:, width : width + 1] * unit.astype(jnp.float32) - back_ref[:, :width]).astype(jnp.bfloat16)
    return_ref[...] = back
    turned_ref[:, :nodes] = full.T.astype(jnp.bfloat16)
    turned_ref[:, nodes:] = (back.astype(jnp.float32) * scaling).T.astype(jnp.bfloat16)
    for step in range(weights.count):
        copies.wait(("mine", step))
        copies.wait(("other", step))


def received_part(rep, arrived, weight_in, weight_out, side, grad, weight, back, chunk=1024):
    rows = arrived.shape[0]
    hidden = weight_in.shape[1]
    nodes, width = grad.shape
    low = jnp.bfloat16
    arrays = (arrived, weight_in, weight_out, side, grad, weight, back)
    return pl.pallas_call(
        received_kernel,
        in_specs=[SMEM] + [HBM] * 7,
        out_specs=(HBM, HBM, VMEM, VMEM, VMEM),
        out_shape=(
            jax.ShapeDtypeStruct((rows, hidden // 2), low),
            jax.ShapeDtypeStruct((rows, hidden // 2), low),
            jax.ShapeDtypeStruct((nodes, width), jnp.float32),
            jax.ShapeDtypeStruct((width, nodes + rows), low),
            jax.ShapeDtypeStruct((rows, width), low),
        ),
        scratch_shapes=[pltpu.VMEM(array.shape, array.dtype) for array in arrays]
        + [
            pltpu.VMEM((rows, hidden // 2), low),
            pltpu.VMEM((rows, hidden // 2), low),
            pltpu.VMEM((rows, chunk), jnp.float32),
            pltpu.VMEM((rows, chunk), jnp.float32),
            pltpu.SemaphoreType.DMA((5 + 4 * (hidden // chunk),)),
        ],
        compiler_params=params(),
        name="received_part",
    )(rep, *arrays)


def chip_total(chunk, arrays, turned_ref, hidden_ref, semaphores, total_ref):
    copies = Copies(semaphores)
    steps = range(0, hidden_ref.shape[1], chunk)
    base = 0
    for index in range(2):
        length = arrays[index].shape[1]
        copies.start(index, arrays[index], turned_ref.at[:, pl.ds(base, length)])
        base += length
    for start in steps:
        place = pl.ds(start, chunk)
        base = 0
        for index in range(2, 6):
            length = arrays[index].shape[0]
            copies.start((index, start), arrays[index].at[:, place], hidden_ref.at[pl.ds(base, length), place])
            base += length
    copies.wait(0)
    copies.wait(1)
    for start in steps:
        for index in range(2, 6):
            copies.wait((index, start))
        total = dot(turned_ref[...], hidden_ref[:, start : start + chunk])
        for step in range(chunk // LANES):
            total_ref[start // LANES + step] = total[:, step * LANES : (step + 1) * LANES]


def total_kernel(chunk, *refs):
    chip_total(chunk, refs[:6], *refs[7:10], refs[6])


def product_kernel(streams, chunk, place_ref, *refs):
    outputs = refs[6 : 6 + 2 * len(streams)]
    turned_ref, hidden_ref, semaphores, total_ref = refs[6 + 2 * len(streams) :]
    chip_total(chunk, refs[:6], turned_ref, hidden_ref, semaphores, total_ref)
    for stream, (order, low, high) in enumerate(streams):
        sent_ref, kept_ref = outputs[2 * stream : 2 * stream + 2]
        for spot in range(sent_ref.shape[0]):
            sent, kept = places(spot, order[0], place_ref[0])
            sent_ref[spot] = total_ref[sent, low:high].astype(jnp.bfloat16)
            kept_ref[spot] = total_ref[kept, low:high]


def places(spot, weight, place, bit=None):
    mine = lax.rem(lax.div(place, 1 << (weight if bit is None else bit)), 2)
    base = ((spot >> weight) << (weight + 1)) | (spot & ((1 << weight) - 1))
    return base + (1 - mine) * (1 << weight), base + mine * (1 << weight)


def fold_kernel(digits, merge, place_ref, *refs):
    count = len(digits)
    outputs = refs[2 * count :]
    base = 0
    for stream, (weight, bit) in enumerate(digits):
        kept_ref, came_ref = refs[2 * stream : 2 * stream + 2]
        target = max(stream - 1, 0) if merge else stream
        if not (merge and stream == 1):
            base = 0
        sent_ref, next_ref = outputs[2 * target : 2 * target + 2]
        rows = slice(base, base + kept_ref.shape[1])
        base = rows.stop
        for spot in range(sent_ref.shape[0]):
            sent, kept = places(spot, weight, place_ref[0], bit)
            sent_ref[spot, rows] = (kept_ref[sent] + came_ref[sent].astype(jnp.float32)).astype(jnp.bfloat16)
            next_ref[spot, rows] = kept_ref[kept] + came_ref[kept].astype(jnp.float32)


def fold_halves(place, digits, merge, kept, came):
    heights = [array.shape[1] for array in kept]
    if merge:
        heights = [heights[0] + heights[1]] + heights[2:]
    blocks, _, depth = kept[0].shape
    shapes = []
    for height in heights:
        shapes.append(jax.ShapeDtypeStruct((blocks // 2, height, depth), jnp.bfloat16))
        shapes.append(jax.ShapeDtypeStruct((blocks // 2, height, depth), jnp.float32))
    operands = [array for pair in zip(kept, came) for array in pair]
    flat = pl.pallas_call(
        functools.partial(fold_kernel, digits, merge),
        in_specs=[SMEM] + [VMEM] * len(operands),
        out_shape=tuple(shapes),
        compiler_params=params(16),
        name="fold_halves",
    )(place, *operands)
    return [tuple(flat[2 * stream : 2 * stream + 2]) for stream in range(len(heights))]


def finish_kernel(factor, *refs):
    base = 0
    for stream in range(len(refs) // 2):
        kept_ref, came_ref = refs[2 * stream : 2 * stream + 2]
        rows = kept_ref.shape[1]
        total = kept_ref[0] + came_ref[0].astype(jnp.float32)
        refs[-1][:, base : base + rows] = total.T * factor
        base += rows


def finish(factor, kept, came):
    width = sum(array.shape[1] for array in kept)
    return pl.pallas_call(
        functools.partial(finish_kernel, factor),
        out_shape=jax.ShapeDtypeStruct((kept[0].shape[2], width), jnp.float32),
        compiler_params=params(16),
        name="finish",
    )(*[array for pair in zip(kept, came) for array in pair])


def product(place, streams, operands, chunk=512):
    width = operands[0].shape[0]
    hidden = operands[2].shape[1]
    blocks = hidden // LANES
    total = (blocks, width, LANES)
    rows = 2 * operands[0].shape[1]
    scratch = [
        pltpu.VMEM((width, rows), jnp.bfloat16),
        pltpu.VMEM((rows, hidden), jnp.bfloat16),
        pltpu.SemaphoreType.DMA((2 + 4 * (hidden // chunk),)),
    ]
    if not streams:
        return pl.pallas_call(
            functools.partial(total_kernel, chunk),
            in_specs=[HBM] * 6,
            out_shape=jax.ShapeDtypeStruct(total, jnp.float32),
            scratch_shapes=scratch,
            compiler_params=params(),
            name="chip_total",
        )(*operands)
    shapes = []
    for _, low, high in streams:
        shapes.append(jax.ShapeDtypeStruct((blocks // 2, high - low, LANES), jnp.bfloat16))
        shapes.append(jax.ShapeDtypeStruct((blocks // 2, high - low, LANES), jnp.float32))
    return pl.pallas_call(
        functools.partial(product_kernel, streams, chunk),
        in_specs=[SMEM] + [HBM] * 6,
        out_shape=tuple(shapes),
        scratch_shapes=scratch + [pltpu.VMEM(total, jnp.float32)],
        compiler_params=params(60),
        name="product",
    )(place, *operands)


def slope_kernel(chunk, *refs):
    full_any, pick_any, back_any, side_any, slope_any, wout_any, out_any = refs[:7]
    full_ref, pick_ref, back_ref, side_ref, slope_ref, wout_ref, grad_ref, semaphores = refs[7:]
    copies = Copies(semaphores)
    first = ((full_any, full_ref), (pick_any, pick_ref), (back_any, back_ref), (side_any, side_ref))
    steps = range(0, slope_ref.shape[1], chunk)
    for index, (source, target) in enumerate(first):
        copies.start(index, source, target)
    for start in steps:
        place = pl.ds(start, chunk)
        copies.start(("out", start), wout_any.at[place], wout_ref.at[place])
        copies.start(("slope", start), slope_any.at[:, place], slope_ref.at[:, place])
    for index in range(len(first)):
        copies.wait(index)
    back = dot(pick_ref[...], back_ref[...], 0, 0)
    node = (full_ref[...] + back * side_ref[:, 1:2]).astype(jnp.bfloat16)
    for start in steps:
        copies.wait(("out", start))
        copies.wait(("slope", start))
        place = slice(start, start + chunk)
        grad_hidden = dot(node, wout_ref[place], 1, 1)
        grad_ref[:, place] = (grad_hidden * slope_ref[:, place].astype(jnp.float32)).astype(jnp.bfloat16)
        copies.start(("grad", start), grad_ref.at[:, pl.ds(start, chunk)], out_any.at[:, pl.ds(start, chunk)])
    for start in steps:
        copies.wait(("grad", start))


def slope_part(full, pick, back, side, slope, weight_out, chunk=1024):
    arrays = (full, pick, back, side, slope, weight_out)
    return pl.pallas_call(
        functools.partial(slope_kernel, chunk),
        in_specs=[HBM] * 6,
        out_specs=HBM,
        out_shape=jax.ShapeDtypeStruct(slope.shape, jnp.bfloat16),
        scratch_shapes=[pltpu.VMEM(array.shape, array.dtype) for array in arrays]
        + [
            pltpu.VMEM(slope.shape, jnp.bfloat16),
            pltpu.SemaphoreType.DMA((4 + 3 * (slope.shape[1] // chunk),)),
        ],
        cost_estimate=pl.CostEstimate(flops=2 * slope.size * full.shape[1], bytes_accessed=16 * MIB, transcendentals=0),
        compiler_params=params(60),
        name="slope_part",
    )(*arrays)


def embed_kernel(chunk, grad_any, win_any, out_ref, grad_ref, win_ref, total_ref, semaphores):
    copies = Copies(semaphores)
    steps = range(0, grad_ref.shape[1], chunk)
    for start in steps:
        place = pl.ds(start, chunk)
        copies.start(("grad", start), grad_any.at[:, place], grad_ref.at[:, place])
        copies.start(("in", start), win_any.at[:, place], win_ref.at[:, place])
    for start in steps:
        copies.wait(("grad", start))
        copies.wait(("in", start))
        place = slice(start, start + chunk)
        part = dot(grad_ref[:, place], win_ref[:, place], 1, 1)
        if start == 0:
            total_ref[...] = part
        elif start + chunk < grad_ref.shape[1]:
            total_ref[...] += part
        else:
            out_ref[...] = (total_ref[...] + part).astype(jnp.bfloat16)


def embed_part(grad, weight_in, chunk=1024):
    nodes, hidden = grad.shape
    depth = weight_in.shape[0]
    return pl.pallas_call(
        functools.partial(embed_kernel, chunk),
        in_specs=[HBM] * 2,
        out_shape=jax.ShapeDtypeStruct((nodes, depth), jnp.bfloat16),
        scratch_shapes=[
            pltpu.VMEM(grad.shape, jnp.bfloat16),
            pltpu.VMEM(weight_in.shape, jnp.bfloat16),
            pltpu.VMEM((nodes, depth), jnp.float32),
            pltpu.SemaphoreType.DMA((2 * (hidden // chunk),)),
        ],
        cost_estimate=pl.CostEstimate(flops=2 * grad.size * depth, bytes_accessed=13 * MIB, transcendentals=0),
        compiler_params=params(60),
        name="embed_part",
    )(grad, weight_in)


def bit_orders(count):
    bits = list(range(count.bit_length() - 1))
    first = len(bits) // 3
    second = first + max(first, (len(bits) - first) // 3)
    low, middle, high = bits[:first], bits[first:second], bits[second:]
    return (low + middle + high, middle + low + high, high + low + middle)


def streams_of(dom_count, width):
    cut = width * 3 // 8
    edges = (0, cut, 2 * cut, width)
    return tuple(zip(bit_orders(dom_count), edges[:-1], edges[1:]))


def halves(part, spot, mine):
    sent = lax.dynamic_index_in_dim(part, 1 - mine, spot, keepdims=False).astype(jnp.bfloat16)
    return sent, lax.dynamic_index_in_dim(part, mine, spot, keepdims=False)


def exchange(sent, bit):
    dom_count = lax.axis_size("dom")
    return lax.ppermute(sent, "dom", [(device, device ^ (1 << bit)) for device in range(dom_count)])


def body(
    embeds,
    weight_in,
    weight_out,
    prototypes,
    tile_column,
    tile_weight,
    send_rows,
    send_count,
    label_rows,
    label_class,
):
    nodes = embeds.shape[0]
    dom_count = lax.axis_size("dom")
    rep_count = lax.axis_size("rep")
    peers = dom_count * rep_count
    slots = send_rows.shape[2]
    hidden_width, width = weight_out.shape
    depth = hidden_width // peers
    place = lax.axis_index("dom")
    rep = lax.axis_index("rep")
    swap = [(0, 1), (1, 0)]
    fold = LANES // depth
    if fold > 1:
        order = (dom_count // fold, fold, rep_count, depth)
        weight_in = weight_in.reshape((-1,) + order).swapaxes(2, 3).reshape(-1, hidden_width)
        weight_out = weight_out.reshape(order + (-1,)).swapaxes(1, 2).reshape(hidden_width, -1)

    outgoing, pick, side = prepare(send_rows[0].T, send_count, tile_weight, embeds)
    arrived = lax.all_to_all(
        outgoing.reshape(peers, slots, -1), both, split_axis=0, concat_axis=0, tiled=True
    ).reshape(peers * slots, -1)
    slope, own, sent_own, grad, weight, back = forward(
        rep[None],
        tile_column,
        embeds,
        weight_in,
        weight_out,
        tile_weight,
        side,
        label_rows[None, :],
        label_class[None, :],
        prototypes,
        peers * slots,
    )
    other_own = lax.ppermute(sent_own, "rep", swap)
    came, sent_came, full, turned, returned = received_part(
        rep[None], arrived, weight_in, weight_out, side, grad, weight, back
    )
    other_turned = lax.ppermute(turned, "rep", swap)
    other_came = lax.ppermute(sent_came, "rep", swap)
    given = lax.all_to_all(
        returned.reshape(peers, slots, width), both, split_axis=0, concat_axis=0, tiled=True
    ).reshape(peers * slots, width)
    operands = (turned, other_turned, own, came, other_own, other_came)

    streams = streams_of(dom_count, width)
    bit_count = dom_count.bit_length() - 1
    parts = []
    if fold > 1:
        total = product(place[None], (), operands)
        total = total.reshape(-1, width, fold, depth).swapaxes(1, 2).reshape((2,) * bit_count + (width, depth))
        for order, low, high in streams:
            spot = bit_count - 1 - order[0]
            pair = halves(total[..., low:high, :], spot, (place >> order[0]) & 1)
            parts.append(tuple(array.reshape(-1, high - low, depth) for array in pair))
    else:
        flat = product(place[None], streams, operands)
        parts = [tuple(flat[2 * stream : 2 * stream + 2]) for stream in range(len(streams))]
    parts, full = lax.optimization_barrier((parts, full))
    grad_pre = slope_part(full, pick, given, side, slope, weight_out)
    left = [[bit for bit in range(bit_count) if bit != order[0]] for order, _, _ in streams]
    orders = [order for order, _, _ in streams]
    shared = next(step for step in range(bit_count) if orders[0][step:] == orders[1][step:])
    embed_grad = None
    for step in range(bit_count):
        came = [exchange(sent, order[step]) for (sent, _), order in zip(parts, orders)]
        if step == 0:
            came, grad_pre = lax.optimization_barrier((came, grad_pre))
        elif step == 1:
            came, embed_grad = lax.optimization_barrier((came, embed_grad))
        else:
            came = lax.optimization_barrier(came)
        kept = [array for _, array in parts]
        if step + 1 == bit_count:
            break
        digits = [(bits.index(order[step + 1]), order[step + 1]) for bits, order in zip(left, orders)]
        for bits, order in zip(left, orders):
            bits.remove(order[step + 1])
        parts = fold_halves(place[None], digits, step + 1 == shared, kept, came)
        if step + 1 == shared:
            left, orders = left[1:], orders[1:]
        if step == 0:
            parts, grad_pre = lax.optimization_barrier((parts, grad_pre))
            embed_grad = embed_part(grad_pre, weight_in)
        else:
            parts = lax.optimization_barrier(parts)
    summed = finish(1.0 / math.sqrt(nodes * peers), kept, came)
    return (embed_grad, summed)


def solution(mesh):
    placed = (
        P(both, None),
        P(),
        P(),
        P(),
        P(both, None),
        P(both, None, None, None),
        P(both, None, None),
        P(both, None),
        P(both),
        P(both),
    )
    return jax.shard_map(
        body,
        mesh=mesh,
        in_specs=placed,
        out_specs=(P(both, None), P(both, None)),
        check_vma=False,
    )
```

```python
import functools
import math

import jax
import jax.numpy as jnp
from jax import lax
from jax.experimental import pallas as pl
from jax.experimental.pallas import tpu as pltpu
from jax.sharding import PartitionSpec as P

gelu_inner = 0.7978845608028654
gelu_cubic = 0.044715
LANES = 128
MIB = 1024 * 1024
both = ("dom", "rep")


def gelu_pair(values):
    square = values * values
    half = 0.5 + 0.5 * jnp.tanh(values * (gelu_inner + gelu_inner * gelu_cubic * square))
    value = values * half
    slope = half + value * (2.0 - 2.0 * half) * (gelu_inner + 3.0 * gelu_inner * gelu_cubic * square)
    return value, slope


def dot(left, right, left_dim=1, right_dim=0):
    return lax.dot_general(
        left, right, (((left_dim,), (right_dim,)), ((), ())), preferred_element_type=jnp.float32
    )


def params(mib=64):
    return pltpu.CompilerParams(vmem_limit_bytes=mib * MIB)


VMEM = pl.BlockSpec(memory_space=pltpu.VMEM)
SMEM = pl.BlockSpec(memory_space=pltpu.SMEM)
HBM = pl.BlockSpec(memory_space=pltpu.HBM)


class Copies:
    def __init__(self, semaphores):
        self.semaphores = semaphores
        self.started = {}

    def start(self, name, source, target):
        copy = pltpu.make_async_copy(source, target, self.semaphores.at[len(self.started)])
        copy.start()
        self.started[name] = copy

    def wait(self, name):
        self.started[name].wait()


def bits_of(values):
    high = values.astype(jnp.bfloat16).astype(jnp.float32)
    middle = (values - high).astype(jnp.bfloat16).astype(jnp.float32)
    return high, middle, values - high - middle


def prepare_kernel(
    rows_any,
    count_any,
    tiles_any,
    embeds_any,
    out_ref,
    pick_ref,
    side_ref,
    rows_ref,
    count_ref,
    tiles_ref,
    embeds_ref,
    semaphores,
):
    copies = Copies(semaphores)
    copies.start("rows", rows_any, rows_ref)
    copies.start("count", count_any, count_ref)
    copies.start("tiles", tiles_any, tiles_ref)
    copies.start("embeds", embeds_any, embeds_ref)
    copies.wait("rows")
    copies.wait("count")
    slots, peers = rows_ref.shape
    nodes, width = embeds_ref.shape
    sent = slots * peers
    blocks, tiles = tiles_ref.shape[:2]
    spread = jnp.concatenate([rows_ref[...].astype(jnp.float32)] * peers, axis=0)
    row = lax.broadcasted_iota(jnp.int32, (sent, peers), 0)
    chosen = lax.div(row, slots) == lax.broadcasted_iota(jnp.int32, (sent, peers), 1)
    index = jnp.sum(jnp.where(chosen, spread, 0.0), axis=1, keepdims=True).astype(jnp.int32)
    counts = jnp.broadcast_to(count_ref[...].astype(jnp.float32), (sent, peers))
    count = jnp.sum(jnp.where(chosen, counts, 0.0), axis=1, keepdims=True).astype(jnp.int32)
    slot = lax.rem(lax.broadcasted_iota(jnp.int32, (sent, nodes), 0), slots)
    node = lax.broadcasted_iota(jnp.int32, (sent, nodes), 1)
    pick = jnp.where((node == index) & (slot < count), 1.0, 0.0).astype(jnp.bfloat16)
    pick_ref[...] = pick
    copies.wait("tiles")
    size = tiles_ref.shape[2]
    lane = lax.broadcasted_iota(jnp.int32, (size, LANES), 1)
    parts = []
    for block in range(blocks):
        total = tiles_ref[block, 0].astype(jnp.float32)
        for tile in range(1, tiles):
            total = total + tiles_ref[block, tile].astype(jnp.float32)
        rowsum = jnp.sum(total, axis=1, keepdims=True)
        scaling = lax.rsqrt(1.0 + rowsum)
        side_ref[block * size : (block + 1) * size, :] = jnp.where(lane == 0, rowsum, scaling)
        high, middle, low = bits_of(scaling)
        part = jnp.where(lane == 0, high, jnp.where(lane == 1, middle, jnp.where(lane == 2, low, 0.0)))
        parts.append(part.astype(jnp.bfloat16))
    out_ref[:, width:] = dot(pick, jnp.concatenate(parts, axis=0)).astype(jnp.bfloat16)
    copies.wait("embeds")
    out_ref[:, :width] = dot(pick, embeds_ref[...]).astype(jnp.bfloat16)


def prepare(rows, count, tile_weight, embeds):
    sent = rows.shape[0] * rows.shape[1]
    nodes, width = embeds.shape
    return pl.pallas_call(
        prepare_kernel,
        in_specs=[HBM] * 4,
        out_shape=(
            jax.ShapeDtypeStruct((sent, width + LANES), jnp.bfloat16),
            jax.ShapeDtypeStruct((sent, nodes), jnp.bfloat16),
            jax.ShapeDtypeStruct((nodes, LANES), jnp.float32),
        ),
        scratch_shapes=[
            pltpu.VMEM(rows.shape, jnp.int32),
            pltpu.VMEM(count.shape, jnp.int32),
            pltpu.VMEM(tile_weight.shape, jnp.bfloat16),
            pltpu.VMEM(embeds.shape, jnp.bfloat16),
            pltpu.SemaphoreType.DMA((4,)),
        ],
        compiler_params=params(),
        name="prepare",
    )(rows, count, tile_weight, embeds)


def split_hidden(hidden, rep, mine_ref, other_ref, start):
    for pair in range(hidden.shape[1] // (2 * LANES)):
        low = hidden[:, 2 * pair * LANES : (2 * pair + 1) * LANES]
        high = hidden[:, (2 * pair + 1) * LANES : (2 * pair + 2) * LANES]
        place = slice(start // 2 + pair * LANES, start // 2 + (pair + 1) * LANES)
        mine_ref[:, place] = jnp.where(rep == 0, low, high)
        other_ref[:, place] = jnp.where(rep == 0, high, low)


def hidden_chunks(x, win_ref, wout_ref, waiting, arrive, take, piece=256):
    chunk = waiting[0].shape[1]
    count = win_ref.shape[1] // chunk
    projected = None
    for step in range(count + 1):
        arrive(step)
        for low in range(0, chunk, piece):
            place = slice(low, low + piece)
            if step < count:
                ahead = step * chunk + low
                waiting[step % 2][:, place] = dot(x, win_ref[:, ahead : ahead + piece])
            if step > 0:
                start = (step - 1) * chunk + low
                value, slope = gelu_pair(waiting[(step - 1) % 2][:, place])
                hidden = value.astype(jnp.bfloat16)
                take(start, hidden, slope)
                part = dot(hidden, wout_ref[start : start + piece])
                projected = part if projected is None else projected + part
    return projected


class Weights:
    def __init__(self, copies, win_any, wout_any, win_ref, wout_ref, chunk):
        self.copies = copies
        self.count = win_ref.shape[1] // chunk
        for step in range(self.count):
            place = pl.ds(step * chunk, chunk)
            copies.start(("in", step), win_any.at[:, place], win_ref.at[:, place])
            copies.start(("out", step), wout_any.at[place], wout_ref.at[place])

    def wait(self, step):
        if step < self.count:
            self.copies.wait(("in", step))
        if step > 0:
            self.copies.wait(("out", step - 1))


def forward_kernel(
    rep_ref,
    column_ref,
    x_any,
    win_any,
    wout_any,
    tiles_any,
    side_any,
    rows_any,
    class_any,
    proto_any,
    slope_any,
    mine_any,
    other_any,
    grad_any,
    weight_any,
    back_any,
    x_ref,
    win_ref,
    wout_ref,
    tiles_ref,
    side_ref,
    rows_ref,
    class_ref,
    proto_ref,
    slope_ref,
    mine_ref,
    other_ref,
    even_ref,
    odd_ref,
    dense_ref,
    high_ref,
    low_ref,
    grad_ref,
    back_ref,
    semaphores,
):
    copies = Copies(semaphores)
    chunk = even_ref.shape[1]
    copies.start("x", x_any, x_ref)
    copies.start("tiles", tiles_any, tiles_ref)
    weights = Weights(copies, win_any, wout_any, win_ref, wout_ref, chunk)
    later = {
        "side": (side_any, side_ref),
        "rows": (rows_any, rows_ref),
        "class": (class_any, class_ref),
        "proto": (proto_any, proto_ref),
    }
    for name, (source, target) in later.items():
        copies.start(name, source, target)
    nodes = x_ref.shape[0]
    copies.wait("x")

    def give(step):
        whole_place = pl.ds(step * chunk, chunk)
        half_place = pl.ds(step * chunk // 2, chunk // 2)
        copies.start(("slope", step), slope_ref.at[:, whole_place], slope_any.at[:, whole_place])
        copies.start(("mine", step), mine_ref.at[:, half_place], mine_any.at[:, half_place])
        copies.start(("other", step), other_ref.at[:, half_place], other_any.at[:, half_place])

    def arrive(step):
        weights.wait(step)
        if step > 1:
            give(step - 2)
        if step == 0:
            copies.wait("tiles")
            dense_graph(column_ref, tiles_ref, dense_ref, high_ref, low_ref)
        if step == 1:
            extra = pl.ds(nodes, high_ref.shape[1] - nodes)
            copies.start("high", high_ref.at[:, extra], weight_any.at[0])
            copies.start("low", low_ref.at[:, extra], weight_any.at[1])

    def take(start, hidden, slope):
        slope_ref[:, start : start + hidden.shape[1]] = slope.astype(jnp.bfloat16)
        split_hidden(hidden, rep_ref[0], mine_ref, other_ref, start)

    projected = hidden_chunks(x_ref[...], win_ref, wout_ref, (even_ref, odd_ref), arrive, take)
    give(weights.count - 1)
    for name in later:
        copies.wait(name)
    width = projected.shape[1]
    rowsum = side_ref[:, 0:1]
    scaling = side_ref[:, 1:2]
    unit = (projected * scaling).astype(jnp.bfloat16)
    unit_float = unit.astype(jnp.float32)
    beside = jnp.concatenate([unit, jnp.ones((nodes, LANES), jnp.bfloat16)], axis=1)
    high, low = high_ref[...], low_ref[...]
    turned = dot(high, beside, 0, 0) + dot(low, beside, 0, 0)
    back_ref[...] = turned[nodes:]
    copies.start("back", back_ref, back_any)
    neighbour = dot(high[:, :nodes], unit) + dot(low[:, :nodes], unit)
    own = turned[:nodes, width : width + 1] * unit_float - turned[:nodes, :width]
    marked = rows_ref.shape[1]
    node = lax.broadcasted_iota(jnp.int32, (nodes, marked), 0)
    label = jnp.where(node == rows_ref[...], 1.0, 0.0)
    name = lax.broadcasted_iota(jnp.int32, (proto_ref.shape[0], marked), 0)
    named = jnp.where(name == class_ref[...], 1.0, 0.0).astype(jnp.bfloat16)
    target = dot(named, proto_ref[...], 0, 0).astype(jnp.bfloat16)
    pull = jnp.sum(label, axis=1, keepdims=True) * projected - dot(label.astype(jnp.bfloat16), target)
    grad_ref[...] = (rowsum * unit_float - neighbour + own) * scaling + pull
    copies.start("grad", grad_ref, grad_any)
    for step in range(weights.count):
        for name in ("slope", "mine", "other"):
            copies.wait((name, step))
    for name in ("high", "low", "back", "grad"):
        copies.wait(name)


def dense_graph(column_ref, tiles_ref, dense_ref, high_ref, low_ref):
    blocks, tiles, size, _ = tiles_ref.shape
    dense_ref[...] = jnp.zeros_like(dense_ref)
    for block in range(blocks):
        for tile in range(tiles):
            column = column_ref[block, tile]
            place = slice(block * size, (block + 1) * size)
            dense_ref[column, place, :] += tiles_ref[block, tile].astype(jnp.float32)
    for column in range(dense_ref.shape[0]):
        dense = dense_ref[column]
        high = dense.astype(jnp.bfloat16)
        place = slice(column * size, (column + 1) * size)
        high_ref[:, place] = high
        low_ref[:, place] = (dense - high.astype(jnp.float32)).astype(jnp.bfloat16)


def forward(
    rep,
    tile_column,
    embeds,
    weight_in,
    weight_out,
    tile_weight,
    side,
    label_rows,
    label_class,
    prototypes,
    received,
    chunk=1024,
):
    nodes, depth = embeds.shape
    hidden = weight_in.shape[1]
    width = weight_out.shape[1]
    size = tile_weight.shape[2]
    low = jnp.bfloat16
    arrays = (embeds, weight_in, weight_out, tile_weight, side, label_rows, label_class, prototypes)
    return pl.pallas_call(
        forward_kernel,
        in_specs=[SMEM] * 2 + [HBM] * 8,
        out_specs=(HBM,) * 6,
        out_shape=(
            jax.ShapeDtypeStruct((nodes, hidden), low),
            jax.ShapeDtypeStruct((nodes, hidden // 2), low),
            jax.ShapeDtypeStruct((nodes, hidden // 2), low),
            jax.ShapeDtypeStruct((nodes, width), jnp.float32),
            jax.ShapeDtypeStruct((2, nodes, received), low),
            jax.ShapeDtypeStruct((received, width + LANES), jnp.float32),
        ),
        scratch_shapes=[pltpu.VMEM(array.shape, array.dtype) for array in arrays]
        + [
            pltpu.VMEM((nodes, hidden), low),
            pltpu.VMEM((nodes, hidden // 2), low),
            pltpu.VMEM((nodes, hidden // 2), low),
            pltpu.VMEM((nodes, chunk), jnp.float32),
            pltpu.VMEM((nodes, chunk), jnp.float32),
            pltpu.VMEM(((nodes + received) // size, nodes, size), jnp.float32),
            pltpu.VMEM((nodes, nodes + received), low),
            pltpu.VMEM((nodes, nodes + received), low),
            pltpu.VMEM((nodes, width), jnp.float32),
            pltpu.VMEM((received, width + LANES), jnp.float32),
            pltpu.SemaphoreType.DMA((10 + 5 * (hidden // chunk),)),
        ],
        compiler_params=params(),
        name="forward",
    )(rep, tile_column, *arrays)


def received_kernel(
    rep_ref,
    x_any,
    win_any,
    wout_any,
    side_any,
    grad_any,
    weight_any,
    back_any,
    mine_any,
    other_any,
    full_ref,
    turned_ref,
    return_ref,
    x_ref,
    win_ref,
    wout_ref,
    side_ref,
    grad_ref,
    weight_ref,
    back_ref,
    mine_ref,
    other_ref,
    even_ref,
    odd_ref,
    semaphores,
):
    depth = win_ref.shape[0]
    nodes, width = grad_ref.shape
    chunk = even_ref.shape[1]
    copies = Copies(semaphores)
    copies.start("x", x_any, x_ref)
    weights = Weights(copies, win_any, wout_any, win_ref, wout_ref, chunk)
    later = {
        "side": (side_any, side_ref),
        "grad": (grad_any, grad_ref),
        "weight": (weight_any, weight_ref),
        "back": (back_any, back_ref),
    }
    for name, (source, target) in later.items():
        copies.start(name, source, target)
    copies.wait("x")

    def give(step):
        place = pl.ds(step * chunk // 2, chunk // 2)
        copies.start(("mine", step), mine_ref.at[:, place], mine_any.at[:, place])
        copies.start(("other", step), other_ref.at[:, place], other_any.at[:, place])

    def arrive(step):
        weights.wait(step)
        if step > 1:
            give(step - 2)

    def take(start, hidden, slope):
        split_hidden(hidden, rep_ref[0], mine_ref, other_ref, start)

    projected = hidden_chunks(x_ref[:, :depth], win_ref, wout_ref, (even_ref, odd_ref), arrive, take)
    give(weights.count - 1)
    for name in later:
        copies.wait(name)
    scaling = jnp.sum(x_ref[:, depth:].astype(jnp.float32), axis=1, keepdims=True)
    unit = (projected * scaling).astype(jnp.bfloat16)
    neighbour = dot(weight_ref[0], unit) + dot(weight_ref[1], unit)
    full = grad_ref[...] - neighbour * side_ref[:, 1:2]
    full_ref[...] = full
    back = (back_ref[:, width : width + 1] * unit.astype(jnp.float32) - back_ref[:, :width]).astype(jnp.bfloat16)
    return_ref[...] = back
    turned_ref[:, :nodes] = full.T.astype(jnp.bfloat16)
    turned_ref[:, nodes:] = (back.astype(jnp.float32) * scaling).T.astype(jnp.bfloat16)
    for step in range(weights.count):
        copies.wait(("mine", step))
        copies.wait(("other", step))


def received_part(rep, arrived, weight_in, weight_out, side, grad, weight, back, chunk=512):
    rows = arrived.shape[0]
    hidden = weight_in.shape[1]
    nodes, width = grad.shape
    low = jnp.bfloat16
    arrays = (arrived, weight_in, weight_out, side, grad, weight, back)
    return pl.pallas_call(
        received_kernel,
        in_specs=[SMEM] + [HBM] * 7,
        out_specs=(HBM, HBM, VMEM, VMEM, VMEM),
        out_shape=(
            jax.ShapeDtypeStruct((rows, hidden // 2), low),
            jax.ShapeDtypeStruct((rows, hidden // 2), low),
            jax.ShapeDtypeStruct((nodes, width), jnp.float32),
            jax.ShapeDtypeStruct((width, nodes + rows), low),
            jax.ShapeDtypeStruct((rows, width), low),
        ),
        scratch_shapes=[pltpu.VMEM(array.shape, array.dtype) for array in arrays]
        + [
            pltpu.VMEM((rows, hidden // 2), low),
            pltpu.VMEM((rows, hidden // 2), low),
            pltpu.VMEM((rows, chunk), jnp.float32),
            pltpu.VMEM((rows, chunk), jnp.float32),
            pltpu.SemaphoreType.DMA((5 + 4 * (hidden // chunk),)),
        ],
        compiler_params=params(),
        name="received_part",
    )(rep, *arrays)


def chip_total(chunk, copies, arrays, turned_ref, hidden_ref, total_ref, arrive):
    steps = range(0, hidden_ref.shape[1], chunk)
    base = 0
    for index in range(2):
        length = arrays[index].shape[1]
        copies.start(index, arrays[index], turned_ref.at[:, pl.ds(base, length)])
        base += length
    for start in steps:
        place = pl.ds(start, chunk)
        base = 0
        for index in range(2, 6):
            length = arrays[index].shape[0]
            copies.start((index, start), arrays[index].at[:, place], hidden_ref.at[pl.ds(base, length), place])
            base += length
    copies.wait(0)
    copies.wait(1)
    for start in steps:
        for index in range(2, 6):
            copies.wait((index, start))
        arrive(start // LANES)
        total = dot(turned_ref[...], hidden_ref[:, start : start + chunk])
        for step in range(chunk // LANES):
            total_ref[start // LANES + step] = total[:, step * LANES : (step + 1) * LANES]


def total_kernel(chunk, *refs):
    turned_ref, hidden_ref, semaphores = refs[7:]
    chip_total(chunk, Copies(semaphores), refs[:6], turned_ref, hidden_ref, refs[6], lambda ready: None)


def product_kernel(streams, chunk, place_ref, *refs):
    count = 2 * len(streams)
    outputs, scratch = refs[6 : 6 + count], refs[6 + count : 6 + 2 * count]
    turned_ref, hidden_ref, semaphores, total_ref = refs[6 + 2 * count :]
    copies = Copies(semaphores)
    done = [0] * len(streams)

    def arrive(ready):
        given = []
        for stream, (order, low, high) in enumerate(streams):
            bit = order[0]
            first = done[stream]
            spot = first
            while spot < scratch[2 * stream].shape[0]:
                base = ((spot >> bit) << (bit + 1)) | (spot & ((1 << bit) - 1))
                if base + (1 << bit) >= ready:
                    break
                sent, kept = places(spot, bit, place_ref[0])
                scratch[2 * stream][spot] = total_ref[sent, low:high].astype(jnp.bfloat16)
                scratch[2 * stream + 1][spot] = total_ref[kept, low:high]
                spot += 1
            done[stream] = spot
            if spot > first:
                given += [(2 * stream, first, spot), (2 * stream + 1, first, spot)]
        for index, first, last in given:
            place = pl.ds(first, last - first)
            copies.start(("give", index, first), scratch[index].at[place], outputs[index].at[place])

    chip_total(chunk, copies, refs[:6], turned_ref, hidden_ref, total_ref, arrive)
    arrive(total_ref.shape[0])
    for name in list(copies.started):
        if isinstance(name, tuple) and name[0] == "give":
            copies.wait(name)


def places(spot, weight, place, bit=None):
    mine = lax.rem(lax.div(place, 1 << (weight if bit is None else bit)), 2)
    base = ((spot >> weight) << (weight + 1)) | (spot & ((1 << weight) - 1))
    return base + (1 - mine) * (1 << weight), base + mine * (1 << weight)


def fold_kernel(digits, merge, place_ref, *refs):
    count = len(digits)
    outputs = refs[2 * count :]
    base = 0
    for stream, (weight, bit) in enumerate(digits):
        kept_ref, came_ref = refs[2 * stream : 2 * stream + 2]
        target = max(stream - 1, 0) if merge else stream
        if not (merge and stream == 1):
            base = 0
        sent_ref, next_ref = outputs[2 * target : 2 * target + 2]
        rows = slice(base, base + kept_ref.shape[1])
        base = rows.stop
        for spot in range(sent_ref.shape[0]):
            sent, kept = places(spot, weight, place_ref[0], bit)
            sent_ref[spot, rows] = (kept_ref[sent] + came_ref[sent].astype(jnp.float32)).astype(jnp.bfloat16)
            next_ref[spot, rows] = kept_ref[kept] + came_ref[kept].astype(jnp.float32)


def fold_halves(place, digits, merge, kept, came):
    heights = [array.shape[1] for array in kept]
    if merge:
        heights = [heights[0] + heights[1]] + heights[2:]
    blocks, _, depth = kept[0].shape
    shapes = []
    for height in heights:
        shapes.append(jax.ShapeDtypeStruct((blocks // 2, height, depth), jnp.bfloat16))
        shapes.append(jax.ShapeDtypeStruct((blocks // 2, height, depth), jnp.float32))
    operands = [array for pair in zip(kept, came) for array in pair]
    flat = pl.pallas_call(
        functools.partial(fold_kernel, digits, merge),
        in_specs=[SMEM] + [VMEM] * len(operands),
        out_shape=tuple(shapes),
        compiler_params=params(16),
        name="fold_halves",
    )(place, *operands)
    return [tuple(flat[2 * stream : 2 * stream + 2]) for stream in range(len(heights))]


def finish_kernel(factor, *refs):
    base = 0
    for stream in range(len(refs) // 2):
        kept_ref, came_ref = refs[2 * stream : 2 * stream + 2]
        rows = kept_ref.shape[1]
        total = kept_ref[0] + came_ref[0].astype(jnp.float32)
        refs[-1][:, base : base + rows] = total.T * factor
        base += rows


def finish(factor, kept, came):
    width = sum(array.shape[1] for array in kept)
    return pl.pallas_call(
        functools.partial(finish_kernel, factor),
        out_shape=jax.ShapeDtypeStruct((kept[0].shape[2], width), jnp.float32),
        compiler_params=params(16),
        name="finish",
    )(*[array for pair in zip(kept, came) for array in pair])


def product(place, streams, operands, chunk=512):
    width = operands[0].shape[0]
    hidden = operands[2].shape[1]
    blocks = hidden // LANES
    total = (blocks, width, LANES)
    rows = 2 * operands[0].shape[1]
    scratch = [
        pltpu.VMEM((width, rows), jnp.bfloat16),
        pltpu.VMEM((rows, hidden), jnp.bfloat16),
        pltpu.SemaphoreType.DMA((2 + 10 * (hidden // chunk),)),
    ]
    if not streams:
        return pl.pallas_call(
            functools.partial(total_kernel, chunk),
            in_specs=[HBM] * 6,
            out_shape=jax.ShapeDtypeStruct(total, jnp.float32),
            scratch_shapes=scratch,
            compiler_params=params(),
            name="chip_total",
        )(*operands)
    shapes = []
    for _, low, high in streams:
        shapes.append(jax.ShapeDtypeStruct((blocks // 2, high - low, LANES), jnp.bfloat16))
        shapes.append(jax.ShapeDtypeStruct((blocks // 2, high - low, LANES), jnp.float32))
    return pl.pallas_call(
        functools.partial(product_kernel, streams, chunk),
        in_specs=[SMEM] + [HBM] * 6,
        out_specs=(HBM,) * len(shapes),
        out_shape=tuple(shapes),
        scratch_shapes=[pltpu.VMEM(shape.shape, shape.dtype) for shape in shapes]
        + scratch
        + [pltpu.VMEM(total, jnp.float32)],
        compiler_params=params(),
        name="product",
    )(place, *operands)


def slope_kernel(chunk, *refs):
    full_any, pick_any, back_any, side_any, slope_any, wout_any, out_any = refs[:7]
    full_ref, pick_ref, back_ref, side_ref, slope_ref, wout_ref, grad_ref, semaphores = refs[7:]
    copies = Copies(semaphores)
    first = ((full_any, full_ref), (pick_any, pick_ref), (back_any, back_ref), (side_any, side_ref))
    steps = range(0, slope_ref.shape[1], chunk)
    for index, (source, target) in enumerate(first):
        copies.start(index, source, target)
    for start in steps:
        place = pl.ds(start, chunk)
        copies.start(("out", start), wout_any.at[place], wout_ref.at[place])
        copies.start(("slope", start), slope_any.at[:, place], slope_ref.at[:, place])
    for index in range(len(first)):
        copies.wait(index)
    back = dot(pick_ref[...], back_ref[...], 0, 0)
    node = (full_ref[...] + back * side_ref[:, 1:2]).astype(jnp.bfloat16)
    for start in steps:
        copies.wait(("out", start))
        copies.wait(("slope", start))
        place = slice(start, start + chunk)
        grad_hidden = dot(node, wout_ref[place], 1, 1)
        grad_ref[:, place] = (grad_hidden * slope_ref[:, place].astype(jnp.float32)).astype(jnp.bfloat16)
        copies.start(("grad", start), grad_ref.at[:, pl.ds(start, chunk)], out_any.at[:, pl.ds(start, chunk)])
    for start in steps:
        copies.wait(("grad", start))


def slope_part(full, pick, back, side, slope, weight_out, chunk=1024):
    arrays = (full, pick, back, side, slope, weight_out)
    return pl.pallas_call(
        functools.partial(slope_kernel, chunk),
        in_specs=[HBM] * 6,
        out_specs=HBM,
        out_shape=jax.ShapeDtypeStruct(slope.shape, jnp.bfloat16),
        scratch_shapes=[pltpu.VMEM(array.shape, array.dtype) for array in arrays]
        + [
            pltpu.VMEM(slope.shape, jnp.bfloat16),
            pltpu.SemaphoreType.DMA((4 + 3 * (slope.shape[1] // chunk),)),
        ],
        cost_estimate=pl.CostEstimate(flops=2 * slope.size * full.shape[1], bytes_accessed=16 * MIB, transcendentals=0),
        compiler_params=params(58),
        name="slope_part",
    )(*arrays)


def embed_kernel(chunk, grad_any, win_any, out_ref, grad_ref, win_ref, total_ref, semaphores):
    copies = Copies(semaphores)
    steps = range(0, grad_ref.shape[1], chunk)
    for start in steps:
        place = pl.ds(start, chunk)
        copies.start(("grad", start), grad_any.at[:, place], grad_ref.at[:, place])
        copies.start(("in", start), win_any.at[:, place], win_ref.at[:, place])
    for start in steps:
        copies.wait(("grad", start))
        copies.wait(("in", start))
        place = slice(start, start + chunk)
        part = dot(grad_ref[:, place], win_ref[:, place], 1, 1)
        if start == 0:
            total_ref[...] = part
        elif start + chunk < grad_ref.shape[1]:
            total_ref[...] += part
        else:
            out_ref[...] = (total_ref[...] + part).astype(jnp.bfloat16)


def embed_part(grad, weight_in, chunk=1024):
    nodes, hidden = grad.shape
    depth = weight_in.shape[0]
    return pl.pallas_call(
        functools.partial(embed_kernel, chunk),
        in_specs=[HBM] * 2,
        out_shape=jax.ShapeDtypeStruct((nodes, depth), jnp.bfloat16),
        scratch_shapes=[
            pltpu.VMEM(grad.shape, jnp.bfloat16),
            pltpu.VMEM(weight_in.shape, jnp.bfloat16),
            pltpu.VMEM((nodes, depth), jnp.float32),
            pltpu.SemaphoreType.DMA((2 * (hidden // chunk),)),
        ],
        cost_estimate=pl.CostEstimate(flops=2 * grad.size * depth, bytes_accessed=13 * MIB, transcendentals=0),
        compiler_params=params(60),
        name="embed_part",
    )(grad, weight_in)


def bit_orders(count):
    bits = list(range(count.bit_length() - 1))
    first = len(bits) // 3
    second = first + max(first, (len(bits) - first) // 3)
    low, middle, high = bits[:first], bits[first:second], bits[second:]
    return (low + middle + high, middle + low + high, high + low + middle)


def streams_of(dom_count, width):
    cut = width * 11 // 32
    edges = (0, cut, 2 * cut, width)
    return tuple(zip(bit_orders(dom_count), edges[:-1], edges[1:]))


def halves(part, spot, mine):
    sent = lax.dynamic_index_in_dim(part, 1 - mine, spot, keepdims=False).astype(jnp.bfloat16)
    return sent, lax.dynamic_index_in_dim(part, mine, spot, keepdims=False)


def exchange(sent, bit):
    dom_count = lax.axis_size("dom")
    return lax.ppermute(sent, "dom", [(device, device ^ (1 << bit)) for device in range(dom_count)])


def body(
    embeds,
    weight_in,
    weight_out,
    prototypes,
    tile_column,
    tile_weight,
    send_rows,
    send_count,
    label_rows,
    label_class,
):
    nodes = embeds.shape[0]
    dom_count = lax.axis_size("dom")
    rep_count = lax.axis_size("rep")
    peers = dom_count * rep_count
    slots = send_rows.shape[2]
    hidden_width, width = weight_out.shape
    depth = hidden_width // peers
    place = lax.axis_index("dom")
    rep = lax.axis_index("rep")
    swap = [(0, 1), (1, 0)]
    fold = LANES // depth
    if fold > 1:
        order = (dom_count // fold, fold, rep_count, depth)
        weight_in = weight_in.reshape((-1,) + order).swapaxes(2, 3).reshape(-1, hidden_width)
        weight_out = weight_out.reshape(order + (-1,)).swapaxes(1, 2).reshape(hidden_width, -1)

    outgoing, pick, side = prepare(send_rows[0].T, send_count, tile_weight, embeds)
    arrived = lax.all_to_all(
        outgoing.reshape(peers, slots, -1), both, split_axis=0, concat_axis=0, tiled=True
    ).reshape(peers * slots, -1)
    slope, own, sent_own, grad, weight, back = forward(
        rep[None],
        tile_column,
        embeds,
        weight_in,
        weight_out,
        tile_weight,
        side,
        label_rows[None, :],
        label_class[None, :],
        prototypes,
        peers * slots,
    )
    other_own = lax.ppermute(sent_own, "rep", swap)
    came, sent_came, full, turned, returned = received_part(
        rep[None], arrived, weight_in, weight_out, side, grad, weight, back
    )
    other_turned = lax.ppermute(turned, "rep", swap)
    other_came = lax.ppermute(sent_came, "rep", swap)
    given = lax.all_to_all(
        returned.reshape(peers, slots, width), both, split_axis=0, concat_axis=0, tiled=True
    ).reshape(peers * slots, width)
    operands = (turned, other_turned, own, came, other_own, other_came)

    streams = streams_of(dom_count, width)
    bit_count = dom_count.bit_length() - 1
    parts = []
    if fold > 1:
        total = product(place[None], (), operands)
        total = total.reshape(-1, width, fold, depth).swapaxes(1, 2).reshape((2,) * bit_count + (width, depth))
        for order, low, high in streams:
            spot = bit_count - 1 - order[0]
            pair = halves(total[..., low:high, :], spot, (place >> order[0]) & 1)
            parts.append(tuple(array.reshape(-1, high - low, depth) for array in pair))
    else:
        flat = product(place[None], streams, operands)
        parts = [tuple(flat[2 * stream : 2 * stream + 2]) for stream in range(len(streams))]
    parts, full = lax.optimization_barrier((parts, full))
    grad_pre = slope_part(full, pick, given, side, slope, weight_out)
    left = [[bit for bit in range(bit_count) if bit != order[0]] for order, _, _ in streams]
    orders = [order for order, _, _ in streams]
    shared = next(step for step in range(bit_count) if orders[0][step:] == orders[1][step:])
    embed_grad = None
    for step in range(bit_count):
        came = [exchange(sent, order[step]) for (sent, _), order in zip(parts, orders)]
        if step == 0:
            came, grad_pre = lax.optimization_barrier((came, grad_pre))
        elif step == 1:
            came, embed_grad = lax.optimization_barrier((came, embed_grad))
        else:
            came = lax.optimization_barrier(came)
        kept = [array for _, array in parts]
        if step + 1 == bit_count:
            break
        digits = [(bits.index(order[step + 1]), order[step + 1]) for bits, order in zip(left, orders)]
        for bits, order in zip(left, orders):
            bits.remove(order[step + 1])
        parts = fold_halves(place[None], digits, step + 1 == shared, kept, came)
        if step + 1 == shared:
            left, orders = left[1:], orders[1:]
        if step == 0:
            parts, grad_pre = lax.optimization_barrier((parts, grad_pre))
            embed_grad = embed_part(grad_pre, weight_in)
        else:
            parts = lax.optimization_barrier(parts)
    summed = finish(1.0 / math.sqrt(nodes * peers), kept, came)
    return (embed_grad, summed)


def solution(mesh):
    placed = (
        P(both, None),
        P(),
        P(),
        P(),
        P(both, None),
        P(both, None, None, None),
        P(both, None, None),
        P(both, None),
        P(both),
        P(both),
    )
    return jax.shard_map(
        body,
        mesh=mesh,
        in_specs=placed,
        out_specs=(P(both, None), P(both, None)),
        check_vma=False,
    )
```

```python
import functools
import math

import jax
import jax.numpy as jnp
from jax import lax
from jax.experimental import pallas as pl
from jax.experimental.pallas import tpu as pltpu
from jax.sharding import PartitionSpec as P

gelu_inner = 0.7978845608028654
gelu_cubic = 0.044715
LANES = 128
SLOPED = 2048
MIB = 1024 * 1024
both = ("dom", "rep")


def gelu_half(values):
    square = values * values
    return 0.5 + 0.5 * jnp.tanh(values * (gelu_inner + gelu_inner * gelu_cubic * square)), square


def gelu_slope(values, half, square):
    return half + values * half * (2.0 - 2.0 * half) * (gelu_inner + 3.0 * gelu_inner * gelu_cubic * square)


def dot(left, right, left_dim=1, right_dim=0):
    return lax.dot_general(
        left, right, (((left_dim,), (right_dim,)), ((), ())), preferred_element_type=jnp.float32
    )


def params(mib=64):
    return pltpu.CompilerParams(vmem_limit_bytes=mib * MIB)


VMEM = pl.BlockSpec(memory_space=pltpu.VMEM)
SMEM = pl.BlockSpec(memory_space=pltpu.SMEM)
HBM = pl.BlockSpec(memory_space=pltpu.HBM)


class Copies:
    def __init__(self, semaphores):
        self.semaphores = semaphores
        self.started = {}

    def start(self, name, source, target):
        copy = pltpu.make_async_copy(source, target, self.semaphores.at[len(self.started)])
        copy.start()
        self.started[name] = copy

    def wait(self, name):
        self.started[name].wait()


def bits_of(values):
    high = values.astype(jnp.bfloat16).astype(jnp.float32)
    middle = (values - high).astype(jnp.bfloat16).astype(jnp.float32)
    return high, middle, values - high - middle


def prepare_kernel(
    rows_any,
    count_any,
    tiles_any,
    embeds_any,
    out_any,
    pick_any,
    side_any,
    rows_ref,
    count_ref,
    tiles_ref,
    embeds_ref,
    out_ref,
    pick_ref,
    side_ref,
    semaphores,
):
    copies = Copies(semaphores)
    copies.start("rows", rows_any, rows_ref)
    copies.start("count", count_any, count_ref)
    copies.start("embeds", embeds_any, embeds_ref)
    copies.start("tiles", tiles_any, tiles_ref)
    copies.wait("rows")
    copies.wait("count")
    slots, peers = rows_ref.shape
    nodes, width = embeds_ref.shape
    sent = slots * peers
    blocks, tiles = tiles_ref.shape[:2]
    spread = jnp.concatenate([rows_ref[...].astype(jnp.float32)] * peers, axis=0)
    row = lax.broadcasted_iota(jnp.int32, (sent, peers), 0)
    chosen = lax.div(row, slots) == lax.broadcasted_iota(jnp.int32, (sent, peers), 1)
    index = jnp.sum(jnp.where(chosen, spread, 0.0), axis=1, keepdims=True).astype(jnp.int32)
    counts = jnp.broadcast_to(count_ref[...].astype(jnp.float32), (sent, peers))
    count = jnp.sum(jnp.where(chosen, counts, 0.0), axis=1, keepdims=True).astype(jnp.int32)
    slot = lax.rem(lax.broadcasted_iota(jnp.int32, (sent, nodes), 0), slots)
    node = lax.broadcasted_iota(jnp.int32, (sent, nodes), 1)
    pick = jnp.where((node == index) & (slot < count), 1.0, 0.0).astype(jnp.bfloat16)
    pick_ref[...] = pick
    copies.wait("embeds")
    copies.start("pick", pick_ref, pick_any)
    out_ref[:, :width] = dot(pick, embeds_ref[...]).astype(jnp.bfloat16)
    copies.wait("tiles")
    copies.start("wide", out_ref.at[:, pl.ds(0, width)], out_any.at[:, pl.ds(0, width)])
    size = tiles_ref.shape[2]
    lane = lax.broadcasted_iota(jnp.int32, (size, LANES), 1)
    parts = []
    for block in range(blocks):
        total = tiles_ref[block, 0].astype(jnp.float32)
        for tile in range(1, tiles):
            total = total + tiles_ref[block, tile].astype(jnp.float32)
        rowsum = jnp.sum(total, axis=1, keepdims=True)
        scaling = lax.rsqrt(1.0 + rowsum)
        side_ref[block * size : (block + 1) * size, :] = jnp.where(lane == 0, rowsum, scaling)
        high, middle, low = bits_of(scaling)
        part = jnp.where(lane == 0, high, jnp.where(lane == 1, middle, jnp.where(lane == 2, low, 0.0)))
        parts.append(part.astype(jnp.bfloat16))
    out_ref[:, width:] = dot(pick, jnp.concatenate(parts, axis=0)).astype(jnp.bfloat16)
    copies.start("side", side_ref, side_any)
    copies.start("narrow", out_ref.at[:, pl.ds(width, LANES)], out_any.at[:, pl.ds(width, LANES)])
    for name in ("pick", "wide", "side", "narrow"):
        copies.wait(name)


def prepare(rows, count, tile_weight, embeds):
    sent = rows.shape[0] * rows.shape[1]
    nodes, width = embeds.shape
    shapes = (
        jax.ShapeDtypeStruct((sent, width + LANES), jnp.bfloat16),
        jax.ShapeDtypeStruct((sent, nodes), jnp.bfloat16),
        jax.ShapeDtypeStruct((nodes, LANES), jnp.float32),
    )
    return pl.pallas_call(
        prepare_kernel,
        in_specs=[HBM] * 4,
        out_specs=(HBM,) * 3,
        out_shape=shapes,
        scratch_shapes=[
            pltpu.VMEM(rows.shape, jnp.int32),
            pltpu.VMEM(count.shape, jnp.int32),
            pltpu.VMEM(tile_weight.shape, jnp.bfloat16),
            pltpu.VMEM(embeds.shape, jnp.bfloat16),
        ]
        + [pltpu.VMEM(shape.shape, shape.dtype) for shape in shapes]
        + [pltpu.SemaphoreType.DMA((8,))],
        compiler_params=params(),
        name="prepare",
    )(rows, count, tile_weight, embeds)


def split_hidden(hidden, rep, mine_ref, other_ref, start):
    for pair in range(hidden.shape[1] // (2 * LANES)):
        low = hidden[:, 2 * pair * LANES : (2 * pair + 1) * LANES]
        high = hidden[:, (2 * pair + 1) * LANES : (2 * pair + 2) * LANES]
        place = slice(start // 2 + pair * LANES, start // 2 + (pair + 1) * LANES)
        mine_ref[:, place] = jnp.where(rep == 0, low, high)
        other_ref[:, place] = jnp.where(rep == 0, high, low)


def hidden_chunks(x, win_ref, wout_ref, waiting, arrive, take, piece=256):
    chunk = waiting[0].shape[1]
    count = win_ref.shape[1] // chunk
    projected = None
    for step in range(count + 1):
        arrive(step)
        for low in range(0, chunk, piece):
            place = slice(low, low + piece)
            if step < count:
                ahead = step * chunk + low
                waiting[step % 2][:, place] = dot(x, win_ref[:, ahead : ahead + piece])
            if step > 0:
                start = (step - 1) * chunk + low
                values = waiting[(step - 1) % 2][:, place]
                half, square = gelu_half(values)
                hidden = (values * half).astype(jnp.bfloat16)
                take(start, hidden, values, half, square)
                part = dot(hidden, wout_ref[start : start + piece])
                projected = part if projected is None else projected + part
    return projected


class Weights:
    def __init__(self, copies, win_any, wout_any, win_ref, wout_ref, chunk):
        self.copies = copies
        self.count = win_ref.shape[1] // chunk
        for step in range(self.count):
            place = pl.ds(step * chunk, chunk)
            copies.start(("in", step), win_any.at[:, place], win_ref.at[:, place])
            copies.start(("out", step), wout_any.at[place], wout_ref.at[place])

    def wait(self, step):
        if step < self.count:
            self.copies.wait(("in", step))
        if step > 0:
            self.copies.wait(("out", step - 1))


def forward_kernel(
    rep_ref,
    column_ref,
    x_any,
    win_any,
    wout_any,
    tiles_any,
    side_any,
    rows_any,
    class_any,
    proto_any,
    pre_any,
    mine_any,
    other_any,
    grad_any,
    weight_any,
    back_any,
    x_ref,
    win_ref,
    wout_ref,
    tiles_ref,
    side_ref,
    rows_ref,
    class_ref,
    proto_ref,
    pre_ref,
    mine_ref,
    other_ref,
    even_ref,
    odd_ref,
    dense_ref,
    high_ref,
    low_ref,
    grad_ref,
    back_ref,
    semaphores,
):
    copies = Copies(semaphores)
    chunk = even_ref.shape[1]
    copies.start("x", x_any, x_ref)
    copies.start("tiles", tiles_any, tiles_ref)
    weights = Weights(copies, win_any, wout_any, win_ref, wout_ref, chunk)
    later = {
        "side": (side_any, side_ref),
        "rows": (rows_any, rows_ref),
        "class": (class_any, class_ref),
        "proto": (proto_any, proto_ref),
    }
    for name, (source, target) in later.items():
        copies.start(name, source, target)
    nodes = x_ref.shape[0]
    copies.wait("x")

    def give(step):
        whole_place = pl.ds(step * chunk, chunk)
        half_place = pl.ds(step * chunk // 2, chunk // 2)
        copies.start(("pre", step), pre_ref.at[:, whole_place], pre_any.at[:, whole_place])
        copies.start(("mine", step), mine_ref.at[:, half_place], mine_any.at[:, half_place])
        copies.start(("other", step), other_ref.at[:, half_place], other_any.at[:, half_place])

    def arrive(step):
        weights.wait(step)
        if step > 1:
            give(step - 2)
        if step == 0:
            copies.wait("tiles")
            dense_graph(column_ref, tiles_ref, dense_ref, high_ref, low_ref)
        if step == 1:
            extra = pl.ds(nodes, high_ref.shape[1] - nodes)
            copies.start("high", high_ref.at[:, extra], weight_any.at[0])
            copies.start("low", low_ref.at[:, extra], weight_any.at[1])

    def take(start, hidden, values, half, square):
        kept = gelu_slope(values, half, square) if start < SLOPED else values
        pre_ref[:, start : start + hidden.shape[1]] = kept.astype(jnp.bfloat16)
        split_hidden(hidden, rep_ref[0], mine_ref, other_ref, start)

    projected = hidden_chunks(x_ref[...], win_ref, wout_ref, (even_ref, odd_ref), arrive, take)
    give(weights.count - 1)
    for name in later:
        copies.wait(name)
    width = projected.shape[1]
    rowsum = side_ref[:, 0:1]
    scaling = side_ref[:, 1:2]
    unit = (projected * scaling).astype(jnp.bfloat16)
    unit_float = unit.astype(jnp.float32)
    beside = jnp.concatenate([unit, jnp.ones((nodes, LANES), jnp.bfloat16)], axis=1)
    high, low = high_ref[...], low_ref[...]
    turned = dot(high, beside, 0, 0) + dot(low, beside, 0, 0)
    back_ref[...] = turned[nodes:]
    copies.start("back", back_ref, back_any)
    neighbour = dot(high[:, :nodes], unit) + dot(low[:, :nodes], unit)
    own = turned[:nodes, width : width + 1] * unit_float - turned[:nodes, :width]
    marked = rows_ref.shape[1]
    node = lax.broadcasted_iota(jnp.int32, (nodes, marked), 0)
    label = jnp.where(node == rows_ref[...], 1.0, 0.0)
    name = lax.broadcasted_iota(jnp.int32, (proto_ref.shape[0], marked), 0)
    named = jnp.where(name == class_ref[...], 1.0, 0.0).astype(jnp.bfloat16)
    target = dot(named, proto_ref[...], 0, 0).astype(jnp.bfloat16)
    pull = jnp.sum(label, axis=1, keepdims=True) * projected - dot(label.astype(jnp.bfloat16), target)
    grad_ref[...] = (rowsum * unit_float - neighbour + own) * scaling + pull
    copies.start("grad", grad_ref, grad_any)
    for step in range(weights.count):
        for name in ("pre", "mine", "other"):
            copies.wait((name, step))
    for name in ("high", "low", "back", "grad"):
        copies.wait(name)


def dense_graph(column_ref, tiles_ref, dense_ref, high_ref, low_ref):
    blocks, tiles, size, _ = tiles_ref.shape
    dense_ref[...] = jnp.zeros_like(dense_ref)
    for block in range(blocks):
        for tile in range(tiles):
            column = column_ref[block, tile]
            place = slice(block * size, (block + 1) * size)
            dense_ref[column, place, :] += tiles_ref[block, tile].astype(jnp.float32)
    for column in range(dense_ref.shape[0]):
        dense = dense_ref[column]
        high = dense.astype(jnp.bfloat16)
        place = slice(column * size, (column + 1) * size)
        high_ref[:, place] = high
        low_ref[:, place] = (dense - high.astype(jnp.float32)).astype(jnp.bfloat16)


def forward(
    rep,
    tile_column,
    embeds,
    weight_in,
    weight_out,
    tile_weight,
    side,
    label_rows,
    label_class,
    prototypes,
    received,
    chunk=1024,
):
    nodes, depth = embeds.shape
    hidden = weight_in.shape[1]
    width = weight_out.shape[1]
    size = tile_weight.shape[2]
    low = jnp.bfloat16
    arrays = (embeds, weight_in, weight_out, tile_weight, side, label_rows, label_class, prototypes)
    return pl.pallas_call(
        forward_kernel,
        in_specs=[SMEM] * 2 + [HBM] * 8,
        out_specs=(HBM,) * 6,
        out_shape=(
            jax.ShapeDtypeStruct((nodes, hidden), low),
            jax.ShapeDtypeStruct((nodes, hidden // 2), low),
            jax.ShapeDtypeStruct((nodes, hidden // 2), low),
            jax.ShapeDtypeStruct((nodes, width), jnp.float32),
            jax.ShapeDtypeStruct((2, nodes, received), low),
            jax.ShapeDtypeStruct((received, width + LANES), jnp.float32),
        ),
        scratch_shapes=[pltpu.VMEM(array.shape, array.dtype) for array in arrays]
        + [
            pltpu.VMEM((nodes, hidden), low),
            pltpu.VMEM((nodes, hidden // 2), low),
            pltpu.VMEM((nodes, hidden // 2), low),
            pltpu.VMEM((nodes, chunk), jnp.float32),
            pltpu.VMEM((nodes, chunk), jnp.float32),
            pltpu.VMEM(((nodes + received) // size, nodes, size), jnp.float32),
            pltpu.VMEM((nodes, nodes + received), low),
            pltpu.VMEM((nodes, nodes + received), low),
            pltpu.VMEM((nodes, width), jnp.float32),
            pltpu.VMEM((received, width + LANES), jnp.float32),
            pltpu.SemaphoreType.DMA((10 + 5 * (hidden // chunk),)),
        ],
        compiler_params=params(),
        name="forward",
    )(rep, tile_column, *arrays)


def received_kernel(
    rep_ref,
    x_any,
    win_any,
    wout_any,
    side_any,
    grad_any,
    weight_any,
    back_any,
    mine_any,
    other_any,
    full_any,
    turned_any,
    return_any,
    x_ref,
    win_ref,
    wout_ref,
    side_ref,
    grad_ref,
    weight_ref,
    back_ref,
    mine_ref,
    other_ref,
    full_ref,
    turned_ref,
    return_ref,
    even_ref,
    odd_ref,
    semaphores,
):
    depth = win_ref.shape[0]
    nodes, width = grad_ref.shape
    chunk = even_ref.shape[1]
    copies = Copies(semaphores)
    copies.start("x", x_any, x_ref)
    weights = Weights(copies, win_any, wout_any, win_ref, wout_ref, chunk)
    later = {
        "side": (side_any, side_ref),
        "grad": (grad_any, grad_ref),
        "weight": (weight_any, weight_ref),
        "back": (back_any, back_ref),
    }
    for name, (source, target) in later.items():
        copies.start(name, source, target)
    copies.wait("x")

    def give(step):
        place = pl.ds(step * chunk // 2, chunk // 2)
        copies.start(("mine", step), mine_ref.at[:, place], mine_any.at[:, place])
        copies.start(("other", step), other_ref.at[:, place], other_any.at[:, place])

    def arrive(step):
        weights.wait(step)
        if step > 1:
            give(step - 2)

    def take(start, hidden, values, half, square):
        split_hidden(hidden, rep_ref[0], mine_ref, other_ref, start)

    projected = hidden_chunks(x_ref[:, :depth], win_ref, wout_ref, (even_ref, odd_ref), arrive, take)
    give(weights.count - 1)
    for name in later:
        copies.wait(name)
    scaling = jnp.sum(x_ref[:, depth:].astype(jnp.float32), axis=1, keepdims=True)
    unit = (projected * scaling).astype(jnp.bfloat16)
    neighbour = dot(weight_ref[0], unit) + dot(weight_ref[1], unit)
    full = grad_ref[...] - neighbour * side_ref[:, 1:2]
    full_ref[...] = full
    back = (back_ref[:, width : width + 1] * unit.astype(jnp.float32) - back_ref[:, :width]).astype(jnp.bfloat16)
    return_ref[...] = back
    copies.start("full", full_ref, full_any)
    copies.start("return", return_ref, return_any)
    turned_ref[:, :nodes] = full.T.astype(jnp.bfloat16)
    turned_ref[:, nodes:] = (back.astype(jnp.float32) * scaling).T.astype(jnp.bfloat16)
    copies.start("turned", turned_ref, turned_any)
    for step in range(weights.count):
        copies.wait(("mine", step))
        copies.wait(("other", step))
    for name in ("full", "return", "turned"):
        copies.wait(name)


def received_part(rep, arrived, weight_in, weight_out, side, grad, weight, back, chunk=512):
    rows = arrived.shape[0]
    hidden = weight_in.shape[1]
    nodes, width = grad.shape
    low = jnp.bfloat16
    arrays = (arrived, weight_in, weight_out, side, grad, weight, back)
    return pl.pallas_call(
        received_kernel,
        in_specs=[SMEM] + [HBM] * 7,
        out_specs=(HBM,) * 5,
        out_shape=(
            jax.ShapeDtypeStruct((rows, hidden // 2), low),
            jax.ShapeDtypeStruct((rows, hidden // 2), low),
            jax.ShapeDtypeStruct((nodes, width), jnp.float32),
            jax.ShapeDtypeStruct((width, nodes + rows), low),
            jax.ShapeDtypeStruct((rows, width), low),
        ),
        scratch_shapes=[pltpu.VMEM(array.shape, array.dtype) for array in arrays]
        + [
            pltpu.VMEM((rows, hidden // 2), low),
            pltpu.VMEM((rows, hidden // 2), low),
            pltpu.VMEM((nodes, width), jnp.float32),
            pltpu.VMEM((width, nodes + rows), low),
            pltpu.VMEM((rows, width), low),
            pltpu.VMEM((rows, chunk), jnp.float32),
            pltpu.VMEM((rows, chunk), jnp.float32),
            pltpu.SemaphoreType.DMA((8 + 4 * (hidden // chunk),)),
        ],
        compiler_params=params(),
        name="received_part",
    )(rep, *arrays)


def chip_total(chunk, copies, arrays, turned_ref, hidden_ref, total_ref, arrive):
    steps = range(0, hidden_ref.shape[1], chunk)
    base = 0
    for index in range(2):
        length = arrays[index].shape[1]
        copies.start(index, arrays[index], turned_ref.at[:, pl.ds(base, length)])
        base += length
    for start in steps:
        place = pl.ds(start, chunk)
        base = 0
        for index in range(2, 6):
            length = arrays[index].shape[0]
            copies.start((index, start), arrays[index].at[:, place], hidden_ref.at[pl.ds(base, length), place])
            base += length
    copies.wait(0)
    copies.wait(1)
    for start in steps:
        for index in range(2, 6):
            copies.wait((index, start))
        arrive(start // LANES)
        total = dot(turned_ref[...], hidden_ref[:, start : start + chunk])
        for step in range(chunk // LANES):
            total_ref[start // LANES + step] = total[:, step * LANES : (step + 1) * LANES]


def total_kernel(chunk, *refs):
    turned_ref, hidden_ref, semaphores = refs[7:]
    chip_total(chunk, Copies(semaphores), refs[:6], turned_ref, hidden_ref, refs[6], lambda ready: None)


def product_kernel(streams, chunk, place_ref, *refs):
    count = 2 * len(streams)
    outputs, scratch = refs[6 : 6 + count], refs[6 + count : 6 + 2 * count]
    turned_ref, hidden_ref, semaphores, total_ref = refs[6 + 2 * count :]
    copies = Copies(semaphores)
    done = [0] * len(streams)

    def arrive(ready):
        given = []
        for stream, (order, low, high) in enumerate(streams):
            bit = order[0]
            first = done[stream]
            spot = first
            while spot < scratch[2 * stream].shape[0]:
                base = ((spot >> bit) << (bit + 1)) | (spot & ((1 << bit) - 1))
                if base + (1 << bit) >= ready:
                    break
                sent, kept = places(spot, bit, place_ref[0])
                scratch[2 * stream][spot] = total_ref[sent, low:high].astype(jnp.bfloat16)
                scratch[2 * stream + 1][spot] = total_ref[kept, low:high]
                spot += 1
            done[stream] = spot
            if spot > first:
                given += [(2 * stream, first, spot), (2 * stream + 1, first, spot)]
        for index, first, last in given:
            place = pl.ds(first, last - first)
            copies.start(("give", index, first), scratch[index].at[place], outputs[index].at[place])

    chip_total(chunk, copies, refs[:6], turned_ref, hidden_ref, total_ref, arrive)
    arrive(total_ref.shape[0])
    for name in list(copies.started):
        if isinstance(name, tuple) and name[0] == "give":
            copies.wait(name)


def places(spot, weight, place, bit=None):
    mine = lax.rem(lax.div(place, 1 << (weight if bit is None else bit)), 2)
    base = ((spot >> weight) << (weight + 1)) | (spot & ((1 << weight) - 1))
    return base + (1 - mine) * (1 << weight), base + mine * (1 << weight)


def fold_kernel(digits, merge, place_ref, *refs):
    count = len(digits)
    outputs = refs[2 * count :]
    base = 0
    for stream, (weight, bit) in enumerate(digits):
        kept_ref, came_ref = refs[2 * stream : 2 * stream + 2]
        target = max(stream - 1, 0) if merge else stream
        if not (merge and stream == 1):
            base = 0
        sent_ref, next_ref = outputs[2 * target : 2 * target + 2]
        rows = slice(base, base + kept_ref.shape[1])
        base = rows.stop
        for spot in range(sent_ref.shape[0]):
            sent, kept = places(spot, weight, place_ref[0], bit)
            sent_ref[spot, rows] = (kept_ref[sent] + came_ref[sent].astype(jnp.float32)).astype(jnp.bfloat16)
            next_ref[spot, rows] = kept_ref[kept] + came_ref[kept].astype(jnp.float32)


def fold_halves(place, digits, merge, kept, came):
    heights = [array.shape[1] for array in kept]
    if merge:
        heights = [heights[0] + heights[1]] + heights[2:]
    blocks, _, depth = kept[0].shape
    shapes = []
    for height in heights:
        shapes.append(jax.ShapeDtypeStruct((blocks // 2, height, depth), jnp.bfloat16))
        shapes.append(jax.ShapeDtypeStruct((blocks // 2, height, depth), jnp.float32))
    operands = [array for pair in zip(kept, came) for array in pair]
    flat = pl.pallas_call(
        functools.partial(fold_kernel, digits, merge),
        in_specs=[SMEM] + [VMEM] * len(operands),
        out_shape=tuple(shapes),
        compiler_params=params(16),
        name="fold_halves",
    )(place, *operands)
    return [tuple(flat[2 * stream : 2 * stream + 2]) for stream in range(len(heights))]


def finish_kernel(factor, *refs):
    base = 0
    for stream in range(len(refs) // 2):
        kept_ref, came_ref = refs[2 * stream : 2 * stream + 2]
        rows = kept_ref.shape[1]
        total = kept_ref[0] + came_ref[0].astype(jnp.float32)
        refs[-1][:, base : base + rows] = total.T * factor
        base += rows


def finish(factor, kept, came):
    width = sum(array.shape[1] for array in kept)
    return pl.pallas_call(
        functools.partial(finish_kernel, factor),
        out_shape=jax.ShapeDtypeStruct((kept[0].shape[2], width), jnp.float32),
        compiler_params=params(16),
        name="finish",
    )(*[array for pair in zip(kept, came) for array in pair])


def product(place, streams, operands, chunk=512):
    width = operands[0].shape[0]
    hidden = operands[2].shape[1]
    blocks = hidden // LANES
    total = (blocks, width, LANES)
    rows = 2 * operands[0].shape[1]
    scratch = [
        pltpu.VMEM((width, rows), jnp.bfloat16),
        pltpu.VMEM((rows, hidden), jnp.bfloat16),
        pltpu.SemaphoreType.DMA((2 + 10 * (hidden // chunk),)),
    ]
    if not streams:
        return pl.pallas_call(
            functools.partial(total_kernel, chunk),
            in_specs=[HBM] * 6,
            out_shape=jax.ShapeDtypeStruct(total, jnp.float32),
            scratch_shapes=scratch,
            compiler_params=params(),
            name="chip_total",
        )(*operands)
    shapes = []
    for _, low, high in streams:
        shapes.append(jax.ShapeDtypeStruct((blocks // 2, high - low, LANES), jnp.bfloat16))
        shapes.append(jax.ShapeDtypeStruct((blocks // 2, high - low, LANES), jnp.float32))
    return pl.pallas_call(
        functools.partial(product_kernel, streams, chunk),
        in_specs=[SMEM] + [HBM] * 6,
        out_specs=(HBM,) * len(shapes),
        out_shape=tuple(shapes),
        scratch_shapes=[pltpu.VMEM(shape.shape, shape.dtype) for shape in shapes]
        + scratch
        + [pltpu.VMEM(total, jnp.float32)],
        compiler_params=params(),
        name="product",
    )(place, *operands)


def slope_kernel(chunk, *refs):
    full_any, pick_any, back_any, side_any, pre_any, wout_any, out_any = refs[:7]
    full_ref, pick_ref, back_ref, side_ref, pre_ref, wout_ref, grad_ref, semaphores = refs[7:]
    copies = Copies(semaphores)
    first = ((full_any, full_ref), (pick_any, pick_ref), (back_any, back_ref), (side_any, side_ref))
    steps = range(0, pre_ref.shape[1], chunk)
    for index, (source, target) in enumerate(first):
        copies.start(index, source, target)
    for start in steps:
        place = pl.ds(start, chunk)
        copies.start(("out", start), wout_any.at[place], wout_ref.at[place])
        copies.start(("pre", start), pre_any.at[:, place], pre_ref.at[:, place])
    for index in range(len(first)):
        copies.wait(index)
    back = dot(pick_ref[...], back_ref[...], 0, 0)
    node = (full_ref[...] + back * side_ref[:, 1:2]).astype(jnp.bfloat16)
    piece = chunk // 2
    for start in steps:
        copies.wait(("out", start))
        copies.wait(("pre", start))
        if start > 0:
            place = pl.ds(start - chunk, chunk)
            copies.start(("grad", start - chunk), grad_ref.at[:, place], out_any.at[:, place])
        for low in range(start, start + chunk, piece):
            place = slice(low, low + piece)
            grad_hidden = dot(node, wout_ref[place], 1, 1)
            slope = pre_ref[:, place].astype(jnp.float32)
            if low >= SLOPED:
                slope = gelu_slope(slope, *gelu_half(slope))
            grad_ref[:, place] = (grad_hidden * slope).astype(jnp.bfloat16)
    place = pl.ds(steps[-1], chunk)
    copies.start(("grad", steps[-1]), grad_ref.at[:, place], out_any.at[:, place])
    for start in steps:
        copies.wait(("grad", start))


def slope_part(full, pick, back, side, pre, weight_out, chunk=1024):
    arrays = (full, pick, back, side, pre, weight_out)
    return pl.pallas_call(
        functools.partial(slope_kernel, chunk),
        in_specs=[HBM] * 6,
        out_specs=HBM,
        out_shape=jax.ShapeDtypeStruct(pre.shape, jnp.bfloat16),
        scratch_shapes=[pltpu.VMEM(array.shape, array.dtype) for array in arrays]
        + [
            pltpu.VMEM(pre.shape, jnp.bfloat16),
            pltpu.SemaphoreType.DMA((4 + 3 * (pre.shape[1] // chunk),)),
        ],
        cost_estimate=pl.CostEstimate(flops=2 * pre.size * full.shape[1], bytes_accessed=16 * MIB, transcendentals=0),
        compiler_params=params(58),
        name="slope_part",
    )(*arrays)


def embed_kernel(chunk, first, grad_any, win_any, *refs):
    out_any, grad_ref, win_ref, out_ref, total_ref, semaphores = refs[-6:]
    copies = Copies(semaphores)
    steps = range(0, grad_ref.shape[1], chunk)
    columns = pl.ds(first, win_ref.shape[0])
    for start in steps:
        place = pl.ds(start, chunk)
        copies.start(("grad", start), grad_any.at[:, place], grad_ref.at[:, place])
        copies.start(("in", start), win_any.at[columns, place], win_ref.at[:, place])
    for start in steps:
        copies.wait(("grad", start))
        copies.wait(("in", start))
        place = slice(start, start + chunk)
        part = dot(grad_ref[:, place], win_ref[:, place], 1, 1)
        if start == 0:
            total_ref[...] = part
        elif start + chunk < grad_ref.shape[1]:
            total_ref[...] += part
        else:
            out_ref[...] = (total_ref[...] + part).astype(jnp.bfloat16)
    copies.start("give", out_ref, out_any.at[:, columns])
    copies.wait("give")


def embed_part(first, length, grad, weight_in, other=None, chunk=1024):
    nodes, hidden = grad.shape
    depth = weight_in.shape[0]
    operands = (grad, weight_in) if other is None else (grad, weight_in, other)
    return pl.pallas_call(
        functools.partial(embed_kernel, chunk, first),
        in_specs=[HBM] * len(operands),
        out_specs=HBM,
        out_shape=jax.ShapeDtypeStruct((nodes, depth), jnp.bfloat16),
        input_output_aliases={} if other is None else {2: 0},
        scratch_shapes=[
            pltpu.VMEM(grad.shape, jnp.bfloat16),
            pltpu.VMEM((length, hidden), jnp.bfloat16),
            pltpu.VMEM((nodes, length), jnp.bfloat16),
            pltpu.VMEM((nodes, length), jnp.float32),
            pltpu.SemaphoreType.DMA((1 + 2 * (hidden // chunk),)),
        ],
        cost_estimate=pl.CostEstimate(flops=2 * grad.size * length, bytes_accessed=9 * MIB, transcendentals=0),
        compiler_params=params(60),
        name="embed_part",
    )(*operands)


def bit_orders(count):
    bits = list(range(count.bit_length() - 1))
    first = len(bits) // 3
    second = first + max(first, (len(bits) - first) // 3)
    low, middle, high = bits[:first], bits[first:second], bits[second:]
    return (low + middle + high, middle + low + high, high + low + middle)


def streams_of(dom_count, width):
    cut = width * 11 // 32
    edges = (0, cut, 2 * cut, width)
    return tuple(zip(bit_orders(dom_count), edges[:-1], edges[1:]))


def halves(part, spot, mine):
    sent = lax.dynamic_index_in_dim(part, 1 - mine, spot, keepdims=False).astype(jnp.bfloat16)
    return sent, lax.dynamic_index_in_dim(part, mine, spot, keepdims=False)


def exchange(sent, bit):
    dom_count = lax.axis_size("dom")
    return lax.ppermute(sent, "dom", [(device, device ^ (1 << bit)) for device in range(dom_count)])


def body(
    embeds,
    weight_in,
    weight_out,
    prototypes,
    tile_column,
    tile_weight,
    send_rows,
    send_count,
    label_rows,
    label_class,
):
    nodes, embed_width = embeds.shape
    dom_count = lax.axis_size("dom")
    rep_count = lax.axis_size("rep")
    peers = dom_count * rep_count
    slots = send_rows.shape[2]
    hidden_width, width = weight_out.shape
    depth = hidden_width // peers
    place = lax.axis_index("dom")
    rep = lax.axis_index("rep")
    swap = [(0, 1), (1, 0)]
    fold = LANES // depth
    if fold > 1:
        order = (dom_count // fold, fold, rep_count, depth)
        weight_in = weight_in.reshape((-1,) + order).swapaxes(2, 3).reshape(-1, hidden_width)
        weight_out = weight_out.reshape(order + (-1,)).swapaxes(1, 2).reshape(hidden_width, -1)

    outgoing, pick, side = prepare(send_rows[0].T, send_count, tile_weight, embeds)
    arrived = lax.all_to_all(
        outgoing.reshape(peers, slots, -1), both, split_axis=0, concat_axis=0, tiled=True
    ).reshape(peers * slots, -1)
    pre_act, own, sent_own, grad, weight, back = forward(
        rep[None],
        tile_column,
        embeds,
        weight_in,
        weight_out,
        tile_weight,
        side,
        label_rows[None, :],
        label_class[None, :],
        prototypes,
        peers * slots,
    )
    other_own = lax.ppermute(sent_own, "rep", swap)
    came, sent_came, full, turned, returned = received_part(
        rep[None], arrived, weight_in, weight_out, side, grad, weight, back
    )
    other_turned = lax.ppermute(turned, "rep", swap)
    other_came = lax.ppermute(sent_came, "rep", swap)
    given = lax.all_to_all(
        returned.reshape(peers, slots, width), both, split_axis=0, concat_axis=0, tiled=True
    ).reshape(peers * slots, width)
    operands = (turned, other_turned, own, came, other_own, other_came)

    streams = streams_of(dom_count, width)
    bit_count = dom_count.bit_length() - 1
    parts = []
    if fold > 1:
        total = product(place[None], (), operands)
        total = total.reshape(-1, width, fold, depth).swapaxes(1, 2).reshape((2,) * bit_count + (width, depth))
        for order, low, high in streams:
            spot = bit_count - 1 - order[0]
            pair = halves(total[..., low:high, :], spot, (place >> order[0]) & 1)
            parts.append(tuple(array.reshape(-1, high - low, depth) for array in pair))
    else:
        flat = product(place[None], streams, operands)
        parts = [tuple(flat[2 * stream : 2 * stream + 2]) for stream in range(len(streams))]
    parts, full = lax.optimization_barrier((parts, full))
    grad_pre = slope_part(full, pick, given, side, pre_act, weight_out)
    left = [[bit for bit in range(bit_count) if bit != order[0]] for order, _, _ in streams]
    orders = [order for order, _, _ in streams]
    shared = next(step for step in range(bit_count) if orders[0][step:] == orders[1][step:])
    cuts = (0, embed_width // 2, embed_width)
    embed_grad = None
    for step in range(bit_count):
        came = [exchange(sent, order[step]) for (sent, _), order in zip(parts, orders)]
        if step == 0:
            came, grad_pre = lax.optimization_barrier((came, grad_pre))
        elif step < len(cuts):
            came, embed_grad = lax.optimization_barrier((came, embed_grad))
        else:
            came = lax.optimization_barrier(came)
        kept = [array for _, array in parts]
        if step + 1 == bit_count:
            break
        digits = [(bits.index(order[step + 1]), order[step + 1]) for bits, order in zip(left, orders)]
        for bits, order in zip(left, orders):
            bits.remove(order[step + 1])
        parts = fold_halves(place[None], digits, step + 1 == shared, kept, came)
        if step + 1 == shared:
            left, orders = left[1:], orders[1:]
        if step + 1 < len(cuts):
            parts, grad_pre = lax.optimization_barrier((parts, grad_pre))
            embed_grad = embed_part(cuts[step], cuts[step + 1] - cuts[step], grad_pre, weight_in, embed_grad)
        else:
            parts = lax.optimization_barrier(parts)
    summed = finish(1.0 / math.sqrt(nodes * peers), kept, came)
    return (embed_grad, summed)


def solution(mesh):
    placed = (
        P(both, None),
        P(),
        P(),
        P(),
        P(both, None),
        P(both, None, None, None),
        P(both, None, None),
        P(both, None),
        P(both),
        P(both),
    )
    return jax.shard_map(
        body,
        mesh=mesh,
        in_specs=placed,
        out_specs=(P(both, None), P(both, None)),
        check_vma=False,
    )
```

```python
import functools
import math

import jax
import jax.numpy as jnp
from jax import lax
from jax.experimental import pallas as pl
from jax.experimental.pallas import tpu as pltpu
from jax.sharding import PartitionSpec as P

gelu_inner = 0.7978845608028654
gelu_cubic = 0.044715
LANES = 128
SLOPED = 2048
MIB = 1024 * 1024
both = ("dom", "rep")


def gelu_half(values):
    square = values * values
    return 0.5 + 0.5 * jnp.tanh(values * (gelu_inner + gelu_inner * gelu_cubic * square)), square


def gelu_slope(values, half, square):
    return half + values * half * (2.0 - 2.0 * half) * (gelu_inner + 3.0 * gelu_inner * gelu_cubic * square)


def dot(left, right, left_dim=1, right_dim=0):
    return lax.dot_general(
        left, right, (((left_dim,), (right_dim,)), ((), ())), preferred_element_type=jnp.float32
    )


def params(mib=64):
    return pltpu.CompilerParams(vmem_limit_bytes=mib * MIB)


VMEM = pl.BlockSpec(memory_space=pltpu.VMEM)
SMEM = pl.BlockSpec(memory_space=pltpu.SMEM)
HBM = pl.BlockSpec(memory_space=pltpu.HBM)


class Copies:
    def __init__(self, semaphores):
        self.semaphores = semaphores
        self.started = {}

    def start(self, name, source, target):
        copy = pltpu.make_async_copy(source, target, self.semaphores.at[len(self.started)])
        copy.start()
        self.started[name] = copy

    def wait(self, name):
        self.started[name].wait()


def bits_of(values):
    high = values.astype(jnp.bfloat16).astype(jnp.float32)
    middle = (values - high).astype(jnp.bfloat16).astype(jnp.float32)
    return high, middle, values - high - middle


def prepare_kernel(
    rows_any,
    count_any,
    tiles_any,
    embeds_any,
    out_any,
    pick_any,
    side_any,
    rows_ref,
    count_ref,
    tiles_ref,
    embeds_ref,
    out_ref,
    pick_ref,
    side_ref,
    semaphores,
):
    copies = Copies(semaphores)
    copies.start("rows", rows_any, rows_ref)
    copies.start("count", count_any, count_ref)
    copies.start("embeds", embeds_any, embeds_ref)
    copies.start("tiles", tiles_any, tiles_ref)
    copies.wait("rows")
    copies.wait("count")
    slots, peers = rows_ref.shape
    nodes, width = embeds_ref.shape
    sent = slots * peers
    blocks, tiles = tiles_ref.shape[:2]
    spread = jnp.concatenate([rows_ref[...].astype(jnp.float32)] * peers, axis=0)
    row = lax.broadcasted_iota(jnp.int32, (sent, peers), 0)
    chosen = lax.div(row, slots) == lax.broadcasted_iota(jnp.int32, (sent, peers), 1)
    index = jnp.sum(jnp.where(chosen, spread, 0.0), axis=1, keepdims=True).astype(jnp.int32)
    counts = jnp.broadcast_to(count_ref[...].astype(jnp.float32), (sent, peers))
    count = jnp.sum(jnp.where(chosen, counts, 0.0), axis=1, keepdims=True).astype(jnp.int32)
    slot = lax.rem(lax.broadcasted_iota(jnp.int32, (sent, nodes), 0), slots)
    node = lax.broadcasted_iota(jnp.int32, (sent, nodes), 1)
    pick = jnp.where((node == index) & (slot < count), 1.0, 0.0).astype(jnp.bfloat16)
    pick_ref[...] = pick
    copies.wait("embeds")
    copies.start("pick", pick_ref, pick_any)
    out_ref[:, :width] = dot(pick, embeds_ref[...]).astype(jnp.bfloat16)
    copies.wait("tiles")
    copies.start("wide", out_ref.at[:, pl.ds(0, width)], out_any.at[:, pl.ds(0, width)])
    size = tiles_ref.shape[2]
    lane = lax.broadcasted_iota(jnp.int32, (size, LANES), 1)
    parts = []
    for block in range(blocks):
        total = tiles_ref[block, 0].astype(jnp.float32)
        for tile in range(1, tiles):
            total = total + tiles_ref[block, tile].astype(jnp.float32)
        rowsum = jnp.sum(total, axis=1, keepdims=True)
        scaling = lax.rsqrt(1.0 + rowsum)
        side_ref[block * size : (block + 1) * size, :] = jnp.where(lane == 0, rowsum, scaling)
        high, middle, low = bits_of(scaling)
        part = jnp.where(lane == 0, high, jnp.where(lane == 1, middle, jnp.where(lane == 2, low, 0.0)))
        parts.append(part.astype(jnp.bfloat16))
    out_ref[:, width:] = dot(pick, jnp.concatenate(parts, axis=0)).astype(jnp.bfloat16)
    copies.start("side", side_ref, side_any)
    copies.start("narrow", out_ref.at[:, pl.ds(width, LANES)], out_any.at[:, pl.ds(width, LANES)])
    for name in ("pick", "wide", "side", "narrow"):
        copies.wait(name)


def prepare(rows, count, tile_weight, embeds):
    sent = rows.shape[0] * rows.shape[1]
    nodes, width = embeds.shape
    shapes = (
        jax.ShapeDtypeStruct((sent, width + LANES), jnp.bfloat16),
        jax.ShapeDtypeStruct((sent, nodes), jnp.bfloat16),
        jax.ShapeDtypeStruct((nodes, LANES), jnp.float32),
    )
    return pl.pallas_call(
        prepare_kernel,
        in_specs=[HBM] * 4,
        out_specs=(HBM,) * 3,
        out_shape=shapes,
        scratch_shapes=[
            pltpu.VMEM(rows.shape, jnp.int32),
            pltpu.VMEM(count.shape, jnp.int32),
            pltpu.VMEM(tile_weight.shape, jnp.bfloat16),
            pltpu.VMEM(embeds.shape, jnp.bfloat16),
        ]
        + [pltpu.VMEM(shape.shape, shape.dtype) for shape in shapes]
        + [pltpu.SemaphoreType.DMA((8,))],
        compiler_params=params(),
        name="prepare",
    )(rows, count, tile_weight, embeds)


def split_hidden(hidden, rep, mine_ref, other_ref, start):
    for pair in range(hidden.shape[1] // (2 * LANES)):
        low = hidden[:, 2 * pair * LANES : (2 * pair + 1) * LANES]
        high = hidden[:, (2 * pair + 1) * LANES : (2 * pair + 2) * LANES]
        place = slice(start // 2 + pair * LANES, start // 2 + (pair + 1) * LANES)
        mine_ref[:, place] = jnp.where(rep == 0, low, high)
        other_ref[:, place] = jnp.where(rep == 0, high, low)


def hidden_chunks(x, win_ref, wout_ref, waiting, arrive, take, piece=256):
    chunk = waiting[0].shape[1]
    count = win_ref.shape[1] // chunk
    projected = None
    for step in range(count + 1):
        arrive(step)
        for low in range(0, chunk, piece):
            place = slice(low, low + piece)
            if step < count:
                ahead = step * chunk + low
                waiting[step % 2][:, place] = dot(x, win_ref[:, ahead : ahead + piece])
            if step > 0:
                start = (step - 1) * chunk + low
                values = waiting[(step - 1) % 2][:, place]
                half, square = gelu_half(values)
                hidden = (values * half).astype(jnp.bfloat16)
                take(start, hidden, values, half, square)
                part = dot(hidden, wout_ref[start : start + piece])
                projected = part if projected is None else projected + part
    return projected


class Weights:
    def __init__(self, copies, win_any, wout_any, win_ref, wout_ref, chunk):
        self.copies = copies
        self.count = win_ref.shape[1] // chunk
        for step in range(self.count):
            place = pl.ds(step * chunk, chunk)
            copies.start(("in", step), win_any.at[:, place], win_ref.at[:, place])
            copies.start(("out", step), wout_any.at[place], wout_ref.at[place])

    def wait(self, step):
        if step < self.count:
            self.copies.wait(("in", step))
        if step > 0:
            self.copies.wait(("out", step - 1))


def forward_kernel(
    rep_ref,
    column_ref,
    x_any,
    win_any,
    wout_any,
    tiles_any,
    side_any,
    rows_any,
    class_any,
    proto_any,
    pre_any,
    mine_any,
    other_any,
    grad_any,
    weight_any,
    back_any,
    x_ref,
    win_ref,
    wout_ref,
    tiles_ref,
    side_ref,
    rows_ref,
    class_ref,
    proto_ref,
    pre_ref,
    mine_ref,
    other_ref,
    even_ref,
    odd_ref,
    dense_ref,
    high_ref,
    low_ref,
    grad_ref,
    back_ref,
    semaphores,
):
    copies = Copies(semaphores)
    chunk = even_ref.shape[1]
    copies.start("x", x_any, x_ref)
    copies.start("tiles", tiles_any, tiles_ref)
    weights = Weights(copies, win_any, wout_any, win_ref, wout_ref, chunk)
    later = {
        "side": (side_any, side_ref),
        "rows": (rows_any, rows_ref),
        "class": (class_any, class_ref),
        "proto": (proto_any, proto_ref),
    }
    for name, (source, target) in later.items():
        copies.start(name, source, target)
    nodes = x_ref.shape[0]
    copies.wait("x")

    def give(step):
        whole_place = pl.ds(step * chunk, chunk)
        half_place = pl.ds(step * chunk // 2, chunk // 2)
        copies.start(("pre", step), pre_ref.at[:, whole_place], pre_any.at[:, whole_place])
        copies.start(("mine", step), mine_ref.at[:, half_place], mine_any.at[:, half_place])
        copies.start(("other", step), other_ref.at[:, half_place], other_any.at[:, half_place])

    def arrive(step):
        weights.wait(step)
        if step > 1:
            give(step - 2)
        if step == 0:
            copies.wait("tiles")
            dense_graph(column_ref, tiles_ref, dense_ref, high_ref, low_ref)
        if step == 1:
            extra = pl.ds(nodes, high_ref.shape[1] - nodes)
            copies.start("high", high_ref.at[:, extra], weight_any.at[0])
            copies.start("low", low_ref.at[:, extra], weight_any.at[1])

    def take(start, hidden, values, half, square):
        kept = gelu_slope(values, half, square) if start < SLOPED else values
        pre_ref[:, start : start + hidden.shape[1]] = kept.astype(jnp.bfloat16)
        split_hidden(hidden, rep_ref[0], mine_ref, other_ref, start)

    projected = hidden_chunks(x_ref[...], win_ref, wout_ref, (even_ref, odd_ref), arrive, take)
    give(weights.count - 1)
    for name in later:
        copies.wait(name)
    width = projected.shape[1]
    rowsum = side_ref[:, 0:1]
    scaling = side_ref[:, 1:2]
    unit = (projected * scaling).astype(jnp.bfloat16)
    unit_float = unit.astype(jnp.float32)
    beside = jnp.concatenate([unit, jnp.ones((nodes, LANES), jnp.bfloat16)], axis=1)
    high, low = high_ref[...], low_ref[...]
    turned = dot(high, beside, 0, 0) + dot(low, beside, 0, 0)
    back_ref[...] = turned[nodes:]
    copies.start("back", back_ref, back_any)
    neighbour = dot(high[:, :nodes], unit) + dot(low[:, :nodes], unit)
    own = turned[:nodes, width : width + 1] * unit_float - turned[:nodes, :width]
    marked = rows_ref.shape[1]
    node = lax.broadcasted_iota(jnp.int32, (nodes, marked), 0)
    label = jnp.where(node == rows_ref[...], 1.0, 0.0)
    name = lax.broadcasted_iota(jnp.int32, (proto_ref.shape[0], marked), 0)
    named = jnp.where(name == class_ref[...], 1.0, 0.0).astype(jnp.bfloat16)
    target = dot(named, proto_ref[...], 0, 0).astype(jnp.bfloat16)
    pull = jnp.sum(label, axis=1, keepdims=True) * projected - dot(label.astype(jnp.bfloat16), target)
    grad_ref[...] = (rowsum * unit_float - neighbour + own) * scaling + pull
    copies.start("grad", grad_ref, grad_any)
    for step in range(weights.count):
        for name in ("pre", "mine", "other"):
            copies.wait((name, step))
    for name in ("high", "low", "back", "grad"):
        copies.wait(name)


def dense_graph(column_ref, tiles_ref, dense_ref, high_ref, low_ref):
    blocks, tiles, size, _ = tiles_ref.shape
    dense_ref[...] = jnp.zeros_like(dense_ref)
    for block in range(blocks):
        for tile in range(tiles):
            column = column_ref[block, tile]
            place = slice(block * size, (block + 1) * size)
            dense_ref[column, place, :] += tiles_ref[block, tile].astype(jnp.float32)
    for column in range(dense_ref.shape[0]):
        dense = dense_ref[column]
        high = dense.astype(jnp.bfloat16)
        place = slice(column * size, (column + 1) * size)
        high_ref[:, place] = high
        low_ref[:, place] = (dense - high.astype(jnp.float32)).astype(jnp.bfloat16)


def forward(
    rep,
    tile_column,
    embeds,
    weight_in,
    weight_out,
    tile_weight,
    side,
    label_rows,
    label_class,
    prototypes,
    received,
    chunk=1024,
):
    nodes, depth = embeds.shape
    hidden = weight_in.shape[1]
    width = weight_out.shape[1]
    size = tile_weight.shape[2]
    low = jnp.bfloat16
    arrays = (embeds, weight_in, weight_out, tile_weight, side, label_rows, label_class, prototypes)
    return pl.pallas_call(
        forward_kernel,
        in_specs=[SMEM] * 2 + [HBM] * 8,
        out_specs=(HBM,) * 6,
        out_shape=(
            jax.ShapeDtypeStruct((nodes, hidden), low),
            jax.ShapeDtypeStruct((nodes, hidden // 2), low),
            jax.ShapeDtypeStruct((nodes, hidden // 2), low),
            jax.ShapeDtypeStruct((nodes, width), jnp.float32),
            jax.ShapeDtypeStruct((2, nodes, received), low),
            jax.ShapeDtypeStruct((received, width + LANES), jnp.float32),
        ),
        scratch_shapes=[pltpu.VMEM(array.shape, array.dtype) for array in arrays]
        + [
            pltpu.VMEM((nodes, hidden), low),
            pltpu.VMEM((nodes, hidden // 2), low),
            pltpu.VMEM((nodes, hidden // 2), low),
            pltpu.VMEM((nodes, chunk), jnp.float32),
            pltpu.VMEM((nodes, chunk), jnp.float32),
            pltpu.VMEM(((nodes + received) // size, nodes, size), jnp.float32),
            pltpu.VMEM((nodes, nodes + received), low),
            pltpu.VMEM((nodes, nodes + received), low),
            pltpu.VMEM((nodes, width), jnp.float32),
            pltpu.VMEM((received, width + LANES), jnp.float32),
            pltpu.SemaphoreType.DMA((10 + 5 * (hidden // chunk),)),
        ],
        compiler_params=params(),
        name="forward",
    )(rep, tile_column, *arrays)


def received_kernel(
    rep_ref,
    x_any,
    win_any,
    wout_any,
    side_any,
    grad_any,
    weight_any,
    back_any,
    mine_any,
    other_any,
    full_any,
    turned_any,
    return_any,
    x_ref,
    win_ref,
    wout_ref,
    side_ref,
    grad_ref,
    weight_ref,
    back_ref,
    mine_ref,
    other_ref,
    full_ref,
    turned_ref,
    return_ref,
    even_ref,
    odd_ref,
    semaphores,
):
    depth = win_ref.shape[0]
    nodes, width = grad_ref.shape
    chunk = even_ref.shape[1]
    copies = Copies(semaphores)
    copies.start("x", x_any, x_ref)
    weights = Weights(copies, win_any, wout_any, win_ref, wout_ref, chunk)
    later = {
        "side": (side_any, side_ref),
        "grad": (grad_any, grad_ref),
        "weight": (weight_any, weight_ref),
        "back": (back_any, back_ref),
    }
    for name, (source, target) in later.items():
        copies.start(name, source, target)
    copies.wait("x")

    def give(step):
        place = pl.ds(step * chunk // 2, chunk // 2)
        copies.start(("mine", step), mine_ref.at[:, place], mine_any.at[:, place])
        copies.start(("other", step), other_ref.at[:, place], other_any.at[:, place])

    def arrive(step):
        weights.wait(step)
        if step > 1:
            give(step - 2)

    def take(start, hidden, values, half, square):
        split_hidden(hidden, rep_ref[0], mine_ref, other_ref, start)

    projected = hidden_chunks(x_ref[:, :depth], win_ref, wout_ref, (even_ref, odd_ref), arrive, take)
    give(weights.count - 1)
    for name in later:
        copies.wait(name)
    scaling = jnp.sum(x_ref[:, depth:].astype(jnp.float32), axis=1, keepdims=True)
    unit = (projected * scaling).astype(jnp.bfloat16)
    neighbour = dot(weight_ref[0], unit) + dot(weight_ref[1], unit)
    full = grad_ref[...] - neighbour * side_ref[:, 1:2]
    full_ref[...] = full
    back = (back_ref[:, width : width + 1] * unit.astype(jnp.float32) - back_ref[:, :width]).astype(jnp.bfloat16)
    return_ref[...] = back
    copies.start("full", full_ref, full_any)
    copies.start("return", return_ref, return_any)
    turned_ref[:, :nodes] = full.T.astype(jnp.bfloat16)
    turned_ref[:, nodes:] = (back.astype(jnp.float32) * scaling).T.astype(jnp.bfloat16)
    copies.start("turned", turned_ref, turned_any)
    for step in range(weights.count):
        copies.wait(("mine", step))
        copies.wait(("other", step))
    for name in ("full", "return", "turned"):
        copies.wait(name)


def received_part(rep, arrived, weight_in, weight_out, side, grad, weight, back, chunk=512):
    rows = arrived.shape[0]
    hidden = weight_in.shape[1]
    nodes, width = grad.shape
    low = jnp.bfloat16
    arrays = (arrived, weight_in, weight_out, side, grad, weight, back)
    return pl.pallas_call(
        received_kernel,
        in_specs=[SMEM] + [HBM] * 7,
        out_specs=(HBM,) * 5,
        out_shape=(
            jax.ShapeDtypeStruct((rows, hidden // 2), low),
            jax.ShapeDtypeStruct((rows, hidden // 2), low),
            jax.ShapeDtypeStruct((nodes, width), jnp.float32),
            jax.ShapeDtypeStruct((width, nodes + rows), low),
            jax.ShapeDtypeStruct((rows, width), low),
        ),
        scratch_shapes=[pltpu.VMEM(array.shape, array.dtype) for array in arrays]
        + [
            pltpu.VMEM((rows, hidden // 2), low),
            pltpu.VMEM((rows, hidden // 2), low),
            pltpu.VMEM((nodes, width), jnp.float32),
            pltpu.VMEM((width, nodes + rows), low),
            pltpu.VMEM((rows, width), low),
            pltpu.VMEM((rows, chunk), jnp.float32),
            pltpu.VMEM((rows, chunk), jnp.float32),
            pltpu.SemaphoreType.DMA((8 + 4 * (hidden // chunk),)),
        ],
        compiler_params=params(),
        name="received_part",
    )(rep, *arrays)


def chip_total(chunk, copies, arrays, turned_ref, hidden_ref, total_ref, arrive):
    steps = range(0, hidden_ref.shape[1], chunk)
    base = 0
    for index in range(2):
        length = arrays[index].shape[1]
        copies.start(index, arrays[index], turned_ref.at[:, pl.ds(base, length)])
        base += length
    for start in steps:
        place = pl.ds(start, chunk)
        base = 0
        for index in range(2, 6):
            length = arrays[index].shape[0]
            copies.start((index, start), arrays[index].at[:, place], hidden_ref.at[pl.ds(base, length), place])
            base += length
    copies.wait(0)
    copies.wait(1)
    for start in steps:
        for index in range(2, 6):
            copies.wait((index, start))
        arrive(start // LANES)
        total = dot(turned_ref[...], hidden_ref[:, start : start + chunk])
        for step in range(chunk // LANES):
            total_ref[start // LANES + step] = total[:, step * LANES : (step + 1) * LANES]


def total_kernel(chunk, *refs):
    turned_ref, hidden_ref, semaphores = refs[7:]
    chip_total(chunk, Copies(semaphores), refs[:6], turned_ref, hidden_ref, refs[6], lambda ready: None)


def product_kernel(streams, chunk, place_ref, *refs):
    count = 2 * len(streams)
    outputs, scratch = refs[6 : 6 + count], refs[6 + count : 6 + 2 * count]
    turned_ref, hidden_ref, semaphores, total_ref = refs[6 + 2 * count :]
    copies = Copies(semaphores)
    done = [0] * len(streams)

    def arrive(ready):
        given = []
        for stream, (order, low, high) in enumerate(streams):
            bit = order[0]
            first = done[stream]
            spot = first
            while spot < scratch[2 * stream].shape[0]:
                base = ((spot >> bit) << (bit + 1)) | (spot & ((1 << bit) - 1))
                if base + (1 << bit) >= ready:
                    break
                sent, kept = places(spot, bit, place_ref[0])
                scratch[2 * stream][spot] = total_ref[sent, low:high].astype(jnp.bfloat16)
                scratch[2 * stream + 1][spot] = total_ref[kept, low:high]
                spot += 1
            done[stream] = spot
            if spot > first:
                given += [(2 * stream, first, spot), (2 * stream + 1, first, spot)]
        for index, first, last in given:
            place = pl.ds(first, last - first)
            copies.start(("give", index, first), scratch[index].at[place], outputs[index].at[place])

    chip_total(chunk, copies, refs[:6], turned_ref, hidden_ref, total_ref, arrive)
    arrive(total_ref.shape[0])
    for name in list(copies.started):
        if isinstance(name, tuple) and name[0] == "give":
            copies.wait(name)


def places(spot, weight, place, bit=None):
    mine = lax.rem(lax.div(place, 1 << (weight if bit is None else bit)), 2)
    base = ((spot >> weight) << (weight + 1)) | (spot & ((1 << weight) - 1))
    return base + (1 - mine) * (1 << weight), base + mine * (1 << weight)


def fold_kernel(digits, merge, place_ref, *refs):
    count = len(digits)
    outputs = refs[2 * count :]
    base = 0
    for stream, (weight, bit) in enumerate(digits):
        kept_ref, came_ref = refs[2 * stream : 2 * stream + 2]
        target = 0 if merge else stream
        if not merge:
            base = 0
        sent_ref, next_ref = outputs[2 * target : 2 * target + 2]
        rows = slice(base, base + kept_ref.shape[1])
        base = rows.stop
        for spot in range(sent_ref.shape[0]):
            sent, kept = places(spot, weight, place_ref[0], bit)
            sent_ref[spot, rows] = (kept_ref[sent] + came_ref[sent].astype(jnp.float32)).astype(jnp.bfloat16)
            next_ref[spot, rows] = kept_ref[kept] + came_ref[kept].astype(jnp.float32)


def fold_halves(place, digits, merge, kept, came):
    heights = [array.shape[1] for array in kept]
    if merge:
        heights = [sum(heights)]
    blocks, _, depth = kept[0].shape
    shapes = []
    for height in heights:
        shapes.append(jax.ShapeDtypeStruct((blocks // 2, height, depth), jnp.bfloat16))
        shapes.append(jax.ShapeDtypeStruct((blocks // 2, height, depth), jnp.float32))
    operands = [array for pair in zip(kept, came) for array in pair]
    flat = pl.pallas_call(
        functools.partial(fold_kernel, digits, merge),
        in_specs=[SMEM] + [VMEM] * len(operands),
        out_shape=tuple(shapes),
        compiler_params=params(16),
        name="fold_halves",
    )(place, *operands)
    return [tuple(flat[2 * stream : 2 * stream + 2]) for stream in range(len(heights))]


def finish_kernel(factor, *refs):
    base = 0
    for stream in range(len(refs) // 2):
        kept_ref, came_ref = refs[2 * stream : 2 * stream + 2]
        rows = kept_ref.shape[1]
        total = kept_ref[0] + came_ref[0].astype(jnp.float32)
        refs[-1][:, base : base + rows] = total.T * factor
        base += rows


def finish(factor, kept, came):
    width = sum(array.shape[1] for array in kept)
    return pl.pallas_call(
        functools.partial(finish_kernel, factor),
        out_shape=jax.ShapeDtypeStruct((kept[0].shape[2], width), jnp.float32),
        compiler_params=params(16),
        name="finish",
    )(*[array for pair in zip(kept, came) for array in pair])


def product(place, streams, operands, chunk=512):
    width = operands[0].shape[0]
    hidden = operands[2].shape[1]
    blocks = hidden // LANES
    total = (blocks, width, LANES)
    rows = 2 * operands[0].shape[1]
    scratch = [
        pltpu.VMEM((width, rows), jnp.bfloat16),
        pltpu.VMEM((rows, hidden), jnp.bfloat16),
        pltpu.SemaphoreType.DMA((2 + 10 * (hidden // chunk),)),
    ]
    if not streams:
        return pl.pallas_call(
            functools.partial(total_kernel, chunk),
            in_specs=[HBM] * 6,
            out_shape=jax.ShapeDtypeStruct(total, jnp.float32),
            scratch_shapes=scratch,
            compiler_params=params(),
            name="chip_total",
        )(*operands)
    shapes = []
    for _, low, high in streams:
        shapes.append(jax.ShapeDtypeStruct((blocks // 2, high - low, LANES), jnp.bfloat16))
        shapes.append(jax.ShapeDtypeStruct((blocks // 2, high - low, LANES), jnp.float32))
    return pl.pallas_call(
        functools.partial(product_kernel, streams, chunk),
        in_specs=[SMEM] + [HBM] * 6,
        out_specs=(HBM,) * len(shapes),
        out_shape=tuple(shapes),
        scratch_shapes=[pltpu.VMEM(shape.shape, shape.dtype) for shape in shapes]
        + scratch
        + [pltpu.VMEM(total, jnp.float32)],
        compiler_params=params(),
        name="product",
    )(place, *operands)


def slope_kernel(chunk, *refs):
    full_any, pick_any, back_any, side_any, pre_any, wout_any, out_any = refs[:7]
    full_ref, pick_ref, back_ref, side_ref, pre_ref, wout_ref, grad_ref, semaphores = refs[7:]
    copies = Copies(semaphores)
    first = ((full_any, full_ref), (pick_any, pick_ref), (back_any, back_ref), (side_any, side_ref))
    steps = range(0, pre_ref.shape[1], chunk)
    for index, (source, target) in enumerate(first):
        copies.start(index, source, target)
    for start in steps:
        place = pl.ds(start, chunk)
        copies.start(("out", start), wout_any.at[place], wout_ref.at[place])
        copies.start(("pre", start), pre_any.at[:, place], pre_ref.at[:, place])
    for index in range(len(first)):
        copies.wait(index)
    back = dot(pick_ref[...], back_ref[...], 0, 0)
    node = (full_ref[...] + back * side_ref[:, 1:2]).astype(jnp.bfloat16)
    piece = chunk // 2
    for start in steps:
        copies.wait(("out", start))
        copies.wait(("pre", start))
        if start > 0:
            place = pl.ds(start - chunk, chunk)
            copies.start(("grad", start - chunk), grad_ref.at[:, place], out_any.at[:, place])
        for low in range(start, start + chunk, piece):
            place = slice(low, low + piece)
            grad_hidden = dot(node, wout_ref[place], 1, 1)
            slope = pre_ref[:, place].astype(jnp.float32)
            if low >= SLOPED:
                slope = gelu_slope(slope, *gelu_half(slope))
            grad_ref[:, place] = (grad_hidden * slope).astype(jnp.bfloat16)
    place = pl.ds(steps[-1], chunk)
    copies.start(("grad", steps[-1]), grad_ref.at[:, place], out_any.at[:, place])
    for start in steps:
        copies.wait(("grad", start))


def slope_part(full, pick, back, side, pre, weight_out, chunk=1024):
    arrays = (full, pick, back, side, pre, weight_out)
    return pl.pallas_call(
        functools.partial(slope_kernel, chunk),
        in_specs=[HBM] * 6,
        out_specs=HBM,
        out_shape=jax.ShapeDtypeStruct(pre.shape, jnp.bfloat16),
        scratch_shapes=[pltpu.VMEM(array.shape, array.dtype) for array in arrays]
        + [
            pltpu.VMEM(pre.shape, jnp.bfloat16),
            pltpu.SemaphoreType.DMA((4 + 3 * (pre.shape[1] // chunk),)),
        ],
        cost_estimate=pl.CostEstimate(flops=2 * pre.size * full.shape[1], bytes_accessed=16 * MIB, transcendentals=0),
        compiler_params=params(58),
        name="slope_part",
    )(*arrays)


def embed_kernel(chunk, first, grad_any, win_any, *refs):
    out_any, grad_ref, win_ref, out_ref, total_ref, semaphores = refs[-6:]
    copies = Copies(semaphores)
    steps = range(0, grad_ref.shape[1], chunk)
    columns = pl.ds(first, win_ref.shape[0])
    for start in steps:
        place = pl.ds(start, chunk)
        copies.start(("grad", start), grad_any.at[:, place], grad_ref.at[:, place])
        copies.start(("in", start), win_any.at[columns, place], win_ref.at[:, place])
    for start in steps:
        copies.wait(("grad", start))
        copies.wait(("in", start))
        place = slice(start, start + chunk)
        part = dot(grad_ref[:, place], win_ref[:, place], 1, 1)
        if start == 0:
            total_ref[...] = part
        elif start + chunk < grad_ref.shape[1]:
            total_ref[...] += part
        else:
            out_ref[...] = (total_ref[...] + part).astype(jnp.bfloat16)
    copies.start("give", out_ref, out_any.at[:, columns])
    copies.wait("give")


def embed_part(first, length, grad, weight_in, other=None, chunk=1024):
    nodes, hidden = grad.shape
    depth = weight_in.shape[0]
    operands = (grad, weight_in) if other is None else (grad, weight_in, other)
    return pl.pallas_call(
        functools.partial(embed_kernel, chunk, first),
        in_specs=[HBM] * len(operands),
        out_specs=HBM,
        out_shape=jax.ShapeDtypeStruct((nodes, depth), jnp.bfloat16),
        input_output_aliases={} if other is None else {2: 0},
        scratch_shapes=[
            pltpu.VMEM(grad.shape, jnp.bfloat16),
            pltpu.VMEM((length, hidden), jnp.bfloat16),
            pltpu.VMEM((nodes, length), jnp.bfloat16),
            pltpu.VMEM((nodes, length), jnp.float32),
            pltpu.SemaphoreType.DMA((1 + 2 * (hidden // chunk),)),
        ],
        cost_estimate=pl.CostEstimate(flops=2 * grad.size * length, bytes_accessed=9 * MIB, transcendentals=0),
        compiler_params=params(60),
        name="embed_part",
    )(*operands)


def bit_orders(count):
    bits = list(range(count.bit_length() - 1))
    first = len(bits) // 3
    groups = [bits[start : start + first] for start in range(0, 3 * first, first)]
    last = bits[3 * first :]
    return tuple(sum(groups[turn:] + groups[:turn], []) + last for turn in range(3))


def streams_of(dom_count, width):
    cut = width * 11 // 32
    edges = (0, cut, 2 * cut, width)
    return tuple(zip(bit_orders(dom_count), edges[:-1], edges[1:]))


def halves(part, spot, mine):
    sent = lax.dynamic_index_in_dim(part, 1 - mine, spot, keepdims=False).astype(jnp.bfloat16)
    return sent, lax.dynamic_index_in_dim(part, mine, spot, keepdims=False)


def exchange(sent, bit):
    dom_count = lax.axis_size("dom")
    return lax.ppermute(sent, "dom", [(device, device ^ (1 << bit)) for device in range(dom_count)])


def body(
    embeds,
    weight_in,
    weight_out,
    prototypes,
    tile_column,
    tile_weight,
    send_rows,
    send_count,
    label_rows,
    label_class,
):
    nodes, embed_width = embeds.shape
    dom_count = lax.axis_size("dom")
    rep_count = lax.axis_size("rep")
    peers = dom_count * rep_count
    slots = send_rows.shape[2]
    hidden_width, width = weight_out.shape
    depth = hidden_width // peers
    place = lax.axis_index("dom")
    rep = lax.axis_index("rep")
    swap = [(0, 1), (1, 0)]
    fold = LANES // depth
    if fold > 1:
        order = (dom_count // fold, fold, rep_count, depth)
        weight_in = weight_in.reshape((-1,) + order).swapaxes(2, 3).reshape(-1, hidden_width)
        weight_out = weight_out.reshape(order + (-1,)).swapaxes(1, 2).reshape(hidden_width, -1)

    outgoing, pick, side = prepare(send_rows[0].T, send_count, tile_weight, embeds)
    arrived = lax.all_to_all(
        outgoing.reshape(peers, slots, -1), both, split_axis=0, concat_axis=0, tiled=True
    ).reshape(peers * slots, -1)
    pre_act, own, sent_own, grad, weight, back = forward(
        rep[None],
        tile_column,
        embeds,
        weight_in,
        weight_out,
        tile_weight,
        side,
        label_rows[None, :],
        label_class[None, :],
        prototypes,
        peers * slots,
    )
    other_own = lax.ppermute(sent_own, "rep", swap)
    came, sent_came, full, turned, returned = received_part(
        rep[None], arrived, weight_in, weight_out, side, grad, weight, back
    )
    other_turned = lax.ppermute(turned, "rep", swap)
    other_came = lax.ppermute(sent_came, "rep", swap)
    given = lax.all_to_all(
        returned.reshape(peers, slots, width), both, split_axis=0, concat_axis=0, tiled=True
    ).reshape(peers * slots, width)
    operands = (turned, other_turned, own, came, other_own, other_came)

    streams = streams_of(dom_count, width)
    bit_count = dom_count.bit_length() - 1
    parts = []
    if fold > 1:
        total = product(place[None], (), operands)
        total = total.reshape(-1, width, fold, depth).swapaxes(1, 2).reshape((2,) * bit_count + (width, depth))
        for order, low, high in streams:
            spot = bit_count - 1 - order[0]
            pair = halves(total[..., low:high, :], spot, (place >> order[0]) & 1)
            parts.append(tuple(array.reshape(-1, high - low, depth) for array in pair))
    else:
        flat = product(place[None], streams, operands)
        parts = [tuple(flat[2 * stream : 2 * stream + 2]) for stream in range(len(streams))]
    parts, full = lax.optimization_barrier((parts, full))
    grad_pre = slope_part(full, pick, given, side, pre_act, weight_out)
    left = [[bit for bit in range(bit_count) if bit != order[0]] for order, _, _ in streams]
    orders = [order for order, _, _ in streams]
    shared = next(step for step in range(bit_count + 1) if all(order[step:] == orders[0][step:] for order in orders))
    beside = (1, bit_count - 1)
    half = embed_width // 2
    embed_grad = None
    for step in range(bit_count):
        if step in beside:
            parts, grad_pre = lax.optimization_barrier((parts, grad_pre))
            embed_grad = embed_part(beside.index(step) * half, half, grad_pre, weight_in, embed_grad)
        elif step > 0:
            parts = lax.optimization_barrier(parts)
        came = [exchange(sent, order[step]) for (sent, _), order in zip(parts, orders)]
        if step == 0:
            came, grad_pre = lax.optimization_barrier((came, grad_pre))
        elif step in beside:
            came, embed_grad = lax.optimization_barrier((came, embed_grad))
        else:
            came = lax.optimization_barrier(came)
        kept = [array for _, array in parts]
        if step + 1 == bit_count:
            break
        digits = [(bits.index(order[step + 1]), order[step + 1]) for bits, order in zip(left, orders)]
        for bits, order in zip(left, orders):
            bits.remove(order[step + 1])
        parts = fold_halves(place[None], digits, step + 1 == shared, kept, came)
        if step + 1 == shared:
            left, orders = left[:1], orders[:1]
    summed = finish(1.0 / math.sqrt(nodes * peers), kept, came)
    return (embed_grad, summed)


def solution(mesh):
    placed = (
        P(both, None),
        P(),
        P(),
        P(),
        P(both, None),
        P(both, None, None, None),
        P(both, None, None),
        P(both, None),
        P(both),
        P(both),
    )
    return jax.shard_map(
        body,
        mesh=mesh,
        in_specs=placed,
        out_specs=(P(both, None), P(both, None)),
        check_vma=False,
    )
```

```python
import functools
import math

import jax
import jax.numpy as jnp
from jax import lax
from jax.experimental import pallas as pl
from jax.experimental.pallas import tpu as pltpu
from jax.sharding import PartitionSpec as P

gelu_inner = 0.7978845608028654
gelu_cubic = 0.044715
LANES = 128
SLOPED = 2048
MIB = 1024 * 1024
both = ("dom", "rep")


def gelu_half(values):
    square = values * values
    return 0.5 + 0.5 * jnp.tanh(values * (gelu_inner + gelu_inner * gelu_cubic * square)), square


def gelu_slope(values, half, square):
    return half + values * half * (2.0 - 2.0 * half) * (gelu_inner + 3.0 * gelu_inner * gelu_cubic * square)


def dot(left, right, left_dim=1, right_dim=0):
    return lax.dot_general(
        left, right, (((left_dim,), (right_dim,)), ((), ())), preferred_element_type=jnp.float32
    )


def params(mib=64):
    return pltpu.CompilerParams(vmem_limit_bytes=mib * MIB)


VMEM = pl.BlockSpec(memory_space=pltpu.VMEM)
SMEM = pl.BlockSpec(memory_space=pltpu.SMEM)
HBM = pl.BlockSpec(memory_space=pltpu.HBM)


class Copies:
    def __init__(self, semaphores):
        self.semaphores = semaphores
        self.started = {}

    def start(self, name, source, target):
        copy = pltpu.make_async_copy(source, target, self.semaphores.at[len(self.started)])
        copy.start()
        self.started[name] = copy

    def wait(self, name):
        self.started[name].wait()


def bits_of(values):
    high = values.astype(jnp.bfloat16).astype(jnp.float32)
    middle = (values - high).astype(jnp.bfloat16).astype(jnp.float32)
    return high, middle, values - high - middle


def prepare_kernel(
    rows_any,
    count_any,
    tiles_any,
    embeds_any,
    out_any,
    pick_any,
    side_any,
    rows_ref,
    count_ref,
    tiles_ref,
    embeds_ref,
    out_ref,
    pick_ref,
    side_ref,
    semaphores,
):
    copies = Copies(semaphores)
    copies.start("rows", rows_any, rows_ref)
    copies.start("count", count_any, count_ref)
    copies.start("embeds", embeds_any, embeds_ref)
    copies.start("tiles", tiles_any, tiles_ref)
    copies.wait("rows")
    copies.wait("count")
    slots, peers = rows_ref.shape
    nodes, width = embeds_ref.shape
    sent = slots * peers
    blocks, tiles = tiles_ref.shape[:2]
    spread = jnp.concatenate([rows_ref[...].astype(jnp.float32)] * peers, axis=0)
    row = lax.broadcasted_iota(jnp.int32, (sent, peers), 0)
    chosen = lax.div(row, slots) == lax.broadcasted_iota(jnp.int32, (sent, peers), 1)
    index = jnp.sum(jnp.where(chosen, spread, 0.0), axis=1, keepdims=True).astype(jnp.int32)
    counts = jnp.broadcast_to(count_ref[...].astype(jnp.float32), (sent, peers))
    count = jnp.sum(jnp.where(chosen, counts, 0.0), axis=1, keepdims=True).astype(jnp.int32)
    slot = lax.rem(lax.broadcasted_iota(jnp.int32, (sent, nodes), 0), slots)
    node = lax.broadcasted_iota(jnp.int32, (sent, nodes), 1)
    pick = jnp.where((node == index) & (slot < count), 1.0, 0.0).astype(jnp.bfloat16)
    pick_ref[...] = pick
    copies.wait("embeds")
    copies.start("pick", pick_ref, pick_any)
    out_ref[:, :width] = dot(pick, embeds_ref[...]).astype(jnp.bfloat16)
    copies.wait("tiles")
    copies.start("wide", out_ref.at[:, pl.ds(0, width)], out_any.at[:, pl.ds(0, width)])
    size = tiles_ref.shape[2]
    lane = lax.broadcasted_iota(jnp.int32, (size, LANES), 1)
    parts = []
    for block in range(blocks):
        total = tiles_ref[block, 0].astype(jnp.float32)
        for tile in range(1, tiles):
            total = total + tiles_ref[block, tile].astype(jnp.float32)
        rowsum = jnp.sum(total, axis=1, keepdims=True)
        scaling = lax.rsqrt(1.0 + rowsum)
        side_ref[block * size : (block + 1) * size, :] = jnp.where(lane == 0, rowsum, scaling)
        high, middle, low = bits_of(scaling)
        part = jnp.where(lane == 0, high, jnp.where(lane == 1, middle, jnp.where(lane == 2, low, 0.0)))
        parts.append(part.astype(jnp.bfloat16))
    out_ref[:, width:] = dot(pick, jnp.concatenate(parts, axis=0)).astype(jnp.bfloat16)
    copies.start("side", side_ref, side_any)
    copies.start("narrow", out_ref.at[:, pl.ds(width, LANES)], out_any.at[:, pl.ds(width, LANES)])
    for name in ("pick", "wide", "side", "narrow"):
        copies.wait(name)


def prepare(rows, count, tile_weight, embeds):
    sent = rows.shape[0] * rows.shape[1]
    nodes, width = embeds.shape
    shapes = (
        jax.ShapeDtypeStruct((sent, width + LANES), jnp.bfloat16),
        jax.ShapeDtypeStruct((sent, nodes), jnp.bfloat16),
        jax.ShapeDtypeStruct((nodes, LANES), jnp.float32),
    )
    return pl.pallas_call(
        prepare_kernel,
        in_specs=[HBM] * 4,
        out_specs=(HBM,) * 3,
        out_shape=shapes,
        scratch_shapes=[
            pltpu.VMEM(rows.shape, jnp.int32),
            pltpu.VMEM(count.shape, jnp.int32),
            pltpu.VMEM(tile_weight.shape, jnp.bfloat16),
            pltpu.VMEM(embeds.shape, jnp.bfloat16),
        ]
        + [pltpu.VMEM(shape.shape, shape.dtype) for shape in shapes]
        + [pltpu.SemaphoreType.DMA((8,))],
        compiler_params=params(),
        name="prepare",
    )(rows, count, tile_weight, embeds)


def split_hidden(hidden, rep, mine_ref, other_ref, start):
    for pair in range(hidden.shape[1] // (2 * LANES)):
        low = hidden[:, 2 * pair * LANES : (2 * pair + 1) * LANES]
        high = hidden[:, (2 * pair + 1) * LANES : (2 * pair + 2) * LANES]
        place = slice(start // 2 + pair * LANES, start // 2 + (pair + 1) * LANES)
        mine_ref[:, place] = jnp.where(rep == 0, low, high)
        other_ref[:, place] = jnp.where(rep == 0, high, low)


def hidden_chunks(x, win_ref, wout_ref, waiting, arrive, take, piece=256):
    chunk = waiting[0].shape[1]
    count = win_ref.shape[1] // chunk
    projected = None
    for step in range(count + 1):
        arrive(step)
        for low in range(0, chunk, piece):
            place = slice(low, low + piece)
            if step < count:
                ahead = step * chunk + low
                waiting[step % 2][:, place] = dot(x, win_ref[:, ahead : ahead + piece])
            if step > 0:
                start = (step - 1) * chunk + low
                values = waiting[(step - 1) % 2][:, place]
                half, square = gelu_half(values)
                hidden = (values * half).astype(jnp.bfloat16)
                take(start, hidden, values, half, square)
                part = dot(hidden, wout_ref[start : start + piece])
                projected = part if projected is None else projected + part
    return projected


class Weights:
    def __init__(self, copies, win_any, wout_any, win_ref, wout_ref, chunk):
        self.copies = copies
        self.count = win_ref.shape[1] // chunk
        for step in range(self.count):
            place = pl.ds(step * chunk, chunk)
            copies.start(("in", step), win_any.at[:, place], win_ref.at[:, place])
            copies.start(("out", step), wout_any.at[place], wout_ref.at[place])

    def wait(self, step):
        if step < self.count:
            self.copies.wait(("in", step))
        if step > 0:
            self.copies.wait(("out", step - 1))


def forward_kernel(
    rep_ref,
    column_ref,
    x_any,
    win_any,
    wout_any,
    tiles_any,
    side_any,
    rows_any,
    class_any,
    proto_any,
    pre_any,
    mine_any,
    other_any,
    grad_any,
    weight_any,
    back_any,
    x_ref,
    win_ref,
    wout_ref,
    tiles_ref,
    side_ref,
    rows_ref,
    class_ref,
    proto_ref,
    pre_ref,
    mine_ref,
    other_ref,
    even_ref,
    odd_ref,
    dense_ref,
    high_ref,
    low_ref,
    grad_ref,
    back_ref,
    semaphores,
):
    copies = Copies(semaphores)
    chunk = even_ref.shape[1]
    copies.start("x", x_any, x_ref)
    copies.start("tiles", tiles_any, tiles_ref)
    weights = Weights(copies, win_any, wout_any, win_ref, wout_ref, chunk)
    later = {
        "side": (side_any, side_ref),
        "rows": (rows_any, rows_ref),
        "class": (class_any, class_ref),
        "proto": (proto_any, proto_ref),
    }
    for name, (source, target) in later.items():
        copies.start(name, source, target)
    nodes = x_ref.shape[0]
    copies.wait("x")

    def give(step):
        whole_place = pl.ds(step * chunk, chunk)
        half_place = pl.ds(step * chunk // 2, chunk // 2)
        copies.start(("pre", step), pre_ref.at[:, whole_place], pre_any.at[:, whole_place])
        copies.start(("mine", step), mine_ref.at[:, half_place], mine_any.at[:, half_place])
        copies.start(("other", step), other_ref.at[:, half_place], other_any.at[:, half_place])

    def arrive(step):
        weights.wait(step)
        if step > 1:
            give(step - 2)
        if step == 0:
            copies.wait("tiles")
            dense_graph(column_ref, tiles_ref, dense_ref, high_ref, low_ref)
        if step == 1:
            extra = pl.ds(nodes, high_ref.shape[1] - nodes)
            copies.start("high", high_ref.at[:, extra], weight_any.at[0])
            copies.start("low", low_ref.at[:, extra], weight_any.at[1])

    def take(start, hidden, values, half, square):
        kept = gelu_slope(values, half, square) if start < SLOPED else values
        pre_ref[:, start : start + hidden.shape[1]] = kept.astype(jnp.bfloat16)
        split_hidden(hidden, rep_ref[0], mine_ref, other_ref, start)

    projected = hidden_chunks(x_ref[...], win_ref, wout_ref, (even_ref, odd_ref), arrive, take)
    give(weights.count - 1)
    for name in later:
        copies.wait(name)
    width = projected.shape[1]
    rowsum = side_ref[:, 0:1]
    scaling = side_ref[:, 1:2]
    unit = (projected * scaling).astype(jnp.bfloat16)
    unit_float = unit.astype(jnp.float32)
    beside = jnp.concatenate([unit, jnp.ones((nodes, LANES), jnp.bfloat16)], axis=1)
    high, low = high_ref[...], low_ref[...]
    turned = dot(high, beside, 0, 0) + dot(low, beside, 0, 0)
    back_ref[...] = turned[nodes:]
    copies.start("back", back_ref, back_any)
    neighbour = dot(high[:, :nodes], unit) + dot(low[:, :nodes], unit)
    own = turned[:nodes, width : width + 1] * unit_float - turned[:nodes, :width]
    marked = rows_ref.shape[1]
    node = lax.broadcasted_iota(jnp.int32, (nodes, marked), 0)
    label = jnp.where(node == rows_ref[...], 1.0, 0.0)
    name = lax.broadcasted_iota(jnp.int32, (proto_ref.shape[0], marked), 0)
    named = jnp.where(name == class_ref[...], 1.0, 0.0).astype(jnp.bfloat16)
    target = dot(named, proto_ref[...], 0, 0).astype(jnp.bfloat16)
    pull = jnp.sum(label, axis=1, keepdims=True) * projected - dot(label.astype(jnp.bfloat16), target)
    grad_ref[...] = (rowsum * unit_float - neighbour + own) * scaling + pull
    copies.start("grad", grad_ref, grad_any)
    for step in range(weights.count):
        for name in ("pre", "mine", "other"):
            copies.wait((name, step))
    for name in ("high", "low", "back", "grad"):
        copies.wait(name)


def dense_graph(column_ref, tiles_ref, dense_ref, high_ref, low_ref):
    blocks, tiles, size, _ = tiles_ref.shape
    dense_ref[...] = jnp.zeros_like(dense_ref)
    for block in range(blocks):
        for tile in range(tiles):
            column = column_ref[block, tile]
            place = slice(block * size, (block + 1) * size)
            dense_ref[column, place, :] += tiles_ref[block, tile].astype(jnp.float32)
    for column in range(dense_ref.shape[0]):
        dense = dense_ref[column]
        high = dense.astype(jnp.bfloat16)
        place = slice(column * size, (column + 1) * size)
        high_ref[:, place] = high
        low_ref[:, place] = (dense - high.astype(jnp.float32)).astype(jnp.bfloat16)


def forward(
    rep,
    tile_column,
    embeds,
    weight_in,
    weight_out,
    tile_weight,
    side,
    label_rows,
    label_class,
    prototypes,
    received,
    chunk=1024,
):
    nodes, depth = embeds.shape
    hidden = weight_in.shape[1]
    width = weight_out.shape[1]
    size = tile_weight.shape[2]
    low = jnp.bfloat16
    arrays = (embeds, weight_in, weight_out, tile_weight, side, label_rows, label_class, prototypes)
    return pl.pallas_call(
        forward_kernel,
        in_specs=[SMEM] * 2 + [HBM] * 8,
        out_specs=(HBM,) * 6,
        out_shape=(
            jax.ShapeDtypeStruct((nodes, hidden), low),
            jax.ShapeDtypeStruct((nodes, hidden // 2), low),
            jax.ShapeDtypeStruct((nodes, hidden // 2), low),
            jax.ShapeDtypeStruct((nodes, width), jnp.float32),
            jax.ShapeDtypeStruct((2, nodes, received), low),
            jax.ShapeDtypeStruct((received, width + LANES), jnp.float32),
        ),
        scratch_shapes=[pltpu.VMEM(array.shape, array.dtype) for array in arrays]
        + [
            pltpu.VMEM((nodes, hidden), low),
            pltpu.VMEM((nodes, hidden // 2), low),
            pltpu.VMEM((nodes, hidden // 2), low),
            pltpu.VMEM((nodes, chunk), jnp.float32),
            pltpu.VMEM((nodes, chunk), jnp.float32),
            pltpu.VMEM(((nodes + received) // size, nodes, size), jnp.float32),
            pltpu.VMEM((nodes, nodes + received), low),
            pltpu.VMEM((nodes, nodes + received), low),
            pltpu.VMEM((nodes, width), jnp.float32),
            pltpu.VMEM((received, width + LANES), jnp.float32),
            pltpu.SemaphoreType.DMA((10 + 5 * (hidden // chunk),)),
        ],
        compiler_params=params(),
        name="forward",
    )(rep, tile_column, *arrays)


def received_kernel(
    rep_ref,
    x_any,
    win_any,
    wout_any,
    side_any,
    grad_any,
    weight_any,
    back_any,
    mine_any,
    other_any,
    full_any,
    turned_any,
    return_any,
    x_ref,
    win_ref,
    wout_ref,
    side_ref,
    grad_ref,
    weight_ref,
    back_ref,
    mine_ref,
    other_ref,
    full_ref,
    turned_ref,
    return_ref,
    even_ref,
    odd_ref,
    semaphores,
):
    depth = win_ref.shape[0]
    nodes, width = grad_ref.shape
    chunk = even_ref.shape[1]
    copies = Copies(semaphores)
    copies.start("x", x_any, x_ref)
    weights = Weights(copies, win_any, wout_any, win_ref, wout_ref, chunk)
    later = {
        "side": (side_any, side_ref),
        "grad": (grad_any, grad_ref),
        "weight": (weight_any, weight_ref),
        "back": (back_any, back_ref),
    }
    for name, (source, target) in later.items():
        copies.start(name, source, target)
    copies.wait("x")

    def give(step):
        place = pl.ds(step * chunk // 2, chunk // 2)
        copies.start(("mine", step), mine_ref.at[:, place], mine_any.at[:, place])
        copies.start(("other", step), other_ref.at[:, place], other_any.at[:, place])

    def arrive(step):
        weights.wait(step)
        if step > 1:
            give(step - 2)

    def take(start, hidden, values, half, square):
        split_hidden(hidden, rep_ref[0], mine_ref, other_ref, start)

    projected = hidden_chunks(x_ref[:, :depth], win_ref, wout_ref, (even_ref, odd_ref), arrive, take)
    give(weights.count - 1)
    for name in later:
        copies.wait(name)
    scaling = jnp.sum(x_ref[:, depth:].astype(jnp.float32), axis=1, keepdims=True)
    unit = (projected * scaling).astype(jnp.bfloat16)
    neighbour = dot(weight_ref[0], unit) + dot(weight_ref[1], unit)
    full = grad_ref[...] - neighbour * side_ref[:, 1:2]
    full_ref[...] = full
    back = (back_ref[:, width : width + 1] * unit.astype(jnp.float32) - back_ref[:, :width]).astype(jnp.bfloat16)
    return_ref[...] = back
    copies.start("full", full_ref, full_any)
    copies.start("return", return_ref, return_any)
    turned_ref[:, :nodes] = full.T.astype(jnp.bfloat16)
    turned_ref[:, nodes:] = (back.astype(jnp.float32) * scaling).T.astype(jnp.bfloat16)
    copies.start("turned", turned_ref, turned_any)
    for step in range(weights.count):
        copies.wait(("mine", step))
        copies.wait(("other", step))
    for name in ("full", "return", "turned"):
        copies.wait(name)


def received_part(rep, arrived, weight_in, weight_out, side, grad, weight, back, chunk=512):
    rows = arrived.shape[0]
    hidden = weight_in.shape[1]
    nodes, width = grad.shape
    low = jnp.bfloat16
    arrays = (arrived, weight_in, weight_out, side, grad, weight, back)
    return pl.pallas_call(
        received_kernel,
        in_specs=[SMEM] + [HBM] * 7,
        out_specs=(HBM,) * 5,
        out_shape=(
            jax.ShapeDtypeStruct((rows, hidden // 2), low),
            jax.ShapeDtypeStruct((rows, hidden // 2), low),
            jax.ShapeDtypeStruct((nodes, width), jnp.float32),
            jax.ShapeDtypeStruct((width, nodes + rows), low),
            jax.ShapeDtypeStruct((rows, width), low),
        ),
        scratch_shapes=[pltpu.VMEM(array.shape, array.dtype) for array in arrays]
        + [
            pltpu.VMEM((rows, hidden // 2), low),
            pltpu.VMEM((rows, hidden // 2), low),
            pltpu.VMEM((nodes, width), jnp.float32),
            pltpu.VMEM((width, nodes + rows), low),
            pltpu.VMEM((rows, width), low),
            pltpu.VMEM((rows, chunk), jnp.float32),
            pltpu.VMEM((rows, chunk), jnp.float32),
            pltpu.SemaphoreType.DMA((8 + 4 * (hidden // chunk),)),
        ],
        compiler_params=params(),
        name="received_part",
    )(rep, *arrays)


def chip_total(chunk, copies, arrays, turned_ref, hidden_ref, total_ref, arrive):
    hidden = hidden_ref.shape[1]
    edges = [0] + list(range(chunk // 2, hidden, chunk)) + [hidden]
    steps = list(zip(edges[:-1], edges[1:]))
    base = 0
    for index in range(2):
        length = arrays[index].shape[1]
        copies.start(index, arrays[index], turned_ref.at[:, pl.ds(base, length)])
        base += length
    for start, end in steps:
        place = pl.ds(start, end - start)
        base = 0
        for index in range(2, 6):
            length = arrays[index].shape[0]
            copies.start((index, start), arrays[index].at[:, place], hidden_ref.at[pl.ds(base, length), place])
            base += length
    copies.wait(0)
    copies.wait(1)
    for start, end in steps:
        for index in range(2, 6):
            copies.wait((index, start))
        arrive(start // LANES)
        total = dot(turned_ref[...], hidden_ref[:, start:end])
        for step in range((end - start) // LANES):
            total_ref[start // LANES + step] = total[:, step * LANES : (step + 1) * LANES]


def total_kernel(chunk, *refs):
    turned_ref, hidden_ref, semaphores = refs[7:]
    chip_total(chunk, Copies(semaphores), refs[:6], turned_ref, hidden_ref, refs[6], lambda ready: None)


def product_kernel(streams, chunk, place_ref, *refs):
    count = 2 * len(streams)
    outputs, scratch = refs[6 : 6 + count], refs[6 + count : 6 + 2 * count]
    turned_ref, hidden_ref, semaphores, total_ref = refs[6 + 2 * count :]
    copies = Copies(semaphores)
    done = [0] * len(streams)

    def arrive(ready):
        given = []
        for stream, (order, low, high) in enumerate(streams):
            bit = order[0]
            first = done[stream]
            spot = first
            while spot < scratch[2 * stream].shape[0]:
                base = ((spot >> bit) << (bit + 1)) | (spot & ((1 << bit) - 1))
                if base + (1 << bit) >= ready:
                    break
                sent, kept = places(spot, bit, place_ref[0])
                scratch[2 * stream][spot] = total_ref[sent, low:high].astype(jnp.bfloat16)
                scratch[2 * stream + 1][spot] = total_ref[kept, low:high]
                spot += 1
            done[stream] = spot
            if spot > first:
                given += [(2 * stream, first, spot), (2 * stream + 1, first, spot)]
        for index, first, last in given:
            place = pl.ds(first, last - first)
            copies.start(("give", index, first), scratch[index].at[place], outputs[index].at[place])

    chip_total(chunk, copies, refs[:6], turned_ref, hidden_ref, total_ref, arrive)
    arrive(total_ref.shape[0])
    for name in list(copies.started):
        if isinstance(name, tuple) and name[0] == "give":
            copies.wait(name)


def places(spot, weight, place, bit=None):
    mine = lax.rem(lax.div(place, 1 << (weight if bit is None else bit)), 2)
    base = ((spot >> weight) << (weight + 1)) | (spot & ((1 << weight) - 1))
    return base + (1 - mine) * (1 << weight), base + mine * (1 << weight)


def fold_kernel(digits, merge, place_ref, *refs):
    count = len(digits)
    outputs = refs[2 * count :]
    base = 0
    for stream, (weight, bit) in enumerate(digits):
        kept_ref, came_ref = refs[2 * stream : 2 * stream + 2]
        target = 0 if merge else stream
        if not merge:
            base = 0
        sent_ref, next_ref = outputs[2 * target : 2 * target + 2]
        rows = slice(base, base + kept_ref.shape[1])
        base = rows.stop
        for spot in range(sent_ref.shape[0]):
            sent, kept = places(spot, weight, place_ref[0], bit)
            sent_ref[spot, rows] = (kept_ref[sent] + came_ref[sent].astype(jnp.float32)).astype(jnp.bfloat16)
            next_ref[spot, rows] = kept_ref[kept] + came_ref[kept].astype(jnp.float32)


def fold_halves(place, digits, merge, kept, came):
    heights = [array.shape[1] for array in kept]
    if merge:
        heights = [sum(heights)]
    blocks, _, depth = kept[0].shape
    shapes = []
    for height in heights:
        shapes.append(jax.ShapeDtypeStruct((blocks // 2, height, depth), jnp.bfloat16))
        shapes.append(jax.ShapeDtypeStruct((blocks // 2, height, depth), jnp.float32))
    operands = [array for pair in zip(kept, came) for array in pair]
    flat = pl.pallas_call(
        functools.partial(fold_kernel, digits, merge),
        in_specs=[SMEM] + [VMEM] * len(operands),
        out_shape=tuple(shapes),
        compiler_params=params(16),
        name="fold_halves",
    )(place, *operands)
    return [tuple(flat[2 * stream : 2 * stream + 2]) for stream in range(len(heights))]


def finish_kernel(factor, *refs):
    base = 0
    for stream in range(len(refs) // 2):
        kept_ref, came_ref = refs[2 * stream : 2 * stream + 2]
        rows = kept_ref.shape[1]
        total = kept_ref[0] + came_ref[0].astype(jnp.float32)
        refs[-1][:, base : base + rows] = total.T * factor
        base += rows


def finish(factor, kept, came):
    width = sum(array.shape[1] for array in kept)
    return pl.pallas_call(
        functools.partial(finish_kernel, factor),
        out_shape=jax.ShapeDtypeStruct((kept[0].shape[2], width), jnp.float32),
        compiler_params=params(16),
        name="finish",
    )(*[array for pair in zip(kept, came) for array in pair])


def product(place, streams, operands, chunk=1024):
    width = operands[0].shape[0]
    hidden = operands[2].shape[1]
    blocks = hidden // LANES
    total = (blocks, width, LANES)
    rows = 2 * operands[0].shape[1]
    scratch = [
        pltpu.VMEM((width, rows), jnp.bfloat16),
        pltpu.VMEM((rows, hidden), jnp.bfloat16),
        pltpu.SemaphoreType.DMA((2 + 10 * (hidden // chunk + 1),)),
    ]
    if not streams:
        return pl.pallas_call(
            functools.partial(total_kernel, chunk),
            in_specs=[HBM] * 6,
            out_shape=jax.ShapeDtypeStruct(total, jnp.float32),
            scratch_shapes=scratch,
            compiler_params=params(),
            name="chip_total",
        )(*operands)
    shapes = []
    for _, low, high in streams:
        shapes.append(jax.ShapeDtypeStruct((blocks // 2, high - low, LANES), jnp.bfloat16))
        shapes.append(jax.ShapeDtypeStruct((blocks // 2, high - low, LANES), jnp.float32))
    return pl.pallas_call(
        functools.partial(product_kernel, streams, chunk),
        in_specs=[SMEM] + [HBM] * 6,
        out_specs=(HBM,) * len(shapes),
        out_shape=tuple(shapes),
        scratch_shapes=[pltpu.VMEM(shape.shape, shape.dtype) for shape in shapes]
        + scratch
        + [pltpu.VMEM(total, jnp.float32)],
        compiler_params=params(),
        name="product",
    )(place, *operands)


def slope_kernel(chunk, *refs):
    full_any, pick_any, back_any, side_any, pre_any, wout_any, out_any = refs[:7]
    full_ref, pick_ref, back_ref, side_ref, pre_ref, wout_ref, grad_ref, semaphores = refs[7:]
    copies = Copies(semaphores)
    first = ((full_any, full_ref), (pick_any, pick_ref), (back_any, back_ref), (side_any, side_ref))
    steps = range(0, pre_ref.shape[1], chunk)
    for index, (source, target) in enumerate(first):
        copies.start(index, source, target)
    for start in steps:
        place = pl.ds(start, chunk)
        copies.start(("out", start), wout_any.at[place], wout_ref.at[place])
        copies.start(("pre", start), pre_any.at[:, place], pre_ref.at[:, place])
    for index in range(len(first)):
        copies.wait(index)
    back = dot(pick_ref[...], back_ref[...], 0, 0)
    node = (full_ref[...] + back * side_ref[:, 1:2]).astype(jnp.bfloat16)
    piece = chunk // 2
    for start in steps:
        copies.wait(("out", start))
        copies.wait(("pre", start))
        if start > 0:
            place = pl.ds(start - chunk, chunk)
            copies.start(("grad", start - chunk), grad_ref.at[:, place], out_any.at[:, place])
        for low in range(start, start + chunk, piece):
            place = slice(low, low + piece)
            grad_hidden = dot(node, wout_ref[place], 1, 1)
            slope = pre_ref[:, place].astype(jnp.float32)
            if low >= SLOPED:
                slope = gelu_slope(slope, *gelu_half(slope))
            grad_ref[:, place] = (grad_hidden * slope).astype(jnp.bfloat16)
    place = pl.ds(steps[-1], chunk)
    copies.start(("grad", steps[-1]), grad_ref.at[:, place], out_any.at[:, place])
    for start in steps:
        copies.wait(("grad", start))


def slope_part(full, pick, back, side, pre, weight_out, chunk=1024):
    arrays = (full, pick, back, side, pre, weight_out)
    return pl.pallas_call(
        functools.partial(slope_kernel, chunk),
        in_specs=[HBM] * 6,
        out_specs=HBM,
        out_shape=jax.ShapeDtypeStruct(pre.shape, jnp.bfloat16),
        scratch_shapes=[pltpu.VMEM(array.shape, array.dtype) for array in arrays]
        + [
            pltpu.VMEM(pre.shape, jnp.bfloat16),
            pltpu.SemaphoreType.DMA((4 + 3 * (pre.shape[1] // chunk),)),
        ],
        cost_estimate=pl.CostEstimate(flops=2 * pre.size * full.shape[1], bytes_accessed=16 * MIB, transcendentals=0),
        compiler_params=params(58),
        name="slope_part",
    )(*arrays)


def embed_kernel(chunk, first, grad_any, win_any, *refs):
    out_any, grad_ref, win_ref, out_ref, total_ref, semaphores = refs[-6:]
    copies = Copies(semaphores)
    steps = range(0, grad_ref.shape[1], chunk)
    columns = pl.ds(first, win_ref.shape[0])
    for start in steps:
        place = pl.ds(start, chunk)
        copies.start(("grad", start), grad_any.at[:, place], grad_ref.at[:, place])
        copies.start(("in", start), win_any.at[columns, place], win_ref.at[:, place])
    for start in steps:
        copies.wait(("grad", start))
        copies.wait(("in", start))
        place = slice(start, start + chunk)
        part = dot(grad_ref[:, place], win_ref[:, place], 1, 1)
        if start == 0:
            total_ref[...] = part
        elif start + chunk < grad_ref.shape[1]:
            total_ref[...] += part
        else:
            out_ref[...] = (total_ref[...] + part).astype(jnp.bfloat16)
    copies.start("give", out_ref, out_any.at[:, columns])
    copies.wait("give")


def embed_part(first, length, grad, weight_in, other=None, chunk=1024):
    nodes, hidden = grad.shape
    depth = weight_in.shape[0]
    operands = (grad, weight_in) if other is None else (grad, weight_in, other)
    return pl.pallas_call(
        functools.partial(embed_kernel, chunk, first),
        in_specs=[HBM] * len(operands),
        out_specs=HBM,
        out_shape=jax.ShapeDtypeStruct((nodes, depth), jnp.bfloat16),
        input_output_aliases={} if other is None else {2: 0},
        scratch_shapes=[
            pltpu.VMEM(grad.shape, jnp.bfloat16),
            pltpu.VMEM((length, hidden), jnp.bfloat16),
            pltpu.VMEM((nodes, length), jnp.bfloat16),
            pltpu.VMEM((nodes, length), jnp.float32),
            pltpu.SemaphoreType.DMA((1 + 2 * (hidden // chunk),)),
        ],
        cost_estimate=pl.CostEstimate(flops=2 * grad.size * length, bytes_accessed=9 * MIB, transcendentals=0),
        compiler_params=params(60),
        name="embed_part",
    )(*operands)


def bit_orders(count):
    bits = list(range(count.bit_length() - 1))
    first = len(bits) // 3
    groups = [bits[start : start + first] for start in range(0, 3 * first, first)]
    last = bits[3 * first :]
    return tuple(sum(groups[turn:] + groups[:turn], []) + last for turn in range(3))


def streams_of(dom_count, width):
    edges = (0, width * 12 // 32, width * 23 // 32, width)
    return tuple(zip(bit_orders(dom_count), edges[:-1], edges[1:]))


def halves(part, spot, mine):
    sent = lax.dynamic_index_in_dim(part, 1 - mine, spot, keepdims=False).astype(jnp.bfloat16)
    return sent, lax.dynamic_index_in_dim(part, mine, spot, keepdims=False)


def exchange(sent, bit):
    dom_count = lax.axis_size("dom")
    return lax.ppermute(sent, "dom", [(device, device ^ (1 << bit)) for device in range(dom_count)])


def body(
    embeds,
    weight_in,
    weight_out,
    prototypes,
    tile_column,
    tile_weight,
    send_rows,
    send_count,
    label_rows,
    label_class,
):
    nodes, embed_width = embeds.shape
    dom_count = lax.axis_size("dom")
    rep_count = lax.axis_size("rep")
    peers = dom_count * rep_count
    slots = send_rows.shape[2]
    hidden_width, width = weight_out.shape
    depth = hidden_width // peers
    place = lax.axis_index("dom")
    rep = lax.axis_index("rep")
    swap = [(0, 1), (1, 0)]
    fold = LANES // depth
    if fold > 1:
        order = (dom_count // fold, fold, rep_count, depth)
        weight_in = weight_in.reshape((-1,) + order).swapaxes(2, 3).reshape(-1, hidden_width)
        weight_out = weight_out.reshape(order + (-1,)).swapaxes(1, 2).reshape(hidden_width, -1)

    outgoing, pick, side = prepare(send_rows[0].T, send_count, tile_weight, embeds)
    arrived = lax.all_to_all(
        outgoing.reshape(peers, slots, -1), both, split_axis=0, concat_axis=0, tiled=True
    ).reshape(peers * slots, -1)
    pre_act, own, sent_own, grad, weight, back = forward(
        rep[None],
        tile_column,
        embeds,
        weight_in,
        weight_out,
        tile_weight,
        side,
        label_rows[None, :],
        label_class[None, :],
        prototypes,
        peers * slots,
    )
    other_own = lax.ppermute(sent_own, "rep", swap)
    came, sent_came, full, turned, returned = received_part(
        rep[None], arrived, weight_in, weight_out, side, grad, weight, back
    )
    other_turned = lax.ppermute(turned, "rep", swap)
    other_came = lax.ppermute(sent_came, "rep", swap)
    given = lax.all_to_all(
        returned.reshape(peers, slots, width), both, split_axis=0, concat_axis=0, tiled=True
    ).reshape(peers * slots, width)
    operands = (turned, other_turned, own, came, other_own, other_came)

    streams = streams_of(dom_count, width)
    bit_count = dom_count.bit_length() - 1
    parts = []
    if fold > 1:
        total = product(place[None], (), operands)
        total = total.reshape(-1, width, fold, depth).swapaxes(1, 2).reshape((2,) * bit_count + (width, depth))
        for order, low, high in streams:
            spot = bit_count - 1 - order[0]
            pair = halves(total[..., low:high, :], spot, (place >> order[0]) & 1)
            parts.append(tuple(array.reshape(-1, high - low, depth) for array in pair))
    else:
        flat = product(place[None], streams, operands)
        parts = [tuple(flat[2 * stream : 2 * stream + 2]) for stream in range(len(streams))]
    parts, full = lax.optimization_barrier((parts, full))
    grad_pre = slope_part(full, pick, given, side, pre_act, weight_out)
    left = [[bit for bit in range(bit_count) if bit != order[0]] for order, _, _ in streams]
    orders = [order for order, _, _ in streams]
    shared = next(step for step in range(bit_count + 1) if all(order[step:] == orders[0][step:] for order in orders))
    beside = (1, bit_count - 1)
    half = embed_width // 2
    embed_grad = None
    for step in range(bit_count):
        if step in beside:
            parts, grad_pre = lax.optimization_barrier((parts, grad_pre))
            embed_grad = embed_part(beside.index(step) * half, half, grad_pre, weight_in, embed_grad)
        elif step > 0:
            parts = lax.optimization_barrier(parts)
        came = [exchange(sent, order[step]) for (sent, _), order in zip(parts, orders)]
        if step == 0:
            came, grad_pre = lax.optimization_barrier((came, grad_pre))
        elif step in beside:
            came, embed_grad = lax.optimization_barrier((came, embed_grad))
        else:
            came = lax.optimization_barrier(came)
        kept = [array for _, array in parts]
        if step + 1 == bit_count:
            break
        digits = [(bits.index(order[step + 1]), order[step + 1]) for bits, order in zip(left, orders)]
        for bits, order in zip(left, orders):
            bits.remove(order[step + 1])
        parts = fold_halves(place[None], digits, step + 1 == shared, kept, came)
        if step + 1 == shared:
            left, orders = left[:1], orders[:1]
    summed = finish(1.0 / math.sqrt(nodes * peers), kept, came)
    return (embed_grad, summed)


def solution(mesh):
    placed = (
        P(both, None),
        P(),
        P(),
        P(),
        P(both, None),
        P(both, None, None, None),
        P(both, None, None),
        P(both, None),
        P(both),
        P(both),
    )
    return jax.shard_map(
        body,
        mesh=mesh,
        in_specs=placed,
        out_specs=(P(both, None), P(both, None)),
        check_vma=False,
    )
```

```python
import functools
import math

import jax
import jax.numpy as jnp
from jax import lax
from jax.experimental import pallas as pl
from jax.experimental.pallas import tpu as pltpu
from jax.sharding import PartitionSpec as P

gelu_inner = 0.7978845608028654
gelu_cubic = 0.044715
LANES = 128
SLOPED = 2048
MIB = 1024 * 1024
both = ("dom", "rep")


def gelu_half(values):
    square = values * values
    return 0.5 + 0.5 * jnp.tanh(values * (gelu_inner + gelu_inner * gelu_cubic * square)), square


def gelu_slope(values, half, square):
    return half + values * half * (2.0 - 2.0 * half) * (gelu_inner + 3.0 * gelu_inner * gelu_cubic * square)


def dot(left, right, left_dim=1, right_dim=0):
    return lax.dot_general(
        left, right, (((left_dim,), (right_dim,)), ((), ())), preferred_element_type=jnp.float32
    )


def params(mib=64):
    return pltpu.CompilerParams(vmem_limit_bytes=mib * MIB)


VMEM = pl.BlockSpec(memory_space=pltpu.VMEM)
SMEM = pl.BlockSpec(memory_space=pltpu.SMEM)
HBM = pl.BlockSpec(memory_space=pltpu.HBM)


class Copies:
    def __init__(self, semaphores):
        self.semaphores = semaphores
        self.started = {}

    def start(self, name, source, target):
        copy = pltpu.make_async_copy(source, target, self.semaphores.at[len(self.started)])
        copy.start()
        self.started[name] = copy

    def wait(self, name):
        self.started[name].wait()


def bits_of(values):
    high = values.astype(jnp.bfloat16).astype(jnp.float32)
    middle = (values - high).astype(jnp.bfloat16).astype(jnp.float32)
    return high, middle, values - high - middle


def prepare_kernel(
    rows_any,
    count_any,
    tiles_any,
    embeds_any,
    out_any,
    pick_any,
    side_any,
    rows_ref,
    count_ref,
    tiles_ref,
    embeds_ref,
    out_ref,
    pick_ref,
    side_ref,
    semaphores,
):
    copies = Copies(semaphores)
    copies.start("rows", rows_any, rows_ref)
    copies.start("count", count_any, count_ref)
    copies.start("embeds", embeds_any, embeds_ref)
    copies.start("tiles", tiles_any, tiles_ref)
    copies.wait("rows")
    copies.wait("count")
    slots, peers = rows_ref.shape
    nodes, width = embeds_ref.shape
    sent = slots * peers
    blocks, tiles = tiles_ref.shape[:2]
    spread = jnp.concatenate([rows_ref[...].astype(jnp.float32)] * peers, axis=0)
    row = lax.broadcasted_iota(jnp.int32, (sent, peers), 0)
    chosen = lax.div(row, slots) == lax.broadcasted_iota(jnp.int32, (sent, peers), 1)
    index = jnp.sum(jnp.where(chosen, spread, 0.0), axis=1, keepdims=True).astype(jnp.int32)
    counts = jnp.broadcast_to(count_ref[...].astype(jnp.float32), (sent, peers))
    count = jnp.sum(jnp.where(chosen, counts, 0.0), axis=1, keepdims=True).astype(jnp.int32)
    slot = lax.rem(lax.broadcasted_iota(jnp.int32, (sent, nodes), 0), slots)
    node = lax.broadcasted_iota(jnp.int32, (sent, nodes), 1)
    pick = jnp.where((node == index) & (slot < count), 1.0, 0.0).astype(jnp.bfloat16)
    pick_ref[...] = pick
    copies.wait("embeds")
    copies.start("pick", pick_ref, pick_any)
    out_ref[:, :width] = dot(pick, embeds_ref[...]).astype(jnp.bfloat16)
    copies.wait("tiles")
    copies.start("wide", out_ref.at[:, pl.ds(0, width)], out_any.at[:, pl.ds(0, width)])
    size = tiles_ref.shape[2]
    lane = lax.broadcasted_iota(jnp.int32, (size, LANES), 1)
    parts = []
    for block in range(blocks):
        total = tiles_ref[block, 0].astype(jnp.float32)
        for tile in range(1, tiles):
            total = total + tiles_ref[block, tile].astype(jnp.float32)
        rowsum = jnp.sum(total, axis=1, keepdims=True)
        scaling = lax.rsqrt(1.0 + rowsum)
        side_ref[block * size : (block + 1) * size, :] = jnp.where(lane == 0, rowsum, scaling)
        high, middle, low = bits_of(scaling)
        part = jnp.where(lane == 0, high, jnp.where(lane == 1, middle, jnp.where(lane == 2, low, 0.0)))
        parts.append(part.astype(jnp.bfloat16))
    out_ref[:, width:] = dot(pick, jnp.concatenate(parts, axis=0)).astype(jnp.bfloat16)
    copies.start("side", side_ref, side_any)
    copies.start("narrow", out_ref.at[:, pl.ds(width, LANES)], out_any.at[:, pl.ds(width, LANES)])
    for name in ("pick", "wide", "side", "narrow"):
        copies.wait(name)


def prepare(rows, count, tile_weight, embeds):
    sent = rows.shape[0] * rows.shape[1]
    nodes, width = embeds.shape
    shapes = (
        jax.ShapeDtypeStruct((sent, width + LANES), jnp.bfloat16),
        jax.ShapeDtypeStruct((sent, nodes), jnp.bfloat16),
        jax.ShapeDtypeStruct((nodes, LANES), jnp.float32),
    )
    return pl.pallas_call(
        prepare_kernel,
        in_specs=[HBM] * 4,
        out_specs=(HBM,) * 3,
        out_shape=shapes,
        scratch_shapes=[
            pltpu.VMEM(rows.shape, jnp.int32),
            pltpu.VMEM(count.shape, jnp.int32),
            pltpu.VMEM(tile_weight.shape, jnp.bfloat16),
            pltpu.VMEM(embeds.shape, jnp.bfloat16),
        ]
        + [pltpu.VMEM(shape.shape, shape.dtype) for shape in shapes]
        + [pltpu.SemaphoreType.DMA((8,))],
        compiler_params=params(),
        name="prepare",
    )(rows, count, tile_weight, embeds)


def split_hidden(hidden, rep, mine_ref, other_ref, start):
    for pair in range(hidden.shape[1] // (2 * LANES)):
        low = hidden[:, 2 * pair * LANES : (2 * pair + 1) * LANES]
        high = hidden[:, (2 * pair + 1) * LANES : (2 * pair + 2) * LANES]
        place = slice(start // 2 + pair * LANES, start // 2 + (pair + 1) * LANES)
        mine_ref[:, place] = jnp.where(rep == 0, low, high)
        other_ref[:, place] = jnp.where(rep == 0, high, low)


def hidden_chunks(x, win_ref, wout_ref, waiting, arrive, take, piece=256):
    chunk = waiting[0].shape[1]
    count = win_ref.shape[1] // chunk
    projected = None
    for step in range(count + 1):
        arrive(step)
        for low in range(0, chunk, piece):
            place = slice(low, low + piece)
            if step < count:
                ahead = step * chunk + low
                waiting[step % 2][:, place] = dot(x, win_ref[:, ahead : ahead + piece])
            if step > 0:
                start = (step - 1) * chunk + low
                values = waiting[(step - 1) % 2][:, place]
                half, square = gelu_half(values)
                hidden = (values * half).astype(jnp.bfloat16)
                take(start, hidden, values, half, square)
                part = dot(hidden, wout_ref[start : start + piece])
                projected = part if projected is None else projected + part
    return projected


class Weights:
    def __init__(self, copies, win_any, wout_any, win_ref, wout_ref, chunk):
        self.copies = copies
        self.count = win_ref.shape[1] // chunk
        for step in range(self.count):
            place = pl.ds(step * chunk, chunk)
            copies.start(("in", step), win_any.at[:, place], win_ref.at[:, place])
            if step % 2 == 0:
                place = pl.ds(step * chunk, 2 * chunk)
                copies.start(("out", step), wout_any.at[place], wout_ref.at[place])

    def wait(self, step):
        if step < self.count:
            self.copies.wait(("in", step))
        if step % 2 == 1:
            self.copies.wait(("out", step - 1))


def forward_kernel(
    rep_ref,
    column_ref,
    x_any,
    win_any,
    wout_any,
    tiles_any,
    side_any,
    rows_any,
    class_any,
    proto_any,
    pre_any,
    mine_any,
    other_any,
    grad_any,
    weight_any,
    back_any,
    x_ref,
    win_ref,
    wout_ref,
    tiles_ref,
    side_ref,
    rows_ref,
    class_ref,
    proto_ref,
    pre_ref,
    mine_ref,
    other_ref,
    even_ref,
    odd_ref,
    dense_ref,
    high_ref,
    low_ref,
    grad_ref,
    back_ref,
    semaphores,
):
    copies = Copies(semaphores)
    chunk = even_ref.shape[1]
    copies.start("x", x_any, x_ref)
    copies.start("tiles", tiles_any, tiles_ref)
    weights = Weights(copies, win_any, wout_any, win_ref, wout_ref, chunk)
    later = {
        "side": (side_any, side_ref),
        "rows": (rows_any, rows_ref),
        "class": (class_any, class_ref),
        "proto": (proto_any, proto_ref),
    }
    for name, (source, target) in later.items():
        copies.start(name, source, target)
    nodes = x_ref.shape[0]
    copies.wait("x")

    def give(step):
        whole_place = pl.ds((step - 1) * chunk, 2 * chunk)
        half_place = pl.ds((step - 1) * chunk // 2, chunk)
        copies.start(("pre", step), pre_ref.at[:, whole_place], pre_any.at[:, whole_place])
        copies.start(("mine", step), mine_ref.at[:, half_place], mine_any.at[:, half_place])
        copies.start(("other", step), other_ref.at[:, half_place], other_any.at[:, half_place])

    def arrive(step):
        weights.wait(step)
        if step > 1 and step % 2 == 1:
            give(step - 2)
        if step == 0:
            copies.wait("tiles")
            dense_graph(column_ref, tiles_ref, dense_ref, high_ref, low_ref)
        if step == 1:
            extra = pl.ds(nodes, high_ref.shape[1] - nodes)
            copies.start("high", high_ref.at[:, extra], weight_any.at[0])
            copies.start("low", low_ref.at[:, extra], weight_any.at[1])

    def take(start, hidden, values, half, square):
        kept = gelu_slope(values, half, square) if start < SLOPED else values
        pre_ref[:, start : start + hidden.shape[1]] = kept.astype(jnp.bfloat16)
        split_hidden(hidden, rep_ref[0], mine_ref, other_ref, start)

    projected = hidden_chunks(x_ref[...], win_ref, wout_ref, (even_ref, odd_ref), arrive, take)
    give(weights.count - 1)
    for name in later:
        copies.wait(name)
    width = projected.shape[1]
    rowsum = side_ref[:, 0:1]
    scaling = side_ref[:, 1:2]
    unit = (projected * scaling).astype(jnp.bfloat16)
    unit_float = unit.astype(jnp.float32)
    beside = jnp.concatenate([unit, jnp.ones((nodes, LANES), jnp.bfloat16)], axis=1)
    high, low = high_ref[...], low_ref[...]
    turned = dot(high, beside, 0, 0) + dot(low, beside, 0, 0)
    back_ref[...] = turned[nodes:]
    copies.start("back", back_ref, back_any)
    neighbour = dot(high[:, :nodes], unit) + dot(low[:, :nodes], unit)
    own = turned[:nodes, width : width + 1] * unit_float - turned[:nodes, :width]
    marked = rows_ref.shape[1]
    node = lax.broadcasted_iota(jnp.int32, (nodes, marked), 0)
    label = jnp.where(node == rows_ref[...], 1.0, 0.0)
    name = lax.broadcasted_iota(jnp.int32, (proto_ref.shape[0], marked), 0)
    named = jnp.where(name == class_ref[...], 1.0, 0.0).astype(jnp.bfloat16)
    target = dot(named, proto_ref[...], 0, 0).astype(jnp.bfloat16)
    pull = jnp.sum(label, axis=1, keepdims=True) * projected - dot(label.astype(jnp.bfloat16), target)
    grad_ref[...] = (rowsum * unit_float - neighbour + own) * scaling + pull
    copies.start("grad", grad_ref, grad_any)
    for step in range(1, weights.count, 2):
        for name in ("pre", "mine", "other"):
            copies.wait((name, step))
    for name in ("high", "low", "back", "grad"):
        copies.wait(name)


def dense_graph(column_ref, tiles_ref, dense_ref, high_ref, low_ref):
    blocks, tiles, size, _ = tiles_ref.shape
    dense_ref[...] = jnp.zeros_like(dense_ref)
    for block in range(blocks):
        for tile in range(tiles):
            column = column_ref[block, tile]
            place = slice(block * size, (block + 1) * size)
            dense_ref[column, place, :] += tiles_ref[block, tile].astype(jnp.float32)
    for column in range(dense_ref.shape[0]):
        dense = dense_ref[column]
        high = dense.astype(jnp.bfloat16)
        place = slice(column * size, (column + 1) * size)
        high_ref[:, place] = high
        low_ref[:, place] = (dense - high.astype(jnp.float32)).astype(jnp.bfloat16)


def forward(
    rep,
    tile_column,
    embeds,
    weight_in,
    weight_out,
    tile_weight,
    side,
    label_rows,
    label_class,
    prototypes,
    received,
    chunk=1024,
):
    nodes, depth = embeds.shape
    hidden = weight_in.shape[1]
    width = weight_out.shape[1]
    size = tile_weight.shape[2]
    low = jnp.bfloat16
    arrays = (embeds, weight_in, weight_out, tile_weight, side, label_rows, label_class, prototypes)
    return pl.pallas_call(
        forward_kernel,
        in_specs=[SMEM] * 2 + [HBM] * 8,
        out_specs=(HBM,) * 6,
        out_shape=(
            jax.ShapeDtypeStruct((nodes, hidden), low),
            jax.ShapeDtypeStruct((nodes, hidden // 2), low),
            jax.ShapeDtypeStruct((nodes, hidden // 2), low),
            jax.ShapeDtypeStruct((nodes, width), jnp.float32),
            jax.ShapeDtypeStruct((2, nodes, received), low),
            jax.ShapeDtypeStruct((received, width + LANES), jnp.float32),
        ),
        scratch_shapes=[pltpu.VMEM(array.shape, array.dtype) for array in arrays]
        + [
            pltpu.VMEM((nodes, hidden), low),
            pltpu.VMEM((nodes, hidden // 2), low),
            pltpu.VMEM((nodes, hidden // 2), low),
            pltpu.VMEM((nodes, chunk), jnp.float32),
            pltpu.VMEM((nodes, chunk), jnp.float32),
            pltpu.VMEM(((nodes + received) // size, nodes, size), jnp.float32),
            pltpu.VMEM((nodes, nodes + received), low),
            pltpu.VMEM((nodes, nodes + received), low),
            pltpu.VMEM((nodes, width), jnp.float32),
            pltpu.VMEM((received, width + LANES), jnp.float32),
            pltpu.SemaphoreType.DMA((10 + 5 * (hidden // chunk),)),
        ],
        compiler_params=params(),
        name="forward",
    )(rep, tile_column, *arrays)


def received_kernel(
    rep_ref,
    x_any,
    win_any,
    wout_any,
    side_any,
    grad_any,
    weight_any,
    back_any,
    mine_any,
    other_any,
    full_any,
    turned_any,
    return_any,
    x_ref,
    win_ref,
    wout_ref,
    side_ref,
    grad_ref,
    weight_ref,
    back_ref,
    mine_ref,
    other_ref,
    full_ref,
    turned_ref,
    return_ref,
    even_ref,
    odd_ref,
    semaphores,
):
    depth = win_ref.shape[0]
    nodes, width = grad_ref.shape
    chunk = even_ref.shape[1]
    copies = Copies(semaphores)
    copies.start("x", x_any, x_ref)
    weights = Weights(copies, win_any, wout_any, win_ref, wout_ref, chunk)
    later = {
        "side": (side_any, side_ref),
        "grad": (grad_any, grad_ref),
        "weight": (weight_any, weight_ref),
        "back": (back_any, back_ref),
    }
    for name, (source, target) in later.items():
        copies.start(name, source, target)
    copies.wait("x")

    group = 4

    def give(step):
        place = pl.ds((step + 1 - group) * chunk // 2, group * chunk // 2)
        copies.start(("mine", step), mine_ref.at[:, place], mine_any.at[:, place])
        copies.start(("other", step), other_ref.at[:, place], other_any.at[:, place])

    def arrive(step):
        weights.wait(step)
        if step > 1 and (step - 1) % group == 0:
            give(step - 2)

    def take(start, hidden, values, half, square):
        split_hidden(hidden, rep_ref[0], mine_ref, other_ref, start)

    projected = hidden_chunks(x_ref[:, :depth], win_ref, wout_ref, (even_ref, odd_ref), arrive, take)
    give(weights.count - 1)
    for name in later:
        copies.wait(name)
    scaling = jnp.sum(x_ref[:, depth:].astype(jnp.float32), axis=1, keepdims=True)
    unit = (projected * scaling).astype(jnp.bfloat16)
    neighbour = dot(weight_ref[0], unit) + dot(weight_ref[1], unit)
    full = grad_ref[...] - neighbour * side_ref[:, 1:2]
    full_ref[...] = full
    back = (back_ref[:, width : width + 1] * unit.astype(jnp.float32) - back_ref[:, :width]).astype(jnp.bfloat16)
    return_ref[...] = back
    copies.start("full", full_ref, full_any)
    copies.start("return", return_ref, return_any)
    turned_ref[:, :nodes] = full.T.astype(jnp.bfloat16)
    turned_ref[:, nodes:] = (back.astype(jnp.float32) * scaling).T.astype(jnp.bfloat16)
    copies.start("turned", turned_ref, turned_any)
    for step in range(group - 1, weights.count, group):
        copies.wait(("mine", step))
        copies.wait(("other", step))
    for name in ("full", "return", "turned"):
        copies.wait(name)


def received_part(rep, arrived, weight_in, weight_out, side, grad, weight, back, chunk=512):
    rows = arrived.shape[0]
    hidden = weight_in.shape[1]
    nodes, width = grad.shape
    low = jnp.bfloat16
    arrays = (arrived, weight_in, weight_out, side, grad, weight, back)
    return pl.pallas_call(
        received_kernel,
        in_specs=[SMEM] + [HBM] * 7,
        out_specs=(HBM,) * 5,
        out_shape=(
            jax.ShapeDtypeStruct((rows, hidden // 2), low),
            jax.ShapeDtypeStruct((rows, hidden // 2), low),
            jax.ShapeDtypeStruct((nodes, width), jnp.float32),
            jax.ShapeDtypeStruct((width, nodes + rows), low),
            jax.ShapeDtypeStruct((rows, width), low),
        ),
        scratch_shapes=[pltpu.VMEM(array.shape, array.dtype) for array in arrays]
        + [
            pltpu.VMEM((rows, hidden // 2), low),
            pltpu.VMEM((rows, hidden // 2), low),
            pltpu.VMEM((nodes, width), jnp.float32),
            pltpu.VMEM((width, nodes + rows), low),
            pltpu.VMEM((rows, width), low),
            pltpu.VMEM((rows, chunk), jnp.float32),
            pltpu.VMEM((rows, chunk), jnp.float32),
            pltpu.SemaphoreType.DMA((8 + 4 * (hidden // chunk),)),
        ],
        compiler_params=params(),
        name="received_part",
    )(rep, *arrays)


def chip_total(chunk, copies, arrays, turned_ref, hidden_ref, total_ref, arrive):
    hidden = hidden_ref.shape[1]
    edges = [0] + list(range(chunk // 2, hidden, chunk)) + [hidden]
    steps = list(zip(edges[:-1], edges[1:]))
    base = 0
    for index in range(2):
        length = arrays[index].shape[1]
        copies.start(index, arrays[index], turned_ref.at[:, pl.ds(base, length)])
        base += length
    for start, end in steps:
        place = pl.ds(start, end - start)
        base = 0
        for index in range(2, 6):
            length = arrays[index].shape[0]
            copies.start((index, start), arrays[index].at[:, place], hidden_ref.at[pl.ds(base, length), place])
            base += length
    copies.wait(0)
    copies.wait(1)
    for start, end in steps:
        for index in range(2, 6):
            copies.wait((index, start))
        arrive(start // LANES)
        total = dot(turned_ref[...], hidden_ref[:, start:end])
        for step in range((end - start) // LANES):
            total_ref[start // LANES + step] = total[:, step * LANES : (step + 1) * LANES]


def total_kernel(chunk, *refs):
    turned_ref, hidden_ref, semaphores = refs[7:]
    chip_total(chunk, Copies(semaphores), refs[:6], turned_ref, hidden_ref, refs[6], lambda ready: None)


def product_kernel(streams, chunk, place_ref, *refs):
    count = 2 * len(streams)
    outputs, scratch = refs[6 : 6 + count], refs[6 + count : 6 + 2 * count]
    turned_ref, hidden_ref, semaphores, total_ref = refs[6 + 2 * count :]
    copies = Copies(semaphores)
    done = [0] * len(streams)

    def arrive(ready):
        given = []
        for stream, (order, low, high) in enumerate(streams):
            bit = order[0]
            first = done[stream]
            spot = first
            while spot < scratch[2 * stream].shape[0]:
                base = ((spot >> bit) << (bit + 1)) | (spot & ((1 << bit) - 1))
                if base + (1 << bit) >= ready:
                    break
                sent, kept = places(spot, bit, place_ref[0])
                scratch[2 * stream][spot] = total_ref[sent, low:high].astype(jnp.bfloat16)
                scratch[2 * stream + 1][spot] = total_ref[kept, low:high]
                spot += 1
            done[stream] = spot
            if spot > first:
                given += [(2 * stream, first, spot), (2 * stream + 1, first, spot)]
        for index, first, last in given:
            place = pl.ds(first, last - first)
            copies.start(("give", index, first), scratch[index].at[place], outputs[index].at[place])

    chip_total(chunk, copies, refs[:6], turned_ref, hidden_ref, total_ref, arrive)
    arrive(total_ref.shape[0])
    for name in list(copies.started):
        if isinstance(name, tuple) and name[0] == "give":
            copies.wait(name)


def places(spot, weight, place, bit=None):
    mine = lax.rem(lax.div(place, 1 << (weight if bit is None else bit)), 2)
    base = ((spot >> weight) << (weight + 1)) | (spot & ((1 << weight) - 1))
    return base + (1 - mine) * (1 << weight), base + mine * (1 << weight)


def fold_kernel(digits, merge, place_ref, *refs):
    count = len(digits)
    outputs = refs[2 * count :]
    base = 0
    for stream, (weight, bit) in enumerate(digits):
        kept_ref, came_ref = refs[2 * stream : 2 * stream + 2]
        target = 0 if merge else stream
        if not merge:
            base = 0
        sent_ref, next_ref = outputs[2 * target : 2 * target + 2]
        rows = slice(base, base + kept_ref.shape[1])
        base = rows.stop
        for spot in range(sent_ref.shape[0]):
            sent, kept = places(spot, weight, place_ref[0], bit)
            sent_ref[spot, rows] = (kept_ref[sent] + came_ref[sent].astype(jnp.float32)).astype(jnp.bfloat16)
            next_ref[spot, rows] = kept_ref[kept] + came_ref[kept].astype(jnp.float32)


def fold_halves(place, digits, merge, kept, came):
    heights = [array.shape[1] for array in kept]
    if merge:
        heights = [sum(heights)]
    blocks, _, depth = kept[0].shape
    shapes = []
    for height in heights:
        shapes.append(jax.ShapeDtypeStruct((blocks // 2, height, depth), jnp.bfloat16))
        shapes.append(jax.ShapeDtypeStruct((blocks // 2, height, depth), jnp.float32))
    operands = [array for pair in zip(kept, came) for array in pair]
    flat = pl.pallas_call(
        functools.partial(fold_kernel, digits, merge),
        in_specs=[SMEM] + [VMEM] * len(operands),
        out_shape=tuple(shapes),
        compiler_params=params(16),
        name="fold_halves",
    )(place, *operands)
    return [tuple(flat[2 * stream : 2 * stream + 2]) for stream in range(len(heights))]


def finish_kernel(factor, *refs):
    base = 0
    for stream in range(len(refs) // 2):
        kept_ref, came_ref = refs[2 * stream : 2 * stream + 2]
        rows = kept_ref.shape[1]
        total = kept_ref[0] + came_ref[0].astype(jnp.float32)
        refs[-1][:, base : base + rows] = total.T * factor
        base += rows


def finish(factor, kept, came):
    width = sum(array.shape[1] for array in kept)
    return pl.pallas_call(
        functools.partial(finish_kernel, factor),
        out_shape=jax.ShapeDtypeStruct((kept[0].shape[2], width), jnp.float32),
        compiler_params=params(16),
        name="finish",
    )(*[array for pair in zip(kept, came) for array in pair])


def product(place, streams, operands, chunk=1024):
    width = operands[0].shape[0]
    hidden = operands[2].shape[1]
    blocks = hidden // LANES
    total = (blocks, width, LANES)
    rows = 2 * operands[0].shape[1]
    scratch = [
        pltpu.VMEM((width, rows), jnp.bfloat16),
        pltpu.VMEM((rows, hidden), jnp.bfloat16),
        pltpu.SemaphoreType.DMA((2 + 10 * (hidden // chunk + 1),)),
    ]
    if not streams:
        return pl.pallas_call(
            functools.partial(total_kernel, chunk),
            in_specs=[HBM] * 6,
            out_shape=jax.ShapeDtypeStruct(total, jnp.float32),
            scratch_shapes=scratch,
            compiler_params=params(),
            name="chip_total",
        )(*operands)
    shapes = []
    for _, low, high in streams:
        shapes.append(jax.ShapeDtypeStruct((blocks // 2, high - low, LANES), jnp.bfloat16))
        shapes.append(jax.ShapeDtypeStruct((blocks // 2, high - low, LANES), jnp.float32))
    return pl.pallas_call(
        functools.partial(product_kernel, streams, chunk),
        in_specs=[SMEM] + [HBM] * 6,
        out_specs=(HBM,) * len(shapes),
        out_shape=tuple(shapes),
        scratch_shapes=[pltpu.VMEM(shape.shape, shape.dtype) for shape in shapes]
        + scratch
        + [pltpu.VMEM(total, jnp.float32)],
        compiler_params=params(),
        name="product",
    )(place, *operands)


def slope_kernel(chunk, *refs):
    full_any, pick_any, back_any, side_any, pre_any, wout_any, out_any = refs[:7]
    full_ref, pick_ref, back_ref, side_ref, pre_ref, wout_ref, grad_ref, semaphores = refs[7:]
    copies = Copies(semaphores)
    first = ((full_any, full_ref), (pick_any, pick_ref), (back_any, back_ref), (side_any, side_ref))
    steps = range(0, pre_ref.shape[1], chunk)
    for index, (source, target) in enumerate(first):
        copies.start(index, source, target)
    for start in steps:
        place = pl.ds(start, chunk)
        copies.start(("out", start), wout_any.at[place], wout_ref.at[place])
        copies.start(("pre", start), pre_any.at[:, place], pre_ref.at[:, place])
    for index in range(len(first)):
        copies.wait(index)
    back = dot(pick_ref[...], back_ref[...], 0, 0)
    node = (full_ref[...] + back * side_ref[:, 1:2]).astype(jnp.bfloat16)
    piece = chunk // 2
    for start in steps:
        copies.wait(("out", start))
        copies.wait(("pre", start))
        if start > 0:
            place = pl.ds(start - chunk, chunk)
            copies.start(("grad", start - chunk), grad_ref.at[:, place], out_any.at[:, place])
        for low in range(start, start + chunk, piece):
            place = slice(low, low + piece)
            grad_hidden = dot(node, wout_ref[place], 1, 1)
            slope = pre_ref[:, place].astype(jnp.float32)
            if low >= SLOPED:
                slope = gelu_slope(slope, *gelu_half(slope))
            grad_ref[:, place] = (grad_hidden * slope).astype(jnp.bfloat16)
    place = pl.ds(steps[-1], chunk)
    copies.start(("grad", steps[-1]), grad_ref.at[:, place], out_any.at[:, place])
    for start in steps:
        copies.wait(("grad", start))


def slope_part(full, pick, back, side, pre, weight_out, chunk=1024):
    arrays = (full, pick, back, side, pre, weight_out)
    return pl.pallas_call(
        functools.partial(slope_kernel, chunk),
        in_specs=[HBM] * 6,
        out_specs=HBM,
        out_shape=jax.ShapeDtypeStruct(pre.shape, jnp.bfloat16),
        scratch_shapes=[pltpu.VMEM(array.shape, array.dtype) for array in arrays]
        + [
            pltpu.VMEM(pre.shape, jnp.bfloat16),
            pltpu.SemaphoreType.DMA((4 + 3 * (pre.shape[1] // chunk),)),
        ],
        cost_estimate=pl.CostEstimate(flops=2 * pre.size * full.shape[1], bytes_accessed=16 * MIB, transcendentals=0),
        compiler_params=params(58),
        name="slope_part",
    )(*arrays)


def embed_kernel(chunk, first, grad_any, win_any, *refs):
    out_any, grad_ref, win_ref, out_ref, total_ref, semaphores = refs[-6:]
    copies = Copies(semaphores)
    steps = range(0, grad_ref.shape[1], chunk)
    columns = pl.ds(first, win_ref.shape[0])
    for start in steps:
        place = pl.ds(start, chunk)
        copies.start(("grad", start), grad_any.at[:, place], grad_ref.at[:, place])
        copies.start(("in", start), win_any.at[columns, place], win_ref.at[:, place])
    for start in steps:
        copies.wait(("grad", start))
        copies.wait(("in", start))
        place = slice(start, start + chunk)
        part = dot(grad_ref[:, place], win_ref[:, place], 1, 1)
        if start == 0:
            total_ref[...] = part
        elif start + chunk < grad_ref.shape[1]:
            total_ref[...] += part
        else:
            out_ref[...] = (total_ref[...] + part).astype(jnp.bfloat16)
    copies.start("give", out_ref, out_any.at[:, columns])
    copies.wait("give")


def embed_part(first, length, grad, weight_in, other=None, chunk=1024):
    nodes, hidden = grad.shape
    depth = weight_in.shape[0]
    operands = (grad, weight_in) if other is None else (grad, weight_in, other)
    return pl.pallas_call(
        functools.partial(embed_kernel, chunk, first),
        in_specs=[HBM] * len(operands),
        out_specs=HBM,
        out_shape=jax.ShapeDtypeStruct((nodes, depth), jnp.bfloat16),
        input_output_aliases={} if other is None else {2: 0},
        scratch_shapes=[
            pltpu.VMEM(grad.shape, jnp.bfloat16),
            pltpu.VMEM((length, hidden), jnp.bfloat16),
            pltpu.VMEM((nodes, length), jnp.bfloat16),
            pltpu.VMEM((nodes, length), jnp.float32),
            pltpu.SemaphoreType.DMA((1 + 2 * (hidden // chunk),)),
        ],
        cost_estimate=pl.CostEstimate(flops=2 * grad.size * length, bytes_accessed=9 * MIB, transcendentals=0),
        compiler_params=params(60),
        name="embed_part",
    )(*operands)


def bit_orders(count):
    bits = list(range(count.bit_length() - 1))
    first = len(bits) // 3
    groups = [bits[start : start + first] for start in range(0, 3 * first, first)]
    last = bits[3 * first :]
    return tuple(sum(groups[turn:] + groups[:turn], []) + last for turn in range(3))


def streams_of(dom_count, width):
    edges = (0, width * 12 // 32, width * 23 // 32, width)
    return tuple(zip(bit_orders(dom_count), edges[:-1], edges[1:]))


def halves(part, spot, mine):
    sent = lax.dynamic_index_in_dim(part, 1 - mine, spot, keepdims=False).astype(jnp.bfloat16)
    return sent, lax.dynamic_index_in_dim(part, mine, spot, keepdims=False)


def exchange(sent, bit):
    dom_count = lax.axis_size("dom")
    return lax.ppermute(sent, "dom", [(device, device ^ (1 << bit)) for device in range(dom_count)])


def body(
    embeds,
    weight_in,
    weight_out,
    prototypes,
    tile_column,
    tile_weight,
    send_rows,
    send_count,
    label_rows,
    label_class,
):
    nodes, embed_width = embeds.shape
    dom_count = lax.axis_size("dom")
    rep_count = lax.axis_size("rep")
    peers = dom_count * rep_count
    slots = send_rows.shape[2]
    hidden_width, width = weight_out.shape
    depth = hidden_width // peers
    place = lax.axis_index("dom")
    rep = lax.axis_index("rep")
    swap = [(0, 1), (1, 0)]
    fold = LANES // depth
    if fold > 1:
        order = (dom_count // fold, fold, rep_count, depth)
        weight_in = weight_in.reshape((-1,) + order).swapaxes(2, 3).reshape(-1, hidden_width)
        weight_out = weight_out.reshape(order + (-1,)).swapaxes(1, 2).reshape(hidden_width, -1)

    outgoing, pick, side = prepare(send_rows[0].T, send_count, tile_weight, embeds)
    arrived = lax.all_to_all(
        outgoing.reshape(peers, slots, -1), both, split_axis=0, concat_axis=0, tiled=True
    ).reshape(peers * slots, -1)
    pre_act, own, sent_own, grad, weight, back = forward(
        rep[None],
        tile_column,
        embeds,
        weight_in,
        weight_out,
        tile_weight,
        side,
        label_rows[None, :],
        label_class[None, :],
        prototypes,
        peers * slots,
    )
    other_own = lax.ppermute(sent_own, "rep", swap)
    came, sent_came, full, turned, returned = received_part(
        rep[None], arrived, weight_in, weight_out, side, grad, weight, back
    )
    other_turned = lax.ppermute(turned, "rep", swap)
    other_came = lax.ppermute(sent_came, "rep", swap)
    given = lax.all_to_all(
        returned.reshape(peers, slots, width), both, split_axis=0, concat_axis=0, tiled=True
    ).reshape(peers * slots, width)
    operands = (turned, other_turned, own, came, other_own, other_came)

    streams = streams_of(dom_count, width)
    bit_count = dom_count.bit_length() - 1
    parts = []
    if fold > 1:
        total = product(place[None], (), operands)
        total = total.reshape(-1, width, fold, depth).swapaxes(1, 2).reshape((2,) * bit_count + (width, depth))
        for order, low, high in streams:
            spot = bit_count - 1 - order[0]
            pair = halves(total[..., low:high, :], spot, (place >> order[0]) & 1)
            parts.append(tuple(array.reshape(-1, high - low, depth) for array in pair))
    else:
        flat = product(place[None], streams, operands)
        parts = [tuple(flat[2 * stream : 2 * stream + 2]) for stream in range(len(streams))]
    parts, full = lax.optimization_barrier((parts, full))
    grad_pre = slope_part(full, pick, given, side, pre_act, weight_out)
    left = [[bit for bit in range(bit_count) if bit != order[0]] for order, _, _ in streams]
    orders = [order for order, _, _ in streams]
    shared = next(step for step in range(bit_count + 1) if all(order[step:] == orders[0][step:] for order in orders))
    beside = (1, bit_count - 1)
    half = embed_width // 2
    embed_grad = None
    for step in range(bit_count):
        if step in beside:
            parts, grad_pre = lax.optimization_barrier((parts, grad_pre))
            embed_grad = embed_part(beside.index(step) * half, half, grad_pre, weight_in, embed_grad)
        elif step > 0:
            parts = lax.optimization_barrier(parts)
        came = [exchange(sent, order[step]) for (sent, _), order in zip(parts, orders)]
        if step == 0:
            came, grad_pre = lax.optimization_barrier((came, grad_pre))
        elif step in beside:
            came, embed_grad = lax.optimization_barrier((came, embed_grad))
        else:
            came = lax.optimization_barrier(came)
        kept = [array for _, array in parts]
        if step + 1 == bit_count:
            break
        digits = [(bits.index(order[step + 1]), order[step + 1]) for bits, order in zip(left, orders)]
        for bits, order in zip(left, orders):
            bits.remove(order[step + 1])
        parts = fold_halves(place[None], digits, step + 1 == shared, kept, came)
        if step + 1 == shared:
            left, orders = left[:1], orders[:1]
    summed = finish(1.0 / math.sqrt(nodes * peers), kept, came)
    return (embed_grad, summed)


def solution(mesh):
    placed = (
        P(both, None),
        P(),
        P(),
        P(),
        P(both, None),
        P(both, None, None, None),
        P(both, None, None),
        P(both, None),
        P(both),
        P(both),
    )
    return jax.shard_map(
        body,
        mesh=mesh,
        in_specs=placed,
        out_specs=(P(both, None), P(both, None)),
        check_vma=False,
    )
```

```python
import functools
import math

import jax
import jax.numpy as jnp
from jax import lax
from jax.experimental import pallas as pl
from jax.experimental.pallas import tpu as pltpu
from jax.sharding import PartitionSpec as P

gelu_inner = 0.7978845608028654
gelu_cubic = 0.044715
LANES = 128
SLOPED = 2560
MIB = 1024 * 1024
both = ("dom", "rep")


def gelu_half(values):
    square = values * values
    return 0.5 + 0.5 * jnp.tanh(values * (gelu_inner + gelu_inner * gelu_cubic * square)), square


def gelu_slope(values, half, square):
    return half + values * half * (2.0 - 2.0 * half) * (gelu_inner + 3.0 * gelu_inner * gelu_cubic * square)


def dot(left, right, left_dim=1, right_dim=0):
    return lax.dot_general(
        left, right, (((left_dim,), (right_dim,)), ((), ())), preferred_element_type=jnp.float32
    )


def params(mib=64):
    return pltpu.CompilerParams(vmem_limit_bytes=mib * MIB)


VMEM = pl.BlockSpec(memory_space=pltpu.VMEM)
SMEM = pl.BlockSpec(memory_space=pltpu.SMEM)
HBM = pl.BlockSpec(memory_space=pltpu.HBM)


class Copies:
    def __init__(self, semaphores):
        self.semaphores = semaphores
        self.started = {}

    def start(self, name, source, target):
        copy = pltpu.make_async_copy(source, target, self.semaphores.at[len(self.started)])
        copy.start()
        self.started[name] = copy

    def wait(self, name):
        self.started[name].wait()


def bits_of(values):
    high = values.astype(jnp.bfloat16).astype(jnp.float32)
    middle = (values - high).astype(jnp.bfloat16).astype(jnp.float32)
    return high, middle, values - high - middle


def prepare_kernel(
    rows_any,
    count_any,
    tiles_any,
    embeds_any,
    out_any,
    pick_any,
    side_any,
    rows_ref,
    count_ref,
    tiles_ref,
    embeds_ref,
    out_ref,
    pick_ref,
    side_ref,
    semaphores,
):
    copies = Copies(semaphores)
    copies.start("rows", rows_any, rows_ref)
    copies.start("count", count_any, count_ref)
    copies.start("embeds", embeds_any, embeds_ref)
    copies.start("tiles", tiles_any, tiles_ref)
    copies.wait("rows")
    copies.wait("count")
    slots, peers = rows_ref.shape
    nodes, width = embeds_ref.shape
    sent = slots * peers
    blocks, tiles = tiles_ref.shape[:2]
    spread = jnp.concatenate([rows_ref[...].astype(jnp.float32)] * peers, axis=0)
    row = lax.broadcasted_iota(jnp.int32, (sent, peers), 0)
    chosen = lax.div(row, slots) == lax.broadcasted_iota(jnp.int32, (sent, peers), 1)
    index = jnp.sum(jnp.where(chosen, spread, 0.0), axis=1, keepdims=True).astype(jnp.int32)
    counts = jnp.broadcast_to(count_ref[...].astype(jnp.float32), (sent, peers))
    count = jnp.sum(jnp.where(chosen, counts, 0.0), axis=1, keepdims=True).astype(jnp.int32)
    slot = lax.rem(lax.broadcasted_iota(jnp.int32, (sent, nodes), 0), slots)
    node = lax.broadcasted_iota(jnp.int32, (sent, nodes), 1)
    pick = jnp.where((node == index) & (slot < count), 1.0, 0.0).astype(jnp.bfloat16)
    pick_ref[...] = pick
    copies.wait("embeds")
    copies.start("pick", pick_ref, pick_any)
    out_ref[:, :width] = dot(pick, embeds_ref[...]).astype(jnp.bfloat16)
    copies.wait("tiles")
    copies.start("wide", out_ref.at[:, pl.ds(0, width)], out_any.at[:, pl.ds(0, width)])
    size = tiles_ref.shape[2]
    lane = lax.broadcasted_iota(jnp.int32, (size, LANES), 1)
    parts = []
    for block in range(blocks):
        total = tiles_ref[block, 0].astype(jnp.float32)
        for tile in range(1, tiles):
            total = total + tiles_ref[block, tile].astype(jnp.float32)
        rowsum = jnp.sum(total, axis=1, keepdims=True)
        scaling = lax.rsqrt(1.0 + rowsum)
        side_ref[block * size : (block + 1) * size, :] = jnp.where(lane == 0, rowsum, scaling)
        high, middle, low = bits_of(scaling)
        part = jnp.where(lane == 0, high, jnp.where(lane == 1, middle, jnp.where(lane == 2, low, 0.0)))
        parts.append(part.astype(jnp.bfloat16))
    out_ref[:, width:] = dot(pick, jnp.concatenate(parts, axis=0)).astype(jnp.bfloat16)
    copies.start("side", side_ref, side_any)
    copies.start("narrow", out_ref.at[:, pl.ds(width, LANES)], out_any.at[:, pl.ds(width, LANES)])
    for name in ("pick", "wide", "side", "narrow"):
        copies.wait(name)


def prepare(rows, count, tile_weight, embeds):
    sent = rows.shape[0] * rows.shape[1]
    nodes, width = embeds.shape
    shapes = (
        jax.ShapeDtypeStruct((sent, width + LANES), jnp.bfloat16),
        jax.ShapeDtypeStruct((sent, nodes), jnp.bfloat16),
        jax.ShapeDtypeStruct((nodes, LANES), jnp.float32),
    )
    return pl.pallas_call(
        prepare_kernel,
        in_specs=[HBM] * 4,
        out_specs=(HBM,) * 3,
        out_shape=shapes,
        scratch_shapes=[
            pltpu.VMEM(rows.shape, jnp.int32),
            pltpu.VMEM(count.shape, jnp.int32),
            pltpu.VMEM(tile_weight.shape, jnp.bfloat16),
            pltpu.VMEM(embeds.shape, jnp.bfloat16),
        ]
        + [pltpu.VMEM(shape.shape, shape.dtype) for shape in shapes]
        + [pltpu.SemaphoreType.DMA((8,))],
        compiler_params=params(),
        name="prepare",
    )(rows, count, tile_weight, embeds)


def split_hidden(hidden, rep, mine_ref, other_ref, start):
    for pair in range(hidden.shape[1] // (2 * LANES)):
        low = hidden[:, 2 * pair * LANES : (2 * pair + 1) * LANES]
        high = hidden[:, (2 * pair + 1) * LANES : (2 * pair + 2) * LANES]
        place = slice(start // 2 + pair * LANES, start // 2 + (pair + 1) * LANES)
        mine_ref[:, place] = jnp.where(rep == 0, low, high)
        other_ref[:, place] = jnp.where(rep == 0, high, low)


def hidden_chunks(x, win_ref, wout_ref, waiting, arrive, take, piece=256):
    chunk = waiting[0].shape[1]
    count = win_ref.shape[1] // chunk
    projected = None
    for step in range(count + 1):
        arrive(step)
        for low in range(0, chunk, piece):
            place = slice(low, low + piece)
            if step < count:
                ahead = step * chunk + low
                waiting[step % 2][:, place] = dot(x, win_ref[:, ahead : ahead + piece])
            if step > 0:
                start = (step - 1) * chunk + low
                values = waiting[(step - 1) % 2][:, place]
                half, square = gelu_half(values)
                hidden = (values * half).astype(jnp.bfloat16)
                take(start, hidden, values, half, square)
                part = dot(hidden, wout_ref[start : start + piece])
                projected = part if projected is None else projected + part
    return projected


class Weights:
    def __init__(self, copies, win_any, wout_any, win_ref, wout_ref, chunk):
        self.copies = copies
        self.count = win_ref.shape[1] // chunk
        for step in range(self.count):
            place = pl.ds(step * chunk, chunk)
            copies.start(("in", step), win_any.at[:, place], win_ref.at[:, place])
            if step % 2 == 0:
                place = pl.ds(step * chunk, 2 * chunk)
                copies.start(("out", step), wout_any.at[place], wout_ref.at[place])

    def wait(self, step):
        if step < self.count:
            self.copies.wait(("in", step))
        if step % 2 == 1:
            self.copies.wait(("out", step - 1))


def forward_kernel(
    rep_ref,
    column_ref,
    x_any,
    win_any,
    wout_any,
    tiles_any,
    side_any,
    rows_any,
    class_any,
    proto_any,
    pre_any,
    mine_any,
    other_any,
    grad_any,
    weight_any,
    back_any,
    x_ref,
    win_ref,
    wout_ref,
    tiles_ref,
    side_ref,
    rows_ref,
    class_ref,
    proto_ref,
    pre_ref,
    mine_ref,
    other_ref,
    even_ref,
    odd_ref,
    dense_ref,
    high_ref,
    low_ref,
    grad_ref,
    back_ref,
    semaphores,
):
    copies = Copies(semaphores)
    chunk = even_ref.shape[1]
    copies.start("x", x_any, x_ref)
    copies.start("tiles", tiles_any, tiles_ref)
    weights = Weights(copies, win_any, wout_any, win_ref, wout_ref, chunk)
    later = {
        "side": (side_any, side_ref),
        "rows": (rows_any, rows_ref),
        "class": (class_any, class_ref),
        "proto": (proto_any, proto_ref),
    }
    for name, (source, target) in later.items():
        copies.start(name, source, target)
    nodes = x_ref.shape[0]
    copies.wait("x")

    def give(step):
        whole_place = pl.ds((step - 1) * chunk, 2 * chunk)
        half_place = pl.ds((step - 1) * chunk // 2, chunk)
        copies.start(("pre", step), pre_ref.at[:, whole_place], pre_any.at[:, whole_place])
        copies.start(("mine", step), mine_ref.at[:, half_place], mine_any.at[:, half_place])
        copies.start(("other", step), other_ref.at[:, half_place], other_any.at[:, half_place])

    def arrive(step):
        weights.wait(step)
        if step > 1 and step % 2 == 1:
            give(step - 2)
        if step == 0:
            copies.wait("tiles")
            dense_graph(column_ref, tiles_ref, dense_ref, high_ref, low_ref)
        if step == 1:
            extra = pl.ds(nodes, high_ref.shape[1] - nodes)
            copies.start("high", high_ref.at[:, extra], weight_any.at[0])
            copies.start("low", low_ref.at[:, extra], weight_any.at[1])

    def take(start, hidden, values, half, square):
        kept = gelu_slope(values, half, square) if start < SLOPED else values
        pre_ref[:, start : start + hidden.shape[1]] = kept.astype(jnp.bfloat16)
        split_hidden(hidden, rep_ref[0], mine_ref, other_ref, start)

    projected = hidden_chunks(x_ref[...], win_ref, wout_ref, (even_ref, odd_ref), arrive, take)
    give(weights.count - 1)
    for name in later:
        copies.wait(name)
    width = projected.shape[1]
    rowsum = side_ref[:, 0:1]
    scaling = side_ref[:, 1:2]
    unit = (projected * scaling).astype(jnp.bfloat16)
    unit_float = unit.astype(jnp.float32)
    beside = jnp.concatenate([unit, jnp.ones((nodes, LANES), jnp.bfloat16)], axis=1)
    high, low = high_ref[...], low_ref[...]
    turned = dot(high, beside, 0, 0) + dot(low, beside, 0, 0)
    back_ref[...] = turned[nodes:]
    copies.start("back", back_ref, back_any)
    neighbour = dot(high[:, :nodes], unit) + dot(low[:, :nodes], unit)
    own = turned[:nodes, width : width + 1] * unit_float - turned[:nodes, :width]
    marked = rows_ref.shape[1]
    node = lax.broadcasted_iota(jnp.int32, (nodes, marked), 0)
    label = jnp.where(node == rows_ref[...], 1.0, 0.0)
    name = lax.broadcasted_iota(jnp.int32, (proto_ref.shape[0], marked), 0)
    named = jnp.where(name == class_ref[...], 1.0, 0.0).astype(jnp.bfloat16)
    target = dot(named, proto_ref[...], 0, 0).astype(jnp.bfloat16)
    pull = jnp.sum(label, axis=1, keepdims=True) * projected - dot(label.astype(jnp.bfloat16), target)
    grad_ref[...] = (rowsum * unit_float - neighbour + own) * scaling + pull
    copies.start("grad", grad_ref, grad_any)
    for step in range(1, weights.count, 2):
        for name in ("pre", "mine", "other"):
            copies.wait((name, step))
    for name in ("high", "low", "back", "grad"):
        copies.wait(name)


def dense_graph(column_ref, tiles_ref, dense_ref, high_ref, low_ref):
    blocks, tiles, size, _ = tiles_ref.shape
    dense_ref[...] = jnp.zeros_like(dense_ref)
    for block in range(blocks):
        for tile in range(tiles):
            column = column_ref[block, tile]
            place = slice(block * size, (block + 1) * size)
            dense_ref[column, place, :] += tiles_ref[block, tile].astype(jnp.float32)
    for column in range(dense_ref.shape[0]):
        dense = dense_ref[column]
        high = dense.astype(jnp.bfloat16)
        place = slice(column * size, (column + 1) * size)
        high_ref[:, place] = high
        low_ref[:, place] = (dense - high.astype(jnp.float32)).astype(jnp.bfloat16)


def forward(
    rep,
    tile_column,
    embeds,
    weight_in,
    weight_out,
    tile_weight,
    side,
    label_rows,
    label_class,
    prototypes,
    received,
    chunk=1024,
):
    nodes, depth = embeds.shape
    hidden = weight_in.shape[1]
    width = weight_out.shape[1]
    size = tile_weight.shape[2]
    low = jnp.bfloat16
    arrays = (embeds, weight_in, weight_out, tile_weight, side, label_rows, label_class, prototypes)
    return pl.pallas_call(
        forward_kernel,
        in_specs=[SMEM] * 2 + [HBM] * 8,
        out_specs=(HBM,) * 6,
        out_shape=(
            jax.ShapeDtypeStruct((nodes, hidden), low),
            jax.ShapeDtypeStruct((nodes, hidden // 2), low),
            jax.ShapeDtypeStruct((nodes, hidden // 2), low),
            jax.ShapeDtypeStruct((nodes, width), jnp.float32),
            jax.ShapeDtypeStruct((2, nodes, received), low),
            jax.ShapeDtypeStruct((received, width + LANES), jnp.float32),
        ),
        scratch_shapes=[pltpu.VMEM(array.shape, array.dtype) for array in arrays]
        + [
            pltpu.VMEM((nodes, hidden), low),
            pltpu.VMEM((nodes, hidden // 2), low),
            pltpu.VMEM((nodes, hidden // 2), low),
            pltpu.VMEM((nodes, chunk), jnp.float32),
            pltpu.VMEM((nodes, chunk), jnp.float32),
            pltpu.VMEM(((nodes + received) // size, nodes, size), jnp.float32),
            pltpu.VMEM((nodes, nodes + received), low),
            pltpu.VMEM((nodes, nodes + received), low),
            pltpu.VMEM((nodes, width), jnp.float32),
            pltpu.VMEM((received, width + LANES), jnp.float32),
            pltpu.SemaphoreType.DMA((10 + 5 * (hidden // chunk),)),
        ],
        compiler_params=params(),
        name="forward",
    )(rep, tile_column, *arrays)


def received_kernel(
    rep_ref,
    x_any,
    win_any,
    wout_any,
    side_any,
    grad_any,
    weight_any,
    back_any,
    mine_any,
    other_any,
    full_any,
    turned_any,
    return_any,
    x_ref,
    win_ref,
    wout_ref,
    side_ref,
    grad_ref,
    weight_ref,
    back_ref,
    mine_ref,
    other_ref,
    full_ref,
    turned_ref,
    return_ref,
    even_ref,
    odd_ref,
    semaphores,
):
    depth = win_ref.shape[0]
    nodes, width = grad_ref.shape
    chunk = even_ref.shape[1]
    copies = Copies(semaphores)
    copies.start("x", x_any, x_ref)
    weights = Weights(copies, win_any, wout_any, win_ref, wout_ref, chunk)
    later = {
        "side": (side_any, side_ref),
        "grad": (grad_any, grad_ref),
        "weight": (weight_any, weight_ref),
        "back": (back_any, back_ref),
    }
    for name, (source, target) in later.items():
        copies.start(name, source, target)
    copies.wait("x")

    group = 4

    def give(step):
        place = pl.ds((step + 1 - group) * chunk // 2, group * chunk // 2)
        copies.start(("mine", step), mine_ref.at[:, place], mine_any.at[:, place])
        copies.start(("other", step), other_ref.at[:, place], other_any.at[:, place])

    def arrive(step):
        weights.wait(step)
        if step > 1 and (step - 1) % group == 0:
            give(step - 2)

    def take(start, hidden, values, half, square):
        split_hidden(hidden, rep_ref[0], mine_ref, other_ref, start)

    projected = hidden_chunks(x_ref[:, :depth], win_ref, wout_ref, (even_ref, odd_ref), arrive, take)
    give(weights.count - 1)
    for name in later:
        copies.wait(name)
    scaling = jnp.sum(x_ref[:, depth:].astype(jnp.float32), axis=1, keepdims=True)
    unit = (projected * scaling).astype(jnp.bfloat16)
    neighbour = dot(weight_ref[0], unit) + dot(weight_ref[1], unit)
    full = grad_ref[...] - neighbour * side_ref[:, 1:2]
    full_ref[...] = full
    back = (back_ref[:, width : width + 1] * unit.astype(jnp.float32) - back_ref[:, :width]).astype(jnp.bfloat16)
    return_ref[...] = back
    copies.start("full", full_ref, full_any)
    copies.start("return", return_ref, return_any)
    turned_ref[:, :nodes] = full.T.astype(jnp.bfloat16)
    turned_ref[:, nodes:] = (back.astype(jnp.float32) * scaling).T.astype(jnp.bfloat16)
    copies.start("turned", turned_ref, turned_any)
    for step in range(group - 1, weights.count, group):
        copies.wait(("mine", step))
        copies.wait(("other", step))
    for name in ("full", "return", "turned"):
        copies.wait(name)


def received_part(rep, arrived, weight_in, weight_out, side, grad, weight, back, chunk=512):
    rows = arrived.shape[0]
    hidden = weight_in.shape[1]
    nodes, width = grad.shape
    low = jnp.bfloat16
    arrays = (arrived, weight_in, weight_out, side, grad, weight, back)
    return pl.pallas_call(
        received_kernel,
        in_specs=[SMEM] + [HBM] * 7,
        out_specs=(HBM,) * 5,
        out_shape=(
            jax.ShapeDtypeStruct((rows, hidden // 2), low),
            jax.ShapeDtypeStruct((rows, hidden // 2), low),
            jax.ShapeDtypeStruct((nodes, width), jnp.float32),
            jax.ShapeDtypeStruct((width, nodes + rows), low),
            jax.ShapeDtypeStruct((rows, width), low),
        ),
        scratch_shapes=[pltpu.VMEM(array.shape, array.dtype) for array in arrays]
        + [
            pltpu.VMEM((rows, hidden // 2), low),
            pltpu.VMEM((rows, hidden // 2), low),
            pltpu.VMEM((nodes, width), jnp.float32),
            pltpu.VMEM((width, nodes + rows), low),
            pltpu.VMEM((rows, width), low),
            pltpu.VMEM((rows, chunk), jnp.float32),
            pltpu.VMEM((rows, chunk), jnp.float32),
            pltpu.SemaphoreType.DMA((8 + 4 * (hidden // chunk),)),
        ],
        compiler_params=params(),
        name="received_part",
    )(rep, *arrays)


def chip_total(chunk, copies, arrays, turned_ref, hidden_ref, total_ref, arrive):
    hidden = hidden_ref.shape[1]
    edges = [0] + list(range(chunk // 2, hidden, chunk)) + [hidden]
    steps = list(zip(edges[:-1], edges[1:]))
    base = 0
    for index in range(2):
        length = arrays[index].shape[1]
        copies.start(index, arrays[index], turned_ref.at[:, pl.ds(base, length)])
        base += length
    for start, end in steps:
        place = pl.ds(start, end - start)
        base = 0
        for index in range(2, 6):
            length = arrays[index].shape[0]
            copies.start((index, start), arrays[index].at[:, place], hidden_ref.at[pl.ds(base, length), place])
            base += length
    copies.wait(0)
    copies.wait(1)
    for start, end in steps:
        for index in range(2, 6):
            copies.wait((index, start))
        arrive(start // LANES)
        total = dot(turned_ref[...], hidden_ref[:, start:end])
        for step in range((end - start) // LANES):
            total_ref[start // LANES + step] = total[:, step * LANES : (step + 1) * LANES]


def total_kernel(chunk, *refs):
    turned_ref, hidden_ref, semaphores = refs[7:]
    chip_total(chunk, Copies(semaphores), refs[:6], turned_ref, hidden_ref, refs[6], lambda ready: None)


def product_kernel(streams, chunk, place_ref, *refs):
    count = 2 * len(streams)
    outputs, scratch = refs[6 : 6 + count], refs[6 + count : 6 + 2 * count]
    turned_ref, hidden_ref, semaphores, total_ref = refs[6 + 2 * count :]
    copies = Copies(semaphores)
    done = [0] * len(streams)

    def arrive(ready):
        given = []
        for stream, (order, low, high) in enumerate(streams):
            bit = order[0]
            first = done[stream]
            spot = first
            while spot < scratch[2 * stream].shape[0]:
                base = ((spot >> bit) << (bit + 1)) | (spot & ((1 << bit) - 1))
                if base + (1 << bit) >= ready:
                    break
                sent, kept = places(spot, bit, place_ref[0])
                scratch[2 * stream][spot] = total_ref[sent, low:high].astype(jnp.bfloat16)
                scratch[2 * stream + 1][spot] = total_ref[kept, low:high]
                spot += 1
            done[stream] = spot
            if spot > first:
                given += [(2 * stream, first, spot), (2 * stream + 1, first, spot)]
        for index, first, last in given:
            place = pl.ds(first, last - first)
            copies.start(("give", index, first), scratch[index].at[place], outputs[index].at[place])

    chip_total(chunk, copies, refs[:6], turned_ref, hidden_ref, total_ref, arrive)
    arrive(total_ref.shape[0])
    for name in list(copies.started):
        if isinstance(name, tuple) and name[0] == "give":
            copies.wait(name)


def places(spot, weight, place, bit=None):
    mine = lax.rem(lax.div(place, 1 << (weight if bit is None else bit)), 2)
    base = ((spot >> weight) << (weight + 1)) | (spot & ((1 << weight) - 1))
    return base + (1 - mine) * (1 << weight), base + mine * (1 << weight)


def fold_kernel(digits, merge, place_ref, *refs):
    count = len(digits)
    outputs = refs[2 * count :]
    base = 0
    for stream, (weight, bit) in enumerate(digits):
        kept_ref, came_ref = refs[2 * stream : 2 * stream + 2]
        target = 0 if merge else stream
        if not merge:
            base = 0
        sent_ref, next_ref = outputs[2 * target : 2 * target + 2]
        rows = slice(base, base + kept_ref.shape[1])
        base = rows.stop
        for spot in range(sent_ref.shape[0]):
            sent, kept = places(spot, weight, place_ref[0], bit)
            sent_ref[spot, rows] = (kept_ref[sent] + came_ref[sent].astype(jnp.float32)).astype(jnp.bfloat16)
            next_ref[spot, rows] = kept_ref[kept] + came_ref[kept].astype(jnp.float32)


def fold_halves(place, digits, merge, kept, came):
    heights = [array.shape[1] for array in kept]
    if merge:
        heights = [sum(heights)]
    blocks, _, depth = kept[0].shape
    shapes = []
    for height in heights:
        shapes.append(jax.ShapeDtypeStruct((blocks // 2, height, depth), jnp.bfloat16))
        shapes.append(jax.ShapeDtypeStruct((blocks // 2, height, depth), jnp.float32))
    operands = [array for pair in zip(kept, came) for array in pair]
    flat = pl.pallas_call(
        functools.partial(fold_kernel, digits, merge),
        in_specs=[SMEM] + [VMEM] * len(operands),
        out_shape=tuple(shapes),
        compiler_params=params(16),
        name="fold_halves",
    )(place, *operands)
    return [tuple(flat[2 * stream : 2 * stream + 2]) for stream in range(len(heights))]


def finish_kernel(factor, *refs):
    base = 0
    for stream in range(len(refs) // 2):
        kept_ref, came_ref = refs[2 * stream : 2 * stream + 2]
        rows = kept_ref.shape[1]
        total = kept_ref[0] + came_ref[0].astype(jnp.float32)
        refs[-1][:, base : base + rows] = total.T * factor
        base += rows


def finish(factor, kept, came):
    width = sum(array.shape[1] for array in kept)
    return pl.pallas_call(
        functools.partial(finish_kernel, factor),
        out_shape=jax.ShapeDtypeStruct((kept[0].shape[2], width), jnp.float32),
        compiler_params=params(16),
        name="finish",
    )(*[array for pair in zip(kept, came) for array in pair])


def product(place, streams, operands, chunk=1024):
    width = operands[0].shape[0]
    hidden = operands[2].shape[1]
    blocks = hidden // LANES
    total = (blocks, width, LANES)
    rows = 2 * operands[0].shape[1]
    scratch = [
        pltpu.VMEM((width, rows), jnp.bfloat16),
        pltpu.VMEM((rows, hidden), jnp.bfloat16),
        pltpu.SemaphoreType.DMA((2 + 10 * (hidden // chunk + 1),)),
    ]
    if not streams:
        return pl.pallas_call(
            functools.partial(total_kernel, chunk),
            in_specs=[HBM] * 6,
            out_shape=jax.ShapeDtypeStruct(total, jnp.float32),
            scratch_shapes=scratch,
            compiler_params=params(),
            name="chip_total",
        )(*operands)
    shapes = []
    for _, low, high in streams:
        shapes.append(jax.ShapeDtypeStruct((blocks // 2, high - low, LANES), jnp.bfloat16))
        shapes.append(jax.ShapeDtypeStruct((blocks // 2, high - low, LANES), jnp.float32))
    return pl.pallas_call(
        functools.partial(product_kernel, streams, chunk),
        in_specs=[SMEM] + [HBM] * 6,
        out_specs=(HBM,) * len(shapes),
        out_shape=tuple(shapes),
        scratch_shapes=[pltpu.VMEM(shape.shape, shape.dtype) for shape in shapes]
        + scratch
        + [pltpu.VMEM(total, jnp.float32)],
        compiler_params=params(),
        name="product",
    )(place, *operands)


def slope_kernel(chunk, *refs):
    full_any, pick_any, back_any, side_any, pre_any, wout_any, out_any = refs[:7]
    full_ref, pick_ref, back_ref, side_ref, pre_ref, wout_ref, grad_ref, semaphores = refs[7:]
    copies = Copies(semaphores)
    first = ((full_any, full_ref), (pick_any, pick_ref), (back_any, back_ref), (side_any, side_ref))
    steps = range(0, pre_ref.shape[1], chunk)
    for index, (source, target) in enumerate(first):
        copies.start(index, source, target)
    for start in steps:
        place = pl.ds(start, chunk)
        copies.start(("out", start), wout_any.at[place], wout_ref.at[place])
        copies.start(("pre", start), pre_any.at[:, place], pre_ref.at[:, place])
    for index in range(len(first)):
        copies.wait(index)
    back = dot(pick_ref[...], back_ref[...], 0, 0)
    node = (full_ref[...] + back * side_ref[:, 1:2]).astype(jnp.bfloat16)
    piece = chunk // 2
    for start in steps:
        copies.wait(("out", start))
        copies.wait(("pre", start))
        if start > 0:
            place = pl.ds(start - chunk, chunk)
            copies.start(("grad", start - chunk), grad_ref.at[:, place], out_any.at[:, place])
        for low in range(start, start + chunk, piece):
            place = slice(low, low + piece)
            grad_hidden = dot(node, wout_ref[place], 1, 1)
            slope = pre_ref[:, place].astype(jnp.float32)
            if low >= SLOPED:
                slope = gelu_slope(slope, *gelu_half(slope))
            grad_ref[:, place] = (grad_hidden * slope).astype(jnp.bfloat16)
    place = pl.ds(steps[-1], chunk)
    copies.start(("grad", steps[-1]), grad_ref.at[:, place], out_any.at[:, place])
    for start in steps:
        copies.wait(("grad", start))


def slope_part(full, pick, back, side, pre, weight_out, chunk=1024):
    arrays = (full, pick, back, side, pre, weight_out)
    return pl.pallas_call(
        functools.partial(slope_kernel, chunk),
        in_specs=[HBM] * 6,
        out_specs=HBM,
        out_shape=jax.ShapeDtypeStruct(pre.shape, jnp.bfloat16),
        scratch_shapes=[pltpu.VMEM(array.shape, array.dtype) for array in arrays]
        + [
            pltpu.VMEM(pre.shape, jnp.bfloat16),
            pltpu.SemaphoreType.DMA((4 + 3 * (pre.shape[1] // chunk),)),
        ],
        cost_estimate=pl.CostEstimate(flops=2 * pre.size * full.shape[1], bytes_accessed=16 * MIB, transcendentals=0),
        compiler_params=params(58),
        name="slope_part",
    )(*arrays)


def embed_kernel(chunk, first, grad_any, win_any, *refs):
    out_any, grad_ref, win_ref, out_ref, total_ref, semaphores = refs[-6:]
    copies = Copies(semaphores)
    steps = range(0, grad_ref.shape[1], chunk)
    columns = pl.ds(first, win_ref.shape[0])
    for start in steps:
        place = pl.ds(start, chunk)
        copies.start(("grad", start), grad_any.at[:, place], grad_ref.at[:, place])
        copies.start(("in", start), win_any.at[columns, place], win_ref.at[:, place])
    for start in steps:
        copies.wait(("grad", start))
        copies.wait(("in", start))
        place = slice(start, start + chunk)
        part = dot(grad_ref[:, place], win_ref[:, place], 1, 1)
        if start == 0:
            total_ref[...] = part
        elif start + chunk < grad_ref.shape[1]:
            total_ref[...] += part
        else:
            out_ref[...] = (total_ref[...] + part).astype(jnp.bfloat16)
    copies.start("give", out_ref, out_any.at[:, columns])
    copies.wait("give")


def embed_part(first, length, grad, weight_in, other=None, chunk=1024):
    nodes, hidden = grad.shape
    depth = weight_in.shape[0]
    operands = (grad, weight_in) if other is None else (grad, weight_in, other)
    return pl.pallas_call(
        functools.partial(embed_kernel, chunk, first),
        in_specs=[HBM] * len(operands),
        out_specs=HBM,
        out_shape=jax.ShapeDtypeStruct((nodes, depth), jnp.bfloat16),
        input_output_aliases={} if other is None else {2: 0},
        scratch_shapes=[
            pltpu.VMEM(grad.shape, jnp.bfloat16),
            pltpu.VMEM((length, hidden), jnp.bfloat16),
            pltpu.VMEM((nodes, length), jnp.bfloat16),
            pltpu.VMEM((nodes, length), jnp.float32),
            pltpu.SemaphoreType.DMA((1 + 2 * (hidden // chunk),)),
        ],
        cost_estimate=pl.CostEstimate(flops=2 * grad.size * length, bytes_accessed=9 * MIB, transcendentals=0),
        compiler_params=params(60),
        name="embed_part",
    )(*operands)


def bit_orders(count):
    bits = list(range(count.bit_length() - 1))
    first = len(bits) // 3
    groups = [bits[start : start + first] for start in range(0, 3 * first, first)]
    last = bits[3 * first :]
    return tuple(sum(groups[turn:] + groups[:turn], []) + last for turn in range(3))


def streams_of(dom_count, width):
    edges = (0, width * 12 // 32, width * 23 // 32, width)
    return tuple(zip(bit_orders(dom_count), edges[:-1], edges[1:]))


def halves(part, spot, mine):
    sent = lax.dynamic_index_in_dim(part, 1 - mine, spot, keepdims=False).astype(jnp.bfloat16)
    return sent, lax.dynamic_index_in_dim(part, mine, spot, keepdims=False)


def exchange(sent, bit):
    dom_count = lax.axis_size("dom")
    return lax.ppermute(sent, "dom", [(device, device ^ (1 << bit)) for device in range(dom_count)])


def body(
    embeds,
    weight_in,
    weight_out,
    prototypes,
    tile_column,
    tile_weight,
    send_rows,
    send_count,
    label_rows,
    label_class,
):
    nodes, embed_width = embeds.shape
    dom_count = lax.axis_size("dom")
    rep_count = lax.axis_size("rep")
    peers = dom_count * rep_count
    slots = send_rows.shape[2]
    hidden_width, width = weight_out.shape
    depth = hidden_width // peers
    place = lax.axis_index("dom")
    rep = lax.axis_index("rep")
    swap = [(0, 1), (1, 0)]
    fold = LANES // depth
    if fold > 1:
        order = (dom_count // fold, fold, rep_count, depth)
        weight_in = weight_in.reshape((-1,) + order).swapaxes(2, 3).reshape(-1, hidden_width)
        weight_out = weight_out.reshape(order + (-1,)).swapaxes(1, 2).reshape(hidden_width, -1)

    outgoing, pick, side = prepare(send_rows[0].T, send_count, tile_weight, embeds)
    arrived = lax.all_to_all(
        outgoing.reshape(peers, slots, -1), both, split_axis=0, concat_axis=0, tiled=True
    ).reshape(peers * slots, -1)
    pre_act, own, sent_own, grad, weight, back = forward(
        rep[None],
        tile_column,
        embeds,
        weight_in,
        weight_out,
        tile_weight,
        side,
        label_rows[None, :],
        label_class[None, :],
        prototypes,
        peers * slots,
    )
    other_own = lax.ppermute(sent_own, "rep", swap)
    came, sent_came, full, turned, returned = received_part(
        rep[None], arrived, weight_in, weight_out, side, grad, weight, back
    )
    other_turned = lax.ppermute(turned, "rep", swap)
    other_came = lax.ppermute(sent_came, "rep", swap)
    given = lax.all_to_all(
        returned.reshape(peers, slots, width), both, split_axis=0, concat_axis=0, tiled=True
    ).reshape(peers * slots, width)
    operands = (turned, other_turned, own, came, other_own, other_came)

    streams = streams_of(dom_count, width)
    bit_count = dom_count.bit_length() - 1
    parts = []
    if fold > 1:
        total = product(place[None], (), operands)
        total = total.reshape(-1, width, fold, depth).swapaxes(1, 2).reshape((2,) * bit_count + (width, depth))
        for order, low, high in streams:
            spot = bit_count - 1 - order[0]
            pair = halves(total[..., low:high, :], spot, (place >> order[0]) & 1)
            parts.append(tuple(array.reshape(-1, high - low, depth) for array in pair))
    else:
        flat = product(place[None], streams, operands)
        parts = [tuple(flat[2 * stream : 2 * stream + 2]) for stream in range(len(streams))]
    parts, full = lax.optimization_barrier((parts, full))
    grad_pre = slope_part(full, pick, given, side, pre_act, weight_out)
    left = [[bit for bit in range(bit_count) if bit != order[0]] for order, _, _ in streams]
    orders = [order for order, _, _ in streams]
    shared = next(step for step in range(bit_count + 1) if all(order[step:] == orders[0][step:] for order in orders))
    beside = (1, bit_count - 1)
    half = embed_width // 2
    embed_grad = None
    for step in range(bit_count):
        if step in beside:
            parts, grad_pre = lax.optimization_barrier((parts, grad_pre))
            embed_grad = embed_part(beside.index(step) * half, half, grad_pre, weight_in, embed_grad)
        elif step > 0:
            parts = lax.optimization_barrier(parts)
        came = [exchange(sent, order[step]) for (sent, _), order in zip(parts, orders)]
        if step == 0:
            came, grad_pre = lax.optimization_barrier((came, grad_pre))
        elif step in beside:
            came, embed_grad = lax.optimization_barrier((came, embed_grad))
        else:
            came = lax.optimization_barrier(came)
        kept = [array for _, array in parts]
        if step + 1 == bit_count:
            break
        digits = [(bits.index(order[step + 1]), order[step + 1]) for bits, order in zip(left, orders)]
        for bits, order in zip(left, orders):
            bits.remove(order[step + 1])
        parts = fold_halves(place[None], digits, step + 1 == shared, kept, came)
        if step + 1 == shared:
            left, orders = left[:1], orders[:1]
    summed = finish(1.0 / math.sqrt(nodes * peers), kept, came)
    return (embed_grad, summed)


def solution(mesh):
    placed = (
        P(both, None),
        P(),
        P(),
        P(),
        P(both, None),
        P(both, None, None, None),
        P(both, None, None),
        P(both, None),
        P(both),
        P(both),
    )
    return jax.shard_map(
        body,
        mesh=mesh,
        in_specs=placed,
        out_specs=(P(both, None), P(both, None)),
        check_vma=False,
    )
```
